512 devices in a mesh: ctx: 64 (over x, y, core), head: 8 (over z).
Axes of the slice: x: 4, y: 8, z: 8, core: 2. Of those that a mesh axis runs over, the one named last changes fastest.
Arguments:
- prefill_query: bfloat16 [32768, 32, 128], P('ctx', 'head'), may hold values from -6 to 6
- prefill_key: bfloat16 [32768, 32, 128], P('ctx', 'head'), may hold values from -0.5 to 0.5
- prefill_value: bfloat16 [32768, 32, 128], P('ctx', 'head'), may hold values from -60 to 60
- log_decay: float32 [32768, 32], P('ctx', 'head'), may hold values from -1 to 0
- lengths: int32 [4], replicated, may hold values from 1 to 24576, as said below
- owner: int32 [4], replicated, may hold values from 0 to 127, as said below
- decode_state: float32 [128, 32, 128, 128], P('ctx', 'head'), may hold values from -20 to 20
- step_query: bfloat16 [8, 128, 32, 128], P(None, 'ctx', 'head'), may hold values from -6 to 6
- step_key: bfloat16 [8, 128, 32, 128], P(None, 'ctx', 'head'), may hold values from -0.5 to 0.5
- step_value: bfloat16 [8, 128, 32, 128], P(None, 'ctx', 'head'), may hold values from -6 to 6
- step_decay: float32 [8, 128, 32], P(None, 'ctx', 'head'), may hold values from -0.7 to -0.01
- soft_query: bfloat16 [8, 128, 64, 128], P(None, 'ctx', 'head'), may hold values from -200 to 200
- cache_keys: bfloat16 [128, 256, 8, 128], P('ctx', None, 'head'), may hold values from -6 to 6
- cache_values: bfloat16 [128, 256, 8, 128], P('ctx', None, 'head'), may hold values from -6 to 6
- new_keys: bfloat16 [8, 128, 8, 128], P(None, 'ctx', 'head'), may hold values from -6 to 6
- new_values: bfloat16 [8, 128, 8, 128], P(None, 'ctx', 'head'), may hold values from -6 to 6
- row_lengths: int32 [128], P('ctx'), may hold values from 2 to 256, as said below
Outputs:
- prefill_out: bfloat16 [32768, 32, 128], P('ctx', 'head')
- decode_out: bfloat16 [8, 128, 32, 128], P(None, 'ctx', 'head')
- soft_out: bfloat16 [8, 128, 64, 128], P(None, 'ctx', 'head')
The draws below stay inside these ranges and needn't reach their ends.
Inputs may be any that keep to these rules, and one draw needn't show every extreme that they name: lengths sum to 32768; the longest is exactly 24576. `owner`: distinct decode rows, including row 0 and row 127. `row_lengths`: row 0 has all 256 slots live.
All inputs are finite; a program needn't handle non-finite values.
Results may differ from the reference program's by a relative error of at most 0.0059.
Values sent between devices are 32-bit elements; how exact they have to be, the bound alone decides.
No kernel may reach another device: no remote copies, remote signals or barrier semaphores. Data moves between devices by JAX's collectives and lax.ppermute only.
A program may use at most 128 MiB of HBM per device.

```python
import math
import jax
import jax.numpy as jnp
from jax import lax

HD = 128
LHEADS = 32
SHEADS = 64
KVH = 8
PROMPTS = 4
STEPS = 8
TOK_DEV = 512
ROW_DEV = 2
CACHE = 256
PROMPT_TOKENS = 32768
MOST = 24576
ROWS = 128


def head_ramp(upper):
    return 1.0 + (upper - 1.0) * jnp.arange(LHEADS, dtype=jnp.float32) / (LHEADS - 1)


def shared_keys(key):
    return jnp.clip(jax.random.normal(key, (ROWS, CACHE, KVH, HD), jnp.float32), -6.0, 6.0)


def packed_lengths(key):
    key = jax.random.fold_in(key, 41)
    key_first, key_second, key_place = jax.random.split(key, 3)
    remainder = PROMPT_TOKENS - MOST
    first_cut = jax.random.randint(key_first, (), 1, remainder)
    second_cut = jax.random.randint(key_second, (), 1, remainder - 1)
    second_cut = second_cut + (second_cut >= first_cut).astype(jnp.int32)
    lower_cut = jnp.minimum(first_cut, second_cut)
    upper_cut = jnp.maximum(first_cut, second_cut)
    pieces = jnp.stack([lower_cut, upper_cut - lower_cut, remainder - upper_cut]).astype(jnp.int32)
    longest_at = jax.random.randint(key_place, (), 0, PROMPTS)
    indices = jnp.arange(PROMPTS, dtype=jnp.int32)
    piece_index = jnp.clip(indices - (indices > longest_at).astype(jnp.int32), 0, PROMPTS - 2)
    return jnp.where(indices == longest_at, MOST, pieces[piece_index]).astype(jnp.int32)


def free_row(candidate, taken):
    tries = (candidate + jnp.arange(PROMPTS + 1, dtype=jnp.int32)) % ROWS
    unused = jnp.all(tries[:, None] != taken[None, :], axis=1)
    return tries[jnp.argmax(unused)].astype(jnp.int32)


def draw_lengths(key, part):
    return packed_lengths(key)


def draw_owner(key, part):
    lengths = packed_lengths(key)
    ctx_count = ROWS // ROW_DEV
    end_device = (jnp.cumsum(lengths) - 1) // TOK_DEV
    longest = jnp.argmax(lengths).astype(jnp.int32)
    second = (longest + 1) % PROMPTS
    third = (longest + 2) % PROMPTS
    fourth = (longest + 3) % PROMPTS
    row_near = ((end_device[longest] - 1) % ctx_count * ROW_DEV).astype(jnp.int32)
    row_far = ((end_device[second] - ctx_count // 2) % ctx_count * ROW_DEV + ROW_DEV - 1).astype(jnp.int32)
    row_far = free_row(row_far, jnp.stack([row_near, row_near]))
    row_low = free_row(jnp.int32(0), jnp.stack([row_near, row_far]))
    row_high = free_row(jnp.int32(ROWS - 1), jnp.stack([row_near, row_far, row_low]))
    picks = jnp.zeros((PROMPTS,), jnp.int32)
    picks = picks.at[longest].set(row_near).at[second].set(row_far)
    picks = picks.at[third].set(row_low).at[fourth].set(row_high)
    return picks.astype(jnp.int32)


def draw_prefill_value(key, part):
    key = jax.random.fold_in(key, 11)
    key_base, key_rows = jax.random.split(key)
    upper = 3.0
    base = jnp.clip(jax.random.normal(key_base, (PROMPT_TOKENS, LHEADS, HD), jnp.float32), -6.0, 6.0)
    row_scale = jnp.exp(jax.random.uniform(key_rows, (PROMPT_TOKENS, 1, 1), jnp.float32, jnp.log(0.3), jnp.log(3.0)))
    return (base * row_scale * head_ramp(upper)[None, :, None]).astype(jnp.bfloat16)


def draw_log_decay(key, part):
    key = jax.random.fold_in(key, 13)
    random_key_select, random_key_quick, random_key_gradual, random_key_block, random_key_coarse, random_key_span, random_key_strength = jax.random.split(key, 7)
    share = 0.5
    fast = jax.random.uniform(random_key_select, (LHEADS,)) < share
    fast_rate = jnp.exp(jax.random.uniform(random_key_quick, (LHEADS,), jnp.float32, jnp.log(1.0 / 50.0), jnp.log(1.0 / 30.0)))
    slow_rate = jnp.exp(jax.random.uniform(random_key_gradual, (LHEADS,), jnp.float32, jnp.log(0.05), jnp.log(0.4))) / PROMPT_TOKENS
    decay_speed = jnp.where(fast, fast_rate, slow_rate)
    block_multiplier = jnp.exp(jax.random.uniform(random_key_block, (PROMPT_TOKENS // TOK_DEV, LHEADS), jnp.float32, jnp.log(0.5), jnp.log(2.0)))
    block_multiplier = jnp.repeat(block_multiplier, TOK_DEV, axis=0)
    coarse_noise = jnp.exp(jax.random.uniform(random_key_coarse, (PROMPT_TOKENS, LHEADS), jnp.float32, jnp.log(0.5), jnp.log(1.5)))
    decay_span_position = jax.random.randint(random_key_span, (3,), 0, PROMPT_TOKENS)
    decay_span = jnp.any(jnp.arange(PROMPT_TOKENS)[:, None] == decay_span_position[None, :], axis=1)[:, None]
    decay_strength = jnp.log(jax.random.uniform(random_key_strength, (PROMPT_TOKENS, LHEADS), jnp.float32, 0.6, 0.8))
    return -decay_speed[None, :] * block_multiplier * coarse_noise + jnp.where(decay_span, decay_strength, 0.0)


def draw_row_lengths(key, part):
    key = jax.random.fold_in(key, 19)
    key_one, key_two = jax.random.split(key)
    first_draw = jax.random.randint(key_one, (ROWS,), 0, CACHE - 1)
    second_draw = jax.random.randint(key_two, (ROWS,), 0, CACHE - 1)
    result = 2 + first_draw * second_draw // CACHE
    return result.at[0].set(CACHE).astype(jnp.int32)


def draw_decode_state(key, part):
    key = jax.random.fold_in(key, 31)
    upper = 3.0
    base = jnp.clip(jax.random.normal(key, (ROWS, LHEADS, HD, HD), jnp.float32), -6.0, 6.0)
    return base * head_ramp(upper)[None, :, None, None]


def draw_cache_keys(key, part):
    base = shared_keys(key)
    return base.astype(jnp.bfloat16)


def draw_soft_query(key, part):
    key = jax.random.fold_in(key, 29)
    query = jnp.clip(jax.random.normal(key, (STEPS, ROWS, SHEADS, HD), jnp.float32), -6.0, 6.0)
    return query.astype(jnp.bfloat16)


def steps_of(rng, extent, cuts, low, top_value):
    def one(dim, blocks):
        steps = jax.random.uniform(jax.random.fold_in(jax.random.fold_in(rng, 6), dim), (blocks,), jnp.float32, low / len(cuts), top_value / len(cuts))
        return jnp.repeat(jnp.exp(steps), extent[dim] // blocks).reshape((-1,) + (1,) * (len(extent) - dim - 1))

    loudness = one(*cuts[0])
    for cut in cuts[1:]:
        loudness = loudness * one(*cut)
    return loudness


def gaussian(rng, extent, scale, reach, cuts=(), kind=jnp.bfloat16):
    factor_of = steps_of(rng, extent, cuts, -0.22, 0.18) if cuts else 1.0
    array = jax.random.normal(rng, extent, jnp.float32) * scale * factor_of
    return jnp.minimum(jnp.maximum(array, -reach), reach).astype(kind)


def setup_inputs(seed: int = 0) -> dict:
    splits = jax.random.split(jax.random.key(seed), 18)
    return {
        "prefill_query": gaussian(splits[0], (PROMPT_TOKENS, LHEADS, HD), 1.0, 6.0, ((0, 64), (1, 8))),
        "prefill_key": gaussian(splits[1], (PROMPT_TOKENS, LHEADS, HD), HD ** -0.5, 0.5, ((0, 64), (1, 8))),
        "prefill_value": draw_prefill_value(jax.random.fold_in(splits[17], 71), 0),
        "log_decay": draw_log_decay(jax.random.fold_in(splits[17], 71), 0),
        "lengths": draw_lengths(jax.random.fold_in(splits[17], 71), 0),
        "owner": draw_owner(jax.random.fold_in(splits[17], 71), 0),
        "decode_state": draw_decode_state(jax.random.fold_in(splits[17], 71), 0),
        "step_query": gaussian(splits[7], (STEPS, ROWS, LHEADS, HD), 1.0, 6.0, ((1, 64), (2, 8))),
        "step_key": gaussian(splits[8], (STEPS, ROWS, LHEADS, HD), HD ** -0.5, 0.5, ((1, 64), (2, 8))),
        "step_value": gaussian(splits[9], (STEPS, ROWS, LHEADS, HD), 1.0, 6.0, ((1, 64), (2, 8))),
        "step_decay": jnp.clip(-0.7 + 0.69 * jax.random.uniform(splits[10], (STEPS, ROWS, LHEADS), jnp.float32) ** steps_of(splits[10], (STEPS, ROWS, LHEADS), ((1, 64), (2, 8)), -0.2, 0.2), -0.7, -0.01),
        "soft_query": draw_soft_query(jax.random.fold_in(splits[17], 71), 0),
        "cache_keys": draw_cache_keys(jax.random.fold_in(splits[17], 71), 0),
        "cache_values": gaussian(splits[13], (ROWS, CACHE, KVH, HD), 1.0, 6.0, ((0, 64), (2, 8))),
        "new_keys": gaussian(splits[14], (STEPS, ROWS, KVH, HD), 1.0, 6.0, ((1, 64), (2, 8))),
        "new_values": gaussian(splits[15], (STEPS, ROWS, KVH, HD), 1.0, 6.0, ((1, 64), (2, 8))),
        "row_lengths": draw_row_lengths(jax.random.fold_in(splits[17], 71), 0),
    }


precise = lax.Precision.HIGHEST
eps = 1e-06

def prompt_of(prompt_ends, positions):
    return lax.optimization_barrier(jnp.sum((positions[:, None] >= prompt_ends[None, :]).astype(jnp.int32), axis=1))

def head_block(pieces, visible):
    queries, key_rows, value_rows, running = pieces
    scores = jnp.dot(queries, key_rows.T, preferred_element_type=jnp.float32)
    decay_grid = jnp.exp(jnp.where(visible, running[:, None] - running[None, :], 0.0))
    weights = jnp.where(visible, scores * decay_grid, 0.0).astype(jnp.bfloat16)
    return jnp.dot(weights, value_rows, preferred_element_type=jnp.float32)

def block_pass(queries, key_rows, value_rows, running, segment, seg_prev, carried):
    block_size = segment.shape[0]
    offsets = jnp.arange(block_size)
    visible = (offsets[:, None] >= offsets[None, :]) & (segment[:, None] == segment[None, :])
    intra = lax.map(lambda pieces: head_block(pieces, visible), (jnp.moveaxis(queries, 1, 0), jnp.moveaxis(key_rows, 1, 0), jnp.moveaxis(value_rows, 1, 0), jnp.moveaxis(running, 1, 0)))
    intra = jnp.moveaxis(intra, 0, 1)
    carry_gate = (segment == seg_prev).astype(jnp.float32)[:, None] * jnp.exp(running)
    carried_term = jnp.einsum('thd,hde->the', queries.astype(jnp.float32), carried, precision=precise)
    return intra + carried_term * carry_gate[:, :, None]

def last_summary(key_rows, value_rows, log_decay, running, segment):
    last_prompt = segment[-1]
    inside = (segment == last_prompt)[:, None]
    weight = jnp.where(inside, jnp.exp(jnp.where(inside, running[-1][None, :] - running, 0.0)), 0.0)
    summary = jnp.einsum('thd,the->hde', key_rows.astype(jnp.float32) * weight[:, :, None], value_rows.astype(jnp.float32), precision=precise)
    decay_total = lax.optimization_barrier(jnp.sum(jnp.where(inside, log_decay, 0.0), axis=0))
    return (decay_total, summary)

def end_states(key_rows, value_rows, running, segment, seg_prev, carried, prompt_ends, block_start):
    block_size = segment.shape[0]
    positions = block_start + jnp.arange(block_size, dtype=jnp.int32)
    key_float = key_rows.astype(jnp.float32)
    value_float = value_rows.astype(jnp.float32)
    collected = []
    for prompt_id in range(prompt_ends.shape[0]):
        last_pos = prompt_ends[prompt_id] - 1
        ends_here = (last_pos >= block_start) & (last_pos < block_start + block_size)
        at_end = (positions == last_pos).astype(jnp.float32)
        running_end = jnp.dot(at_end, running, precision=precise)
        inside = (segment == prompt_id)[:, None] & ends_here
        weight = jnp.where(inside, jnp.exp(jnp.where(inside, running_end[None, :] - running, 0.0)), 0.0)
        summary = jnp.einsum('thd,the->hde', key_float * weight[:, :, None], value_float, precision=precise)
        lead_term = jnp.where(ends_here & (seg_prev == prompt_id), jnp.exp(running_end), 0.0)
        collected.append(summary + lead_term[:, None, None] * carried)
    return jnp.stack(collected)

def normalize(values_in, axes, count):
    square_sum = lax.optimization_barrier(jnp.sum(values_in * values_in, axis=axes, keepdims=True))
    return (values_in * lax.rsqrt(square_sum / count + eps)).astype(jnp.bfloat16)

def attend(query, cache_keys, cache_values, new_keys, new_values, row_lengths):
    step_count, row_count, head_count, head_width = query.shape
    groups = cache_keys.shape[2]
    grouped = query.astype(jnp.float32).reshape(step_count, row_count, groups, head_count // groups, head_width)
    inv_root = 1.0 / math.sqrt(head_width)
    cached_scores = jnp.einsum('srkgd,rckd->srkgc', grouped, cache_keys.astype(jnp.float32)) * inv_root
    fresh_scores = jnp.einsum('srkgd,jrkd->srkgj', grouped, new_keys.astype(jnp.float32)) * inv_root
    slot_ids = jnp.arange(cache_keys.shape[1], dtype=jnp.int32)
    live_mask = (slot_ids[None, :] < row_lengths[:, None])[None, :, None, None, :]
    step_ids = jnp.arange(step_count)
    seen_mask = (step_ids[None, :] <= step_ids[:, None])[:, None, None, None, :]
    cached_scores = jnp.where(live_mask, cached_scores, -jnp.inf)
    fresh_scores = jnp.where(seen_mask, fresh_scores, -jnp.inf)
    row_top = jnp.maximum(lax.optimization_barrier(jnp.max(cached_scores, axis=-1)), lax.optimization_barrier(jnp.max(fresh_scores, axis=-1)))[..., None]
    cached_exp = jnp.exp(cached_scores - row_top)
    fresh_exp = jnp.exp(fresh_scores - row_top)
    normalizer = (lax.optimization_barrier(jnp.sum(cached_exp, axis=-1)) + lax.optimization_barrier(jnp.sum(fresh_exp, axis=-1)))[..., None]
    cached_probs = (cached_exp / normalizer).astype(jnp.bfloat16)
    fresh_probs = (fresh_exp / normalizer).astype(jnp.bfloat16)
    mixed = jnp.einsum('srkgc,rckd->srkgd', cached_probs.astype(jnp.float32), cache_values.astype(jnp.float32))
    mixed = mixed + jnp.einsum('srkgj,jrkd->srkgd', fresh_probs.astype(jnp.float32), new_values.astype(jnp.float32))
    return mixed.reshape(step_count, row_count, head_count, head_width).astype(jnp.bfloat16)

def reference(prefill_query, prefill_key, prefill_value, log_decay, lengths, owner, decode_state, step_query, step_key, step_value, step_decay, soft_query, cache_keys, cache_values, new_keys, new_values, row_lengths):
    prompt_ends = jnp.cumsum(lengths).astype(jnp.int32)
    prompt_starts = prompt_ends - lengths

    def one_block(carry, block_id):
        carried, handed = carry
        block_start = (block_id * TOK_DEV).astype(jnp.int32)

        def take_rows(source):
            return lax.dynamic_slice_in_dim(source, block_start, TOK_DEV, 0)
        queries = take_rows(prefill_query)
        key_rows = take_rows(prefill_key)
        value_rows = take_rows(prefill_value)
        decay_rows = take_rows(log_decay)
        positions = block_start + jnp.arange(TOK_DEV, dtype=jnp.int32)
        segment = prompt_of(prompt_ends, positions)
        seg_prev = jnp.where(block_start > 0, prompt_of(prompt_ends, (block_start - 1)[None])[0], -1)
        running = jnp.cumsum(decay_rows, axis=0)
        mixed = block_pass(queries, key_rows, value_rows, running, segment, seg_prev, carried)
        handed = handed + end_states(key_rows, value_rows, running, segment, seg_prev, carried, prompt_ends, block_start)
        decay_total, summary = last_summary(key_rows, value_rows, decay_rows, running, segment)
        restart = jnp.any((prompt_starts >= block_start) & (prompt_starts < block_start + TOK_DEV))
        carried = jnp.where(restart, summary, jnp.exp(decay_total)[:, None, None] * carried + summary)
        return ((carried, handed), normalize(mixed, (1, 2), LHEADS * HD))
    initial = (jnp.zeros((LHEADS, HD, HD), jnp.float32), jnp.zeros((PROMPTS, LHEADS, HD, HD), jnp.float32))
    (carried, handed), blocks_out = lax.scan(one_block, initial, jnp.arange(PROMPT_TOKENS // TOK_DEV, dtype=jnp.int32))
    prefill_out = blocks_out.reshape(PROMPT_TOKENS, LHEADS, HD)
    row_ids = jnp.arange(ROWS, dtype=jnp.int32)
    owner_pick = (owner[None, :] == row_ids[:, None]).astype(jnp.float32)
    state = jnp.einsum('rp,phde->rhde', owner_pick, handed, precision=precise)
    state = state + (1.0 - lax.optimization_barrier(jnp.sum(owner_pick, axis=1)))[:, None, None, None] * decode_state
    step_reads = []
    for step_id in range(STEPS):
        outer_term = jnp.einsum('rhd,rhe->rhde', step_key[step_id].astype(jnp.float32), step_value[step_id].astype(jnp.float32), precision=precise)
        state = jnp.exp(step_decay[step_id])[:, :, None, None] * state + outer_term
        step_reads.append(jnp.einsum('rhd,rhde->rhe', step_query[step_id].astype(jnp.float32), state, precision=precise))
    decode_out = normalize(jnp.stack(step_reads), (2, 3), LHEADS * HD)
    soft_out = attend(soft_query, cache_keys, cache_values, new_keys, new_values, row_lengths)
    return (prefill_out, decode_out, soft_out)
```

```python
import functools
import math

import jax
import jax.numpy as jnp
from jax import lax
from jax.experimental import pallas as pl
from jax.experimental.pallas import tpu as pltpu
from jax.sharding import PartitionSpec as P

f32 = jnp.float32
bf16 = jnp.bfloat16
eps = 1e-06
HD = 128
HALF = HD // 2
ROW_END = 8
ROW_QUERY = 24
ROW_DECAY = 26
ROWS_OUT = 32
ROWS_BACK = 16
NT = (((1,), (1,)), ((), ()))
TN = (((0,), (0,)), ((), ()))
NN = (((1,), (0,)), ((), ()))


def mm(a, b, dims=NN):
    return lax.dot_general(a, b, dims, preferred_element_type=f32)


def iota(shape, dim):
    return lax.broadcasted_iota(jnp.int32, shape, dim)


def two(x):
    high = x.astype(bf16)
    return high, (x - high.astype(f32)).astype(bf16)


def three(x):
    high = x.astype(bf16)
    rest = x - high.astype(f32)
    mid = rest.astype(bf16)
    return high, mid, (rest - mid.astype(f32)).astype(bf16)


def prompt_bounds(lengths):
    ends, total = [], jnp.int32(0)
    starts = []
    for p in range(lengths.shape[0]):
        starts.append(total)
        total = total + lengths[p]
        ends.append(total)
    return starts, ends


def segment_of(positions, ends):
    segment = jnp.zeros(positions.shape, jnp.int32)
    for end in ends:
        segment = segment + (positions >= end).astype(jnp.int32)
    return segment


def scalar_segment(position, ends):
    segment = jnp.int32(0)
    for end in ends:
        segment = segment + (position >= end).astype(jnp.int32)
    return segment


def swap_halves(first, second):
    left = iota((1, HD), 1) < HALF
    shape = first.shape
    rolled_first = pltpu.roll(first.reshape(-1, HD), HALF, 1).reshape(shape)
    rolled_second = pltpu.roll(second.reshape(-1, HD), HALF, 1).reshape(shape)
    left = left.reshape((1,) * (len(shape) - 1) + (HD,))
    return jnp.where(left, first, rolled_second), jnp.where(left, rolled_first, second)


def cut(matrix):
    split = matrix.reshape(8, 2, 8, HD)
    low, high = swap_halves(split[:, 0], split[:, 1])
    return jnp.stack([low, high], axis=1).reshape(16, 8, HD)


def uncut(chunks):
    split = chunks.reshape(8, 2, 8, HD)
    low, high = swap_halves(split[:, 0], split[:, 1])
    return jnp.stack([low, high], axis=1).reshape(HD, HD)


def end_slot(slot, ends, block_start, block):
    prompt, offset = jnp.int32(-1), jnp.int32(-1)
    for p in range(len(ends)):
        if p % 2 != slot:
            continue
        local = ends[p] - 1 - block_start
        inside = (local >= 0) & (local < block) & (lax.rem(ends[p], block) != 0)
        prompt = jnp.where(inside, p, prompt)
        offset = jnp.where(inside, local, offset)
    return prompt, offset


def summary_kernel(lengths, decay, key, value, step_query, out, running_out):
    heads, block = decay.shape
    block_start = lax.axis_index("ctx") * block
    _, ends = prompt_bounds(lengths)
    place = iota((1, block), 1)
    segment = segment_of(place + block_start, ends)
    last = scalar_segment(block_start + block - 1, ends)
    prompt_a, offset_a = end_slot(0, ends, block_start, block)
    prompt_b, offset_b = end_slot(1, ends, block_start, block)

    parts = jnp.concatenate(three(decay[...]), axis=0)
    upto = (iota((block, block), 0) <= iota((block, block), 1)).astype(f32).astype(bf16)
    sums = mm(parts, upto)
    running = sums[:heads] + sums[heads : 2 * heads] + sums[2 * heads :]
    running_out[...] = jnp.concatenate([running, running], axis=0)

    row = iota((8, block), 0)
    spot = iota((8, block), 1)
    span = jnp.where(
        row == 0,
        (jnp.broadcast_to(segment, (8, block)) == last).astype(f32),
        jnp.where(
            row == 1,
            (spot <= offset_a).astype(f32),
            jnp.where(row == 2, (spot <= offset_b).astype(f32), 0.0),
        ),
    )
    spans = mm(span.astype(bf16), parts, NT)
    totals = spans[:, :heads] + spans[:, heads : 2 * heads] + spans[:, 2 * heads :]
    totals = jnp.concatenate([totals, jnp.zeros((8, HD - heads), f32)], axis=1)
    out[:, ROW_QUERY:ROWS_OUT, :] = jnp.zeros((out.shape[0], ROWS_OUT - ROW_QUERY, HD), f32)
    out[:, ROW_DECAY : ROW_DECAY + 3, :] = jnp.broadcast_to(
        totals[None, 0:3], (out.shape[0], 3, HD)
    )

    def weight(prompt, offset):
        inside = segment == prompt
        at = jnp.sum(jnp.where(place == offset, running, 0.0), axis=1, keepdims=True)
        return jnp.where(inside, jnp.exp(jnp.where(inside, at - running, 0.0)), 0.0)

    weights = jnp.concatenate(
        [
            weight(last, jnp.int32(block - 1)),
            weight(prompt_a, offset_a),
            weight(prompt_b, offset_b),
            jnp.zeros((4, block), f32),
        ],
        axis=0,
    )
    columns = weights.T

    keys = jnp.swapaxes(key[...], 0, 1)
    values = jnp.swapaxes(value[...], 0, 1)
    for h in range(heads):
        value_h = values[h].astype(f32)
        right = []
        for k in range(3):
            c = k * heads + h
            right.extend(two(value_h * columns[:, c : c + 1]))
        product = mm(keys[h], jnp.concatenate(right, axis=1), TN)
        for k in range(3):
            low = 2 * k * HD
            state = product[:, low : low + HD] + product[:, low + HD : low + 2 * HD]
            out[16 * h : 16 * h + 16, 8 * k : 8 * k + 8, :] = cut(state)

    steps, rows = step_query.shape[0], step_query.shape[1]
    flat = step_query[...].astype(f32).reshape(steps * rows * heads, HD).astype(bf16)
    d_at, lane = iota((HD, 8 * HD), 0), iota((HD, 8 * HD), 1)
    pick = (d_at == (lane // HD) * 16 + lane % 16).astype(f32).astype(bf16)
    spread = mm(flat, pick).reshape(steps, rows * heads, 8 * HD)
    step_at = iota((steps, 1, 8 * HD), 0)
    lane3 = iota((steps, 1, 8 * HD), 2)
    spread = jnp.sum(jnp.where((lane3 % HD) // 16 == step_at, spread, 0.0), axis=0)
    for r in range(rows):
        for h in range(heads):
            for d in range(8):
                piece = spread[r * heads + h : r * heads + h + 1, d * HD : (d + 1) * HD]
                for e in range(2):
                    j = 16 * h + 2 * d + e
                    out[j, ROW_QUERY + r : ROW_QUERY + r + 1, :] = piece


def local_kernel(
    lengths,
    owner,
    row_lengths,
    running_in,
    query,
    key,
    value,
    decode_state,
    step_query,
    step_key,
    step_value,
    step_decay,
    soft_query,
    cache_keys,
    cache_values,
    new_keys,
    new_values,
    intra_out,
    query_out,
    gate_out,
    base_out,
    coef_out,
    soft_out,
):
    block, heads, _ = query.shape
    device = lax.axis_index("ctx")
    block_start = device * block
    _, ends = prompt_bounds(lengths)
    running = running_in[...]
    columns = running.T
    place_row = iota((1, block), 1) + block_start
    place_col = iota((block, 1), 0) + block_start
    segment_row = segment_of(place_row, ends)
    segment_col = segment_of(place_col, ends)
    before = jnp.where(block_start > 0, scalar_segment(block_start - 1, ends), -1)
    gate_out[...] = jnp.where(segment_col == before, jnp.exp(columns), 0.0)

    queries = jnp.swapaxes(query[...], 0, 1)
    keys = jnp.swapaxes(key[...], 0, 1)
    values = jnp.swapaxes(value[...], 0, 1)
    query_out[...] = queries
    half = block // 2
    tiles = ((0, 0), (1, 0), (1, 1))
    masks = {}
    for a, b in tiles:
        rows = slice(a * half, (a + 1) * half)
        cols = slice(b * half, (b + 1) * half)
        seen = segment_col[rows] == segment_row[:, cols]
        if a == b:
            seen = seen & (place_col[rows] >= place_row[:, cols])
        masks[a, b] = jnp.where(seen, 0.0, -1e30)
    for h in range(heads):
        mixed = [None, None]
        for a, b in tiles:
            rows = slice(a * half, (a + 1) * half)
            cols = slice(b * half, (b + 1) * half)
            scores = mm(queries[h][rows], keys[h][cols], NT)
            gap = columns[rows, h : h + 1] - running[h : h + 1, cols]
            weights = (scores * jnp.exp(gap + masks[a, b])).astype(bf16)
            term = mm(weights, values[h][cols])
            mixed[a] = term if mixed[a] is None else mixed[a] + term
        intra_out[h, :half, :] = mixed[0]
        intra_out[h, half:, :] = mixed[1]

    steps, rows_n = step_query.shape[0], step_query.shape[1]

    def by_head(ref):
        whole = ref[...].astype(f32).reshape(steps, rows_n * heads, HD)
        return jnp.swapaxes(whole, 0, 1)

    sq, sk, sv = by_head(step_query), by_head(step_key), by_head(step_value)
    decays = step_decay[...].reshape(rows_n * heads, steps)
    upto = (iota((steps, steps), 0) <= iota((steps, steps), 1)).astype(f32)
    cum_row = lax.dot_general(
        decays, upto, NN, precision=lax.Precision.HIGHEST, preferred_element_type=f32
    )
    cum_col = cum_row.T
    causal = iota((steps, steps), 0) >= iota((steps, steps), 1)
    for r in range(rows_n):
        owned = jnp.int32(0)
        for p in range(len(ends)):
            owned = owned + (owner[p] == device * rows_n + r).astype(jnp.int32)
        owned = jnp.where(owned > 0, 1.0, 0.0)
        for h in range(heads):
            n = r * heads + h
            cum = cum_col[:, n : n + 1]
            gap = jnp.where(causal, cum - cum_row[n : n + 1, :], 0.0)
            inner = mm(sq[n].astype(bf16), sk[n].astype(bf16), NT)
            inner = jnp.where(causal, inner * jnp.exp(gap), 0.0)
            fresh = lax.dot_general(
                inner, sv[n], NN, precision=lax.Precision.HIGHEST, preferred_element_type=f32
            )
            high, low = two(decode_state[r, h])
            read = mm(sq[n].astype(bf16), jnp.concatenate([high, low], axis=1))
            grown = jnp.exp(cum)
            read = (read[:, :HD] + read[:, HD:]) * grown
            base_out[n] = fresh + jnp.where(owned > 0.5, 0.0, read)
            coef_out[n] = jnp.broadcast_to(grown * owned, (steps, HD))

    fresh_keys = jnp.swapaxes(new_keys[...].astype(f32), 0, 1)
    fresh_values = jnp.swapaxes(new_values[...].astype(f32), 0, 1)
    group = soft_query.shape[2]
    cache = cache_keys.shape[1]
    scale = 1.0 / math.sqrt(HD)
    whole = soft_query[...].astype(f32)
    for r in range(rows_n):
        rows_q = whole[:, r].reshape(steps * group, HD).astype(bf16)
        cached = mm(rows_q, cache_keys[r], NT) * scale
        recent = mm(rows_q, fresh_keys[r].astype(bf16), NT) * scale
        slot = iota((steps * group, cache), 1)
        cached = jnp.where(slot < row_lengths[r], cached, -jnp.inf)
        step_of = iota((steps * group, steps), 0) // group
        recent = jnp.where(iota((steps * group, steps), 1) <= step_of, recent, -jnp.inf)
        top = jnp.maximum(
            jnp.max(cached, axis=1, keepdims=True), jnp.max(recent, axis=1, keepdims=True)
        )
        cached = jnp.exp(cached - top)
        recent = jnp.exp(recent - top)
        total = jnp.sum(cached, axis=1, keepdims=True) + jnp.sum(recent, axis=1, keepdims=True)
        cached = (cached / total).astype(bf16)
        recent = (recent / total).astype(bf16)
        mixed = mm(cached, cache_values[r]) + mm(recent, fresh_values[r].astype(bf16))
        soft_out[:, r, :, :] = mixed.reshape(steps, group, HD).astype(bf16)


def scan_kernel(lengths, owner, got, out, carried):
    blocks = got.shape[0]
    block = lengths_block(blocks)
    device = lax.axis_index("ctx")
    head = device // 16
    starts, ends = prompt_bounds(lengths)
    padded = carried.shape[0]

    decays = got[:, ROW_DECAY, :]
    decay = jnp.sum(
        jnp.where(iota((blocks, HD), 1) == head, decays, 0.0), axis=1, keepdims=True
    )
    k_at, b_at = iota((blocks, blocks), 0), iota((blocks, blocks), 1)
    later = jnp.concatenate(
        [jnp.where(k_at > b_at, part.astype(f32), 0.0).astype(bf16) for part in three(decay)],
        axis=1,
    )
    earlier = (iota((padded, blocks), 1) < iota((padded, blocks), 0)).astype(f32).astype(bf16)
    gaps = mm(earlier, later)
    gap = gaps[:, :blocks] + gaps[:, blocks : 2 * blocks] + gaps[:, 2 * blocks :]
    to, frm = iota((padded, blocks), 0), iota((padded, blocks), 1)
    linked = frm < to
    for start in starts:
        restart = start // block
        linked = linked & ~((restart > frm) & (restart < to))
    weight = jnp.where(linked, jnp.exp(jnp.where(linked, gap, 0.0)), 0.0)
    weights = jnp.concatenate(two(weight), axis=0)
    for i in range(8):
        high, low = two(got[:, i, :])
        product = mm(weights, jnp.concatenate([high, low], axis=1))
        state = product[:padded, :HD] + product[padded:, :HD] + product[:padded, HD:]
        carried[:, i, :] = state
        out[:, i, :] = state[:blocks]

    out[:, 8:ROWS_BACK, :] = jnp.zeros((blocks, ROWS_BACK - 8, HD), f32)
    rows_n = 2
    for p in range(len(ends)):
        slot = p % 2
        index = ends[p] // block
        source = jnp.minimum(index, blocks - 1)
        partial = (lax.rem(ends[p], block) != 0).astype(f32)
        leads = (starts[p] < index * block).astype(f32)
        run = got[source, ROW_DECAY + 1 + slot : ROW_DECAY + 2 + slot, :]
        run = jnp.sum(jnp.where(iota((1, HD), 1) == head, run, 0.0), axis=1, keepdims=True)
        lead = leads * jnp.exp(run * partial)
        low_row = ROW_END + 8 * slot
        handed = carried[index] * lead + got[source, low_row : low_row + 8, :] * partial
        high, low = two(jnp.concatenate([handed[:, :HALF], handed[:, HALF:]], axis=0))
        right = jnp.concatenate([jnp.concatenate([high, low], axis=1)] * 8, axis=0)
        place = owner[p] // rows_n
        side = lax.rem(owner[p], rows_n)
        pair = got[place, ROW_QUERY : ROW_QUERY + rows_n, :]
        query = jnp.where(side == 0, pair[0:1], pair[1:2])
        steps = 8
        lane = iota((steps, HD), 1)
        query = jnp.where(lane // 16 == iota((steps, HD), 0), query, 0.0).astype(bf16)
        read = mm(query, right)
        read = read[:, :HALF] + read[:, HALF:]
        both = jnp.concatenate([read, read], axis=1)
        old = out[place, 8:ROWS_BACK, :]
        out[place, 8:ROWS_BACK, :] = jnp.where(lane // HALF == side, both, old)


def lengths_block(blocks):
    return 512


def mix_kernel(got, intra, query, gate, base, coef, mixed_out, reads_out, squares_out):
    heads, block, _ = intra.shape
    total = None
    for h in range(heads):
        state = uncut(got[16 * h : 16 * h + 16, 0:8, :])
        high, low = two(state)
        read = mm(query[h], jnp.concatenate([high, low], axis=1))
        mixed = intra[h] + (read[:, :HD] + read[:, HD:]) * gate[:, h : h + 1]
        mixed_out[h] = mixed
        total = mixed * mixed if total is None else total + mixed * mixed
    ones = jnp.ones((8, HD), bf16)
    high, low = two(total)
    squares_out[:, 0, :block] = mm(ones, high, NT) + mm(ones, low, NT)

    rows_n = base.shape[0] // heads
    squares = [None] * rows_n
    for h in range(heads):
        first, second = None, None
        for d in range(8):
            a = got[16 * h + 2 * d, 8:16, :]
            b = got[16 * h + 2 * d + 1, 8:16, :]
            first = a if first is None else first + a
            second = b if second is None else second + b
        for r, handed in enumerate(swap_halves(first, second)):
            n = r * heads + h
            read = base[n] + coef[n] * handed
            reads_out[n] = read
            squares[r] = read * read if squares[r] is None else squares[r] + read * read
    high, low = two(jnp.concatenate(squares, axis=0))
    sums = mm(ones, high, NT) + mm(ones, low, NT)
    squares_out[:, 0, block:] = jnp.concatenate(
        [sums, jnp.zeros((8, HD - sums.shape[1]), f32)], axis=1
    )


def norm_kernel(count, got, mixed, reads, prefill_out, decode_out):
    heads, block, _ = mixed.shape
    parts = jnp.concatenate(three(got[:, 0, :]), axis=0)
    ones = jnp.ones((parts.shape[0], HD), bf16)
    total = mm(parts, ones, TN)
    scale = lax.rsqrt(total / count + eps)
    scaled = jnp.stack([mixed[h] * scale[:block] for h in range(heads)], axis=0)
    prefill_out[...] = jnp.swapaxes(scaled, 0, 1).astype(bf16)
    steps, rows_n = decode_out.shape[0], decode_out.shape[1]
    pieces = []
    for r in range(rows_n):
        low = block + r * steps
        for h in range(heads):
            pieces.append(reads[r * heads + h] * scale[low : low + steps])
    scaled = jnp.swapaxes(jnp.stack(pieces, axis=0), 0, 1)
    decode_out[...] = scaled.reshape(decode_out.shape).astype(bf16)


def call(kernel, name, outs, scalars, arrays, scratch=(), cost=0):
    shapes = [jax.ShapeDtypeStruct(shape, dtype) for shape, dtype in outs]
    specs = [pl.BlockSpec(memory_space=pltpu.SMEM)] * len(scalars)
    specs += [pl.BlockSpec(memory_space=pltpu.VMEM)] * len(arrays)
    return pl.pallas_call(
        kernel,
        name=name,
        out_shape=shapes,
        in_specs=specs,
        out_specs=[pl.BlockSpec(memory_space=pltpu.VMEM)] * len(outs),
        scratch_shapes=list(scratch),
        compiler_params=pltpu.CompilerParams(vmem_limit_bytes=24 * 2**20),
        cost_estimate=pl.CostEstimate(flops=cost, bytes_accessed=4 * 2**20, transcendentals=0),
    )(*scalars, *arrays)


def body(
    prefill_query,
    prefill_key,
    prefill_value,
    log_decay,
    lengths,
    owner,
    decode_state,
    step_query,
    step_key,
    step_value,
    step_decay,
    soft_query,
    cache_keys,
    cache_values,
    new_keys,
    new_values,
    row_lengths,
):
    block, heads, _ = prefill_query.shape
    steps, rows_n = step_query.shape[0], step_query.shape[1]
    blocks = lax.axis_size("ctx")
    planes = lax.axis_size("head")
    pairs = rows_n * heads
    decay_rows = jnp.swapaxes(log_decay, 0, 1)
    outgoing, running = call(
        summary_kernel,
        "summary",
        [((blocks, ROWS_OUT, HD), f32), ((8, block), f32)],
        [lengths],
        [decay_rows, prefill_key, prefill_value, step_query],
    )
    gathered = lax.all_to_all(outgoing, "ctx", 0, 0, tiled=True)
    intra, queries, gate, base, coef, soft_out = call(
        local_kernel,
        "local",
        [
            ((heads, block, HD), f32),
            ((heads, block, HD), bf16),
            ((block, 8), f32),
            ((pairs, steps, HD), f32),
            ((pairs, steps, HD), f32),
            (soft_query.shape, bf16),
        ],
        [lengths, owner, row_lengths],
        [
            running,
            prefill_query,
            prefill_key,
            prefill_value,
            decode_state,
            step_query,
            step_key,
            step_value,
            jnp.transpose(step_decay, (1, 2, 0)),
            soft_query,
            cache_keys.reshape(rows_n, -1, HD),
            cache_values.reshape(rows_n, -1, HD),
            new_keys.reshape(steps, rows_n, HD),
            new_values.reshape(steps, rows_n, HD),
        ],
        cost=2 * 10**9,
    )
    returning = call(
        scan_kernel,
        "scan",
        [((blocks, ROWS_BACK, HD), f32)],
        [lengths, owner],
        [gathered],
        scratch=[pltpu.VMEM((blocks + 8, 8, HD), f32)],
    )[0]
    returned = lax.all_to_all(returning, "ctx", 0, 0, tiled=True)
    mixed, reads, squares = call(
        mix_kernel,
        "mix",
        [
            ((heads, block, HD), f32),
            ((pairs, steps, HD), f32),
            ((planes, 1, block + HD), f32),
        ],
        [],
        [returned, intra, queries, gate, base, coef],
    )
    squares = lax.all_to_all(squares, "head", 0, 0, tiled=True)
    prefill_out, decode_out = call(
        functools.partial(norm_kernel, float(planes * heads * HD)),
        "norm",
        [(prefill_query.shape, bf16), (step_query.shape, bf16)],
        [],
        [squares, mixed, reads],
    )
    return (prefill_out, decode_out, soft_out)


def solution(mesh):
    placed = (
        P("ctx", "head", None),
        P("ctx", "head", None),
        P("ctx", "head", None),
        P("ctx", "head"),
        P(),
        P(),
        P("ctx", "head", None, None),
        P(None, "ctx", "head", None),
        P(None, "ctx", "head", None),
        P(None, "ctx", "head", None),
        P(None, "ctx", "head"),
        P(None, "ctx", "head", None),
        P("ctx", None, "head", None),
        P("ctx", None, "head", None),
        P(None, "ctx", "head", None),
        P(None, "ctx", "head", None),
        P("ctx"),
    )
    return jax.shard_map(
        body,
        mesh=mesh,
        in_specs=placed,
        out_specs=(
            P("ctx", "head", None),
            P(None, "ctx", "head", None),
            P(None, "ctx", "head", None),
        ),
        check_vma=False,
    )
```

```python
import functools
import math

import jax
import jax.numpy as jnp
from jax import lax
from jax.experimental import pallas as pl
from jax.experimental.pallas import tpu as pltpu
from jax.sharding import PartitionSpec as P

f32 = jnp.float32
bf16 = jnp.bfloat16
eps = 1e-06
HD = 128
HALF = HD // 2
ROW_END = 8
ROW_QUERY = 16
ROW_DECAY = 18
ROWS_OUT = 19
ROWS_BACK = 16
NT = (((1,), (1,)), ((), ()))
TN = (((0,), (0,)), ((), ()))
NN = (((1,), (0,)), ((), ()))


def mm(a, b, dims=NN):
    return lax.dot_general(a, b, dims, preferred_element_type=f32)


def iota(shape, dim):
    return lax.broadcasted_iota(jnp.int32, shape, dim)


def two(x):
    high = x.astype(bf16)
    return high, (x - high.astype(f32)).astype(bf16)


def three(x):
    high = x.astype(bf16)
    rest = x - high.astype(f32)
    mid = rest.astype(bf16)
    return high, mid, (rest - mid.astype(f32)).astype(bf16)


def prompt_bounds(lengths):
    ends, total = [], jnp.int32(0)
    starts = []
    for p in range(lengths.shape[0]):
        starts.append(total)
        total = total + lengths[p]
        ends.append(total)
    return starts, ends


def segment_of(positions, ends):
    segment = jnp.zeros(positions.shape, jnp.int32)
    for end in ends:
        segment = segment + (positions >= end).astype(jnp.int32)
    return segment


def scalar_segment(position, ends):
    segment = jnp.int32(0)
    for end in ends:
        segment = segment + (position >= end).astype(jnp.int32)
    return segment


def swap_halves(first, second):
    left = iota((1, HD), 1) < HALF
    shape = first.shape
    rolled_first = pltpu.roll(first.reshape(-1, HD), HALF, 1).reshape(shape)
    rolled_second = pltpu.roll(second.reshape(-1, HD), HALF, 1).reshape(shape)
    left = left.reshape((1,) * (len(shape) - 1) + (HD,))
    return jnp.where(left, first, rolled_second), jnp.where(left, rolled_first, second)


def cut(matrix):
    split = matrix.reshape(8, 2, 8, HD)
    low, high = swap_halves(split[:, 0], split[:, 1])
    return jnp.stack([low, high], axis=1).reshape(16, 8, HD)


def uncut(chunks):
    split = chunks.reshape(8, 2, 8, HD)
    low, high = swap_halves(split[:, 0], split[:, 1])
    return jnp.stack([low, high], axis=1).reshape(HD, HD)


def running_sums(decay):
    heads, block = decay.shape
    upto = (iota((HD, 1), 0) <= iota((1, HD), 1)).astype(f32).astype(bf16)
    pieces = [decay[:, low : low + HD] for low in range(0, block, HD)]
    stacked = jnp.concatenate(pieces, axis=0)
    local = sum(mm(part, upto) for part in three(stacked))
    out, before = [], None
    for k in range(len(pieces)):
        piece = local[k * heads : (k + 1) * heads]
        if before is not None:
            piece = piece + before
        out.append(piece)
        before = piece[:, HD - 1 : HD]
    return jnp.concatenate(out, axis=1)


def end_slot(slot, ends, block_start, block):
    prompt, offset = jnp.int32(-1), jnp.int32(-1)
    for p in range(len(ends)):
        if p % 2 != slot:
            continue
        local = ends[p] - 1 - block_start
        inside = (local >= 0) & (local < block) & (lax.rem(ends[p], block) != 0)
        prompt = jnp.where(inside, p, prompt)
        offset = jnp.where(inside, local, offset)
    return prompt, offset


def block_shares(first, second, block):
    inside = (lax.rem(first, block) != 0) & (lax.rem(second, block) != 0)
    return inside & (first // block == second // block)


def summary_kernel(
    lengths,
    decay,
    key,
    value,
    step_query,
    out,
    second_out,
    shared_out,
    key_buf,
    value_buf,
    decay_buf,
    query_buf,
    sems,
):
    copies = [
        pltpu.make_async_copy(decay, decay_buf, sems.at[0]),
        pltpu.make_async_copy(step_query, query_buf, sems.at[1]),
    ]
    heads, block = decay_buf.shape
    quarter = block // 4
    for k in range(4):
        part = pl.ds(k * quarter, quarter)
        copies.append(pltpu.make_async_copy(key.at[part], key_buf.at[part], sems.at[2 + k]))
        copies.append(pltpu.make_async_copy(value.at[part], value_buf.at[part], sems.at[6 + k]))
    for copy in copies:
        copy.start()

    block_start = lax.axis_index("ctx") * block
    _, ends = prompt_bounds(lengths)
    shared = jnp.bool_(False)
    for other in range(0, len(ends), 2):
        shared = shared | block_shares(ends[1], ends[other], block)
    shared_out[0] = shared.astype(jnp.int32)
    place = iota((1, block), 1)
    segment = segment_of(place + block_start, ends)
    last = scalar_segment(block_start + block - 1, ends)
    prompt_a, offset_a = end_slot(0, ends, block_start, block)
    prompt_b, offset_b = end_slot(1, ends, block_start, block)
    both = (prompt_a >= 0) & (prompt_b >= 0)
    prompt_a = jnp.where(prompt_a >= 0, prompt_a, prompt_b)
    offset_a = jnp.where(offset_a >= 0, offset_a, offset_b)
    copies[0].wait()
    running = running_sums(decay_buf[...])

    def weight(prompt, offset):
        inside = segment == prompt
        at = jnp.sum(jnp.where(place == offset, running, 0.0), axis=1, keepdims=True)
        weight = jnp.where(inside, jnp.exp(jnp.where(inside, at - running, 0.0)), 0.0)
        return weight, at

    weight_last, _ = weight(last, jnp.int32(block - 1))
    weight_a, at_a = weight(prompt_a, offset_a)
    weight_b, at_b = weight(prompt_b, offset_b)
    whole = jnp.sum(jnp.where(segment == last, decay_buf[...], 0.0), axis=1, keepdims=True)
    lane, head = iota((heads, HD), 1), iota((heads, HD), 0)
    totals = jnp.where(lane == head, whole, 0.0)
    totals = jnp.where(lane == heads + head, at_a, totals)
    totals = jnp.where(lane == 2 * heads + head, at_b, totals)
    totals = jnp.sum(totals, axis=0, keepdims=True)
    out[:, ROW_DECAY, 0, :] = jnp.broadcast_to(totals, (out.shape[0], HD))

    weights = jnp.concatenate(
        [
            weight_last,
            weight_a,
            weight_b,
            jnp.zeros((4, block), f32),
        ],
        axis=0,
    )
    columns = weights.T

    copies[1].wait()
    steps, rows = query_buf.shape[0], query_buf.shape[1]
    flat = query_buf[...].astype(f32).reshape(steps * rows * heads, HD).astype(bf16)
    lane = iota((1, 8 * HD), 1)
    pick = (iota((HD, 1), 0) == (lane // HD) * 16 + lane % 16).astype(f32).astype(bf16)
    read = mm(flat, pick)
    spread = None
    for step in range(steps):
        mine = (lane % HD) // 16 == step
        part = jnp.where(mine, read[step * rows * heads : (step + 1) * rows * heads], 0.0)
        spread = part if spread is None else spread + part
    for r in range(rows):
        for h in range(heads):
            for d in range(8):
                piece = spread[r * heads + h : r * heads + h + 1, d * HD : (d + 1) * HD]
                for e in range(2):
                    out[16 * h + 2 * d + e, ROW_QUERY + r, :, :] = piece

    for copy in copies[2:]:
        copy.wait()
    keys = jnp.swapaxes(key_buf[...], 0, 1)
    values = jnp.swapaxes(value_buf[...], 0, 1)
    for h in range(heads):
        value_h = values[h].astype(f32)
        right = []
        for k in range(2):
            c = k * heads + h
            right.extend(two(value_h * columns[:, c : c + 1]))
        product = mm(keys[h], jnp.concatenate(right, axis=1), TN)
        for k in range(2):
            low = 2 * k * HD
            state = product[:, low : low + HD] + product[:, low + HD : low + 2 * HD]
            out[16 * h : 16 * h + 16, 8 * k : 8 * k + 8, 0, :] = cut(state)

    @pl.when(both)
    def _():
        for h in range(heads):
            c = 2 * heads + h
            right = jnp.concatenate(two(values[h].astype(f32) * columns[:, c : c + 1]), axis=1)
            product = mm(keys[h], right, TN)
            second_out[16 * h : 16 * h + 16] = cut(product[:, :HD] + product[:, HD:])

    @pl.when(jnp.logical_not(both))
    def _():
        second_out[...] = jnp.zeros(second_out.shape, f32)


def local_kernel(lengths, owner, row_lengths, *refs):
    count = (len(refs) - 7) // 2
    sources, outs = refs[:count], refs[count : count + 6]
    buffers, sems = refs[count + 6 : -1], refs[-1]
    copies = [
        pltpu.make_async_copy(source, buffer, sems.at[k])
        for k, (source, buffer) in enumerate(zip(sources, buffers))
    ]
    for copy in copies:
        copy.start()
    for copy in copies:
        copy.wait()
    (
        log_decay,
        query,
        key,
        value,
        decode_state,
        step_query,
        step_key,
        step_value,
        step_decay,
        soft_query,
        cache_keys,
        cache_values,
        new_keys,
        new_values,
    ) = buffers
    intra_out, query_out, gate_out, base_out, coef_out, soft_out = outs
    block, heads, _ = query.shape
    device = lax.axis_index("ctx")
    block_start = device * block
    _, ends = prompt_bounds(lengths)
    running = running_sums(log_decay[...])
    columns = jnp.concatenate([running, running], axis=0).T
    place_row = iota((1, block), 1) + block_start
    place_col = iota((block, 1), 0) + block_start
    segment_row = segment_of(place_row, ends)
    segment_col = segment_of(place_col, ends)
    before = jnp.where(block_start > 0, scalar_segment(block_start - 1, ends), -1)
    gate_out[...] = jnp.where(segment_col == before, jnp.exp(columns), 0.0)

    queries = jnp.swapaxes(query[...], 0, 1)
    keys = jnp.swapaxes(key[...], 0, 1)
    values = jnp.swapaxes(value[...], 0, 1)
    query_out[...] = queries
    half = block // 2
    tiles = ((0, 0), (1, 0), (1, 1))
    masks = {}
    for a, b in tiles:
        rows = slice(a * half, (a + 1) * half)
        cols = slice(b * half, (b + 1) * half)
        seen = segment_col[rows] == segment_row[:, cols]
        if a == b:
            seen = seen & (place_col[rows] >= place_row[:, cols])
        masks[a, b] = jnp.where(seen, 0.0, -1e30)
    for h in range(heads):
        mixed = [None, None]
        for a, b in tiles:
            rows = slice(a * half, (a + 1) * half)
            cols = slice(b * half, (b + 1) * half)
            scores = mm(queries[h][rows], keys[h][cols], NT)
            gap = columns[rows, h : h + 1] - running[h : h + 1, cols]
            weights = (scores * jnp.exp(gap + masks[a, b])).astype(bf16)
            term = mm(weights, values[h][cols])
            mixed[a] = term if mixed[a] is None else mixed[a] + term
        intra_out[h, :half, :] = mixed[0]
        intra_out[h, half:, :] = mixed[1]

    steps, rows_n = step_query.shape[0], step_query.shape[1]

    def by_head(ref):
        whole = ref[...].astype(f32).reshape(steps, rows_n * heads, HD)
        return jnp.swapaxes(whole, 0, 1)

    sq, sk, sv = by_head(step_query), by_head(step_key), by_head(step_value)
    decays = step_decay[...].reshape(rows_n * heads, steps)
    upto = (iota((steps, steps), 0) <= iota((steps, steps), 1)).astype(f32)
    cum_row = lax.dot_general(
        decays, upto, NN, precision=lax.Precision.HIGHEST, preferred_element_type=f32
    )
    cum_col = cum_row.T
    causal = iota((steps, steps), 0) >= iota((steps, steps), 1)
    for r in range(rows_n):
        owned = jnp.int32(0)
        for p in range(len(ends)):
            owned = owned + (owner[p] == device * rows_n + r).astype(jnp.int32)
        owned = jnp.where(owned > 0, 1.0, 0.0)
        for h in range(heads):
            n = r * heads + h
            cum = cum_col[:, n : n + 1]
            gap = jnp.where(causal, cum - cum_row[n : n + 1, :], 0.0)
            inner = mm(sq[n].astype(bf16), sk[n].astype(bf16), NT)
            inner = jnp.where(causal, inner * jnp.exp(gap), 0.0)
            fresh = lax.dot_general(
                inner, sv[n], NN, precision=lax.Precision.HIGHEST, preferred_element_type=f32
            )
            high, low = two(decode_state[r, h])
            read = mm(sq[n].astype(bf16), jnp.concatenate([high, low], axis=1))
            grown = jnp.exp(cum)
            read = (read[:, :HD] + read[:, HD:]) * grown
            base_out[n] = fresh + jnp.where(owned > 0.5, 0.0, read)
            coef_out[n] = jnp.broadcast_to(grown * owned, (steps, HD))

    fresh_keys = jnp.swapaxes(new_keys[...].astype(f32), 0, 1)
    fresh_values = jnp.swapaxes(new_values[...].astype(f32), 0, 1)
    group = soft_query.shape[2]
    cache = cache_keys.shape[1]
    scale = 1.0 / math.sqrt(HD)
    whole = soft_query[...].astype(f32)
    for r in range(rows_n):
        rows_q = whole[:, r].reshape(steps * group, HD).astype(bf16)
        cached = mm(rows_q, cache_keys[r], NT) * scale
        recent = mm(rows_q, fresh_keys[r].astype(bf16), NT) * scale
        slot = iota((steps * group, cache), 1)
        cached = jnp.where(slot < row_lengths[r], cached, -jnp.inf)
        step_of = iota((steps * group, steps), 0) // group
        recent = jnp.where(iota((steps * group, steps), 1) <= step_of, recent, -jnp.inf)
        top = jnp.maximum(
            jnp.max(cached, axis=1, keepdims=True), jnp.max(recent, axis=1, keepdims=True)
        )
        cached = jnp.exp(cached - top)
        recent = jnp.exp(recent - top)
        total = jnp.sum(cached, axis=1, keepdims=True) + jnp.sum(recent, axis=1, keepdims=True)
        cached = (cached / total).astype(bf16)
        recent = (recent / total).astype(bf16)
        mixed = mm(cached, cache_values[r]) + mm(recent, fresh_values[r].astype(bf16))
        soft_out[:, r, :, :] = mixed.reshape(steps, group, HD).astype(bf16)


def scan_kernel(block, lengths, owner, got, second, out, carried):
    blocks = got.shape[0]
    device = lax.axis_index("ctx")
    head = device // 16
    starts, ends = prompt_bounds(lengths)
    padded = carried.shape[0]
    heads = blocks // 16

    decays = got[:, ROW_DECAY, 0, :]
    decay = jnp.sum(
        jnp.where(iota((blocks, HD), 1) == head, decays, 0.0), axis=1, keepdims=True
    )
    k_at, b_at = iota((blocks, blocks), 0), iota((blocks, blocks), 1)
    later = jnp.concatenate(
        [jnp.where(k_at > b_at, part.astype(f32), 0.0).astype(bf16) for part in three(decay)],
        axis=0,
    )
    earlier = iota((padded, 3 * blocks), 1) % blocks < iota((padded, 3 * blocks), 0)
    gap = mm(earlier.astype(f32).astype(bf16), later)
    to, frm = iota((padded, blocks), 0), iota((padded, blocks), 1)
    linked = frm < to
    for start in starts:
        restart = start // block
        linked = linked & ~((restart > frm) & (restart < to))
    weight = jnp.where(linked, jnp.exp(jnp.where(linked, gap, 0.0)), 0.0)
    high, low = two(weight)
    weights = jnp.concatenate([high, high, low], axis=1)
    right = []
    for i in range(8):
        high, low = two(got[:, i, 0, :])
        right.append(jnp.concatenate([high, low, high], axis=0))
    product = mm(weights, jnp.concatenate(right, axis=1))
    for i in range(8):
        state = product[:, i * HD : (i + 1) * HD]
        carried[:, i, :] = state
        out[:, i, 0, :] = state[:blocks]
        out[:, 8 + i, 0, :] = jnp.zeros((blocks, HD), f32)

    rows_n = ROW_DECAY - ROW_QUERY
    steps = 8
    lane = iota((steps, HD), 1)
    reads = []
    for p in range(len(ends)):
        index = ends[p] // block
        source = jnp.minimum(index, blocks - 1)
        partial = lax.rem(ends[p], block) != 0
        leads = (starts[p] < index * block).astype(f32)
        if p % 2:
            shared = jnp.bool_(False)
            for other in range(0, len(ends), 2):
                shared = shared | block_shares(ends[p], ends[other], block)
        else:
            shared = jnp.bool_(False)
        run = got[source, ROW_DECAY, :, :]
        at = jnp.where(shared, 2 * heads, heads) + head
        run = jnp.sum(jnp.where(iota((1, HD), 1) == at, run, 0.0), axis=1, keepdims=True)
        lead = leads * jnp.exp(jnp.where(partial, run, 0.0))
        rest = got[source, ROW_END : ROW_END + 8, 0, :]
        if p % 2:
            rest = jnp.where(shared, second[source], rest)
        handed = carried[index] * lead + jnp.where(partial, rest, 0.0)
        high, low = two(jnp.concatenate([handed[:, :HALF], handed[:, HALF:]], axis=0))
        both = jnp.concatenate([jnp.concatenate([high, low], axis=1)] * 8, axis=0)
        place = owner[p] // rows_n
        side = lax.rem(owner[p], rows_n)
        query = got[place, ROW_QUERY + side, :, :]
        query = jnp.where(lane // 16 == iota((steps, HD), 0), query, 0.0).astype(bf16)
        read = mm(query, both)
        read = read[:, :HALF] + read[:, HALF:]
        reads.append((place, side, jnp.concatenate([read, read], axis=1)))
    for place, side, read in reads:
        old = out[place, 8:ROWS_BACK, 0, :]
        out[place, 8:ROWS_BACK, 0, :] = jnp.where(lane // HALF == side, read, old)


def mix_kernel(got, intra, query, gate, base, coef, mixed_out, reads_out, squares_out):
    heads, block, _ = intra.shape
    total = None
    for h in range(heads):
        state = uncut(got[16 * h : 16 * h + 16, 0:8, 0, :])
        high, low = two(state)
        read = mm(query[h], jnp.concatenate([high, low], axis=1))
        mixed = intra[h] + (read[:, :HD] + read[:, HD:]) * gate[:, h : h + 1]
        mixed_out[h] = mixed
        total = mixed * mixed if total is None else total + mixed * mixed
    ones = jnp.ones((8, HD), bf16)
    high, low = two(total)
    squares_out[:, 0, :block] = mm(ones, high, NT) + mm(ones, low, NT)

    rows_n = base.shape[0] // heads
    squares = [None] * rows_n
    for h in range(heads):
        first, second = None, None
        for d in range(8):
            a = got[16 * h + 2 * d, 8:16, 0, :]
            b = got[16 * h + 2 * d + 1, 8:16, 0, :]
            first = a if first is None else first + a
            second = b if second is None else second + b
        for r, handed in enumerate(swap_halves(first, second)):
            n = r * heads + h
            read = base[n] + coef[n] * handed
            reads_out[n] = read
            squares[r] = read * read if squares[r] is None else squares[r] + read * read
    high, low = two(jnp.concatenate(squares, axis=0))
    sums = mm(ones, high, NT) + mm(ones, low, NT)
    squares_out[:, 0, block:] = jnp.concatenate(
        [sums, jnp.zeros((8, HD - sums.shape[1]), f32)], axis=1
    )


def norm_kernel(count, got, mixed, reads, prefill_out, decode_out):
    heads, block, _ = mixed.shape
    parts = jnp.concatenate(three(got[:, 0, :]), axis=0)
    ones = jnp.ones((parts.shape[0], HD), bf16)
    total = mm(parts, ones, TN)
    scale = lax.rsqrt(total / count + eps)
    scaled = jnp.stack([mixed[h] * scale[:block] for h in range(heads)], axis=0)
    prefill_out[...] = jnp.swapaxes(scaled, 0, 1).astype(bf16)
    steps, rows_n = decode_out.shape[0], decode_out.shape[1]
    pieces = []
    for r in range(rows_n):
        low = block + r * steps
        for h in range(heads):
            pieces.append(reads[r * heads + h] * scale[low : low + steps])
    scaled = jnp.swapaxes(jnp.stack(pieces, axis=0), 0, 1)
    decode_out[...] = scaled.reshape(decode_out.shape).astype(bf16)


def call(kernel, name, outs, scalars, arrays, scratch=(), cost=0, space=pltpu.VMEM):
    scalars = [pltpu.with_memory_space_constraint(x, pltpu.HBM) for x in scalars]
    if space is pltpu.HBM:
        arrays = [pltpu.with_memory_space_constraint(x, space) for x in arrays]
    shapes = [jax.ShapeDtypeStruct(shape, dtype) for shape, dtype in outs]
    specs = [pl.BlockSpec(memory_space=pltpu.SMEM)] * len(scalars)
    specs += [pl.BlockSpec(memory_space=space)] * len(arrays)
    return pl.pallas_call(
        kernel,
        name=name,
        out_shape=shapes,
        in_specs=specs,
        out_specs=[
            pl.BlockSpec(memory_space=pltpu.SMEM if dtype == jnp.int32 else pltpu.VMEM)
            for _, dtype in outs
        ],
        scratch_shapes=list(scratch),
        compiler_params=pltpu.CompilerParams(vmem_limit_bytes=24 * 2**20),
        cost_estimate=pl.CostEstimate(flops=cost, bytes_accessed=4 * 2**20, transcendentals=0),
    )(*scalars, *arrays)


def body(
    prefill_query,
    prefill_key,
    prefill_value,
    log_decay,
    lengths,
    owner,
    decode_state,
    step_query,
    step_key,
    step_value,
    step_decay,
    soft_query,
    cache_keys,
    cache_values,
    new_keys,
    new_values,
    row_lengths,
):
    block, heads, _ = prefill_query.shape
    steps, rows_n = step_query.shape[0], step_query.shape[1]
    blocks = lax.axis_size("ctx")
    planes = lax.axis_size("head")
    pairs = rows_n * heads
    decay_rows = jnp.swapaxes(log_decay, 0, 1)
    outgoing, second, shared = call(
        summary_kernel,
        "summary",
        [
            ((blocks, ROWS_OUT, 1, HD), f32),
            ((blocks, 8, HD), f32),
            ((1,), jnp.int32),
        ],
        [lengths],
        [decay_rows, prefill_key, prefill_value, step_query],
        scratch=[
            pltpu.VMEM(prefill_key.shape, bf16),
            pltpu.VMEM(prefill_value.shape, bf16),
            pltpu.VMEM(decay_rows.shape, f32),
            pltpu.VMEM(step_query.shape, bf16),
            pltpu.SemaphoreType.DMA((10,)),
        ],
        space=pltpu.HBM,
    )
    gathered = lax.all_to_all(outgoing, "ctx", 0, 0, tiled=True)
    second = lax.cond(
        shared[0] > 0,
        lambda x: lax.all_to_all(x, "ctx", 0, 0, tiled=True),
        lambda x: x,
        second,
    )
    local_inputs = [
        decay_rows,
        prefill_query,
        prefill_key,
        prefill_value,
        decode_state,
        step_query,
        step_key,
        step_value,
        jnp.transpose(step_decay, (1, 2, 0)),
        soft_query,
        cache_keys.reshape(rows_n, -1, HD),
        cache_values.reshape(rows_n, -1, HD),
        new_keys.reshape(steps, rows_n, HD),
        new_values.reshape(steps, rows_n, HD),
    ]
    intra, queries, gate, base, coef, soft_out = call(
        local_kernel,
        "local",
        [
            ((heads, block, HD), f32),
            ((heads, block, HD), bf16),
            ((block, 8), f32),
            ((pairs, steps, HD), f32),
            ((pairs, steps, HD), f32),
            (soft_query.shape, bf16),
        ],
        [lengths, owner, row_lengths],
        local_inputs,
        scratch=[pltpu.VMEM(x.shape, x.dtype) for x in local_inputs]
        + [pltpu.SemaphoreType.DMA((len(local_inputs),))],
        cost=2 * 10**9,
        space=pltpu.HBM,
    )
    returning = call(
        functools.partial(scan_kernel, block),
        "scan",
        [((blocks, ROWS_BACK, 1, HD), f32)],
        [lengths, owner],
        [gathered, second],
        scratch=[pltpu.VMEM((blocks + 8, 8, HD), f32)],
    )[0]
    returned = lax.all_to_all(returning, "ctx", 0, 0, tiled=True)
    mixed, reads, squares = call(
        mix_kernel,
        "mix",
        [
            ((heads, block, HD), f32),
            ((pairs, steps, HD), f32),
            ((planes, 1, block + HD), f32),
        ],
        [],
        [returned, intra, queries, gate, base, coef],
    )
    squares = lax.all_to_all(squares, "head", 0, 0, tiled=True)
    prefill_out, decode_out = call(
        functools.partial(norm_kernel, float(planes * heads * HD)),
        "norm",
        [(prefill_query.shape, bf16), (step_query.shape, bf16)],
        [],
        [squares, mixed, reads],
    )
    return (prefill_out, decode_out, soft_out)


def solution(mesh):
    placed = (
        P("ctx", "head", None),
        P("ctx", "head", None),
        P("ctx", "head", None),
        P("ctx", "head"),
        P(),
        P(),
        P("ctx", "head", None, None),
        P(None, "ctx", "head", None),
        P(None, "ctx", "head", None),
        P(None, "ctx", "head", None),
        P(None, "ctx", "head"),
        P(None, "ctx", "head", None),
        P("ctx", None, "head", None),
        P("ctx", None, "head", None),
        P(None, "ctx", "head", None),
        P(None, "ctx", "head", None),
        P("ctx"),
    )
    return jax.shard_map(
        body,
        mesh=mesh,
        in_specs=placed,
        out_specs=(
            P("ctx", "head", None),
            P(None, "ctx", "head", None),
            P(None, "ctx", "head", None),
        ),
        check_vma=False,
    )
```

```python
import functools
import math

import jax
import jax.numpy as jnp
from jax import lax
from jax.experimental import pallas as pl
from jax.experimental.pallas import tpu as pltpu
from jax.sharding import PartitionSpec as P

f32 = jnp.float32
bf16 = jnp.bfloat16
eps = 1e-06
HD = 128
QUARTER = HD // 4
ROW_END = 8
ROW_QUERY = 16
ROW_DECAY = 20
ROWS_OUT = 21
ROWS_BACK = 12
NT = (((1,), (1,)), ((), ()))
TN = (((0,), (0,)), ((), ()))
NN = (((1,), (0,)), ((), ()))


def mm(a, b, dims=NN):
    return lax.dot_general(a, b, dims, preferred_element_type=f32)


def iota(shape, dim):
    return lax.broadcasted_iota(jnp.int32, shape, dim)


def two(x):
    high = x.astype(bf16)
    return high, (x - high.astype(f32)).astype(bf16)


def three(x):
    high = x.astype(bf16)
    rest = x - high.astype(f32)
    mid = rest.astype(bf16)
    return high, mid, (rest - mid.astype(f32)).astype(bf16)


def prompt_bounds(lengths):
    ends, total = [], jnp.int32(0)
    starts = []
    for p in range(lengths.shape[0]):
        starts.append(total)
        total = total + lengths[p]
        ends.append(total)
    return starts, ends


def segment_of(positions, ends):
    segment = jnp.zeros(positions.shape, jnp.int32)
    for end in ends:
        segment = segment + (positions >= end).astype(jnp.int32)
    return segment


def scalar_segment(position, ends):
    segment = jnp.int32(0)
    for end in ends:
        segment = segment + (position >= end).astype(jnp.int32)
    return segment


def swap(first, second, width):
    shape = first.shape
    even = ((iota((1, HD), 1) // width) % 2 == 0).reshape((1,) * (len(shape) - 1) + (HD,))
    up = pltpu.roll(second.reshape(-1, HD), width, 1).reshape(shape)
    down = pltpu.roll(first.reshape(-1, HD), HD - width, 1).reshape(shape)
    return jnp.where(even, first, up), jnp.where(even, down, second)


def turn(a, b, c, d):
    a, c = swap(a, c, 2 * QUARTER)
    b, d = swap(b, d, 2 * QUARTER)
    a, b = swap(a, b, QUARTER)
    c, d = swap(c, d, QUARTER)
    return a, b, c, d


def cut(matrix):
    split = matrix.reshape(4, 4, 8, HD)
    return jnp.stack(turn(*(split[:, k] for k in range(4))), axis=1).reshape(16, 8, HD)


def uncut(chunks):
    return cut(chunks.reshape(HD, HD)).reshape(HD, HD)


def running_sums(decay):
    heads, block = decay.shape
    upto = (iota((HD, 1), 0) <= iota((1, HD), 1)).astype(f32).astype(bf16)
    pieces = [decay[:, low : low + HD] for low in range(0, block, HD)]
    stacked = jnp.concatenate(pieces, axis=0)
    local = sum(mm(part, upto) for part in three(stacked))
    out, before = [], None
    for k in range(len(pieces)):
        piece = local[k * heads : (k + 1) * heads]
        if before is not None:
            piece = piece + before
        out.append(piece)
        before = piece[:, HD - 1 : HD]
    return jnp.concatenate(out, axis=1)


def end_slot(slot, ends, block_start, block):
    prompt, offset = jnp.int32(-1), jnp.int32(-1)
    for p in range(len(ends)):
        if p % 2 != slot:
            continue
        local = ends[p] - 1 - block_start
        inside = (local >= 0) & (local < block) & (lax.rem(ends[p], block) != 0)
        prompt = jnp.where(inside, p, prompt)
        offset = jnp.where(inside, local, offset)
    return prompt, offset


def block_shares(first, second, block):
    inside = (lax.rem(first, block) != 0) & (lax.rem(second, block) != 0)
    return inside & (first // block == second // block)


def summary_kernel(
    lengths_in,
    decay,
    key,
    value,
    step_query,
    out,
    second_out,
    shared_out,
    key_buf,
    value_buf,
    decay_buf,
    query_buf,
    lengths,
    sems,
):
    copies = [
        pltpu.make_async_copy(decay, decay_buf, sems.at[0]),
        pltpu.make_async_copy(step_query, query_buf, sems.at[1]),
    ]
    heads, block = decay_buf.shape
    quarter = block // 4
    for k in range(4):
        part = pl.ds(k * quarter, quarter)
        copies.append(pltpu.make_async_copy(key.at[part], key_buf.at[part], sems.at[2 + k]))
        copies.append(pltpu.make_async_copy(value.at[part], value_buf.at[part], sems.at[6 + k]))
    bounds = pltpu.make_async_copy(lengths_in, lengths, sems.at[10])
    bounds.start()
    for copy in copies:
        copy.start()
    block_start = lax.axis_index("ctx") * block
    bounds.wait()
    _, ends = prompt_bounds(lengths)
    shared = jnp.bool_(False)
    for other in range(0, len(ends), 2):
        shared = shared | block_shares(ends[1], ends[other], block)
    shared_out[0] = shared.astype(jnp.int32)
    place = iota((1, block), 1)
    segment = segment_of(place + block_start, ends)
    last = scalar_segment(block_start + block - 1, ends)
    prompt_a, offset_a = end_slot(0, ends, block_start, block)
    prompt_b, offset_b = end_slot(1, ends, block_start, block)
    both = (prompt_a >= 0) & (prompt_b >= 0)
    prompt_a = jnp.where(prompt_a >= 0, prompt_a, prompt_b)
    offset_a = jnp.where(offset_a >= 0, offset_a, offset_b)
    copies[0].wait()
    running = running_sums(decay_buf[...])

    def weight(prompt, offset):
        inside = segment == prompt
        at = jnp.sum(jnp.where(place == offset, running, 0.0), axis=1, keepdims=True)
        weight = jnp.where(inside, jnp.exp(jnp.where(inside, at - running, 0.0)), 0.0)
        return weight, at

    weight_last, _ = weight(last, jnp.int32(block - 1))
    weight_a, at_a = weight(prompt_a, offset_a)
    weight_b, at_b = weight(prompt_b, offset_b)
    whole = jnp.sum(jnp.where(segment == last, decay_buf[...], 0.0), axis=1, keepdims=True)
    lane, head = iota((heads, HD), 1), iota((heads, HD), 0)
    totals = jnp.where(lane == head, whole, 0.0)
    totals = jnp.where(lane == heads + head, at_a, totals)
    totals = jnp.where(lane == 2 * heads + head, at_b, totals)
    totals = jnp.sum(totals, axis=0, keepdims=True)
    out[:, ROW_DECAY, 0, :] = jnp.broadcast_to(totals, (out.shape[0], HD))

    copies[1].wait()
    steps, rows = query_buf.shape[0], query_buf.shape[1]
    pairs = rows * heads
    flat = query_buf[...].astype(f32).reshape(steps * pairs, HD).astype(bf16)
    lane = iota((1, 4 * HD), 1)
    pick = iota((HD, 1), 0) == (lane // HD) * QUARTER + lane % QUARTER
    read = mm(flat, pick.astype(f32).astype(bf16))
    spread = []
    for k in range(2):
        total = None
        for step in range(4):
            low = (4 * k + step) * pairs
            mine = (lane % HD) // QUARTER == step
            part = jnp.where(mine, read[low : low + pairs], 0.0)
            total = part if total is None else total + part
        spread.append(total)
    spread = jnp.concatenate(spread, axis=0).reshape(2 * rows, heads, 4 * HD)
    spread = jnp.swapaxes(spread, 0, 1)
    for h in range(heads):
        for d in range(4):
            piece = spread[h, :, d * HD : (d + 1) * HD]
            j = 16 * h + 4 * d
            out[j : j + 4, ROW_QUERY:ROW_DECAY, 0, :] = jnp.broadcast_to(
                piece[None], (4, 2 * rows, HD)
            )

    for copy in copies[2:]:
        copy.wait()
    keys = jnp.swapaxes(key_buf[...], 0, 1)
    values = jnp.swapaxes(value_buf[...], 0, 1)
    for h in range(heads):
        key_h = keys[h].T.astype(f32)
        left = []
        for weight_k in (weight_last, weight_a):
            left.extend(two(key_h * weight_k[h : h + 1]))
        product = mm(jnp.concatenate(left, axis=0), values[h])
        for k in range(2):
            low = 2 * k * HD
            state = product[low : low + HD] + product[low + HD : low + 2 * HD]
            out[16 * h : 16 * h + 16, 8 * k : 8 * k + 8, 0, :] = cut(state)

    @pl.when(both)
    def _():
        for h in range(heads):
            left = two(keys[h].T.astype(f32) * weight_b[h : h + 1])
            product = mm(jnp.concatenate(left, axis=0), values[h])
            second_out[16 * h : 16 * h + 16] = cut(product[:HD] + product[HD:])

    @pl.when(jnp.logical_not(both))
    def _():
        second_out[...] = jnp.zeros(second_out.shape, f32)


def local_kernel(lengths, owner, row_lengths, *refs):
    count = (len(refs) - 7) // 2
    sources, outs = refs[:count], refs[count : count + 6]
    buffers, sems = refs[count + 6 : -1], refs[-1]
    copies = [
        pltpu.make_async_copy(source, buffer, sems.at[k])
        for k, (source, buffer) in enumerate(zip(sources, buffers))
    ]
    for copy in copies:
        copy.start()
    for copy in copies:
        copy.wait()
    (
        log_decay,
        query,
        key,
        value,
        decode_state,
        step_query,
        step_key,
        step_value,
        step_decay,
        soft_query,
        cache_keys,
        cache_values,
        new_keys,
        new_values,
    ) = buffers
    intra_out, query_out, gate_out, base_out, coef_out, soft_out = outs
    block, heads, _ = query.shape
    device = lax.axis_index("ctx")
    block_start = device * block
    _, ends = prompt_bounds(lengths)
    running = running_sums(log_decay[...])
    columns = jnp.concatenate([running, running], axis=0).T
    place_row = iota((1, block), 1) + block_start
    place_col = iota((block, 1), 0) + block_start
    segment_row = segment_of(place_row, ends)
    segment_col = segment_of(place_col, ends)
    before = jnp.where(block_start > 0, scalar_segment(block_start - 1, ends), -1)
    gate_out[...] = jnp.where(segment_col == before, jnp.exp(columns), 0.0)

    queries = jnp.swapaxes(query[...], 0, 1)
    keys = jnp.swapaxes(key[...], 0, 1)
    values = jnp.swapaxes(value[...], 0, 1)
    query_out[...] = queries
    half = block // 2
    tiles = ((0, 0), (1, 0), (1, 1))
    masks = {}
    for a, b in tiles:
        rows = slice(a * half, (a + 1) * half)
        cols = slice(b * half, (b + 1) * half)
        seen = segment_col[rows] == segment_row[:, cols]
        if a == b:
            seen = seen & (place_col[rows] >= place_row[:, cols])
        masks[a, b] = jnp.where(seen, 0.0, -1e30)
    for h in range(heads):
        mixed = [None, None]
        for a, b in tiles:
            rows = slice(a * half, (a + 1) * half)
            cols = slice(b * half, (b + 1) * half)
            scores = mm(queries[h][rows], keys[h][cols], NT)
            gap = columns[rows, h : h + 1] - running[h : h + 1, cols]
            weights = (scores * jnp.exp(gap + masks[a, b])).astype(bf16)
            term = mm(weights, values[h][cols])
            mixed[a] = term if mixed[a] is None else mixed[a] + term
        intra_out[h, :half, :] = mixed[0]
        intra_out[h, half:, :] = mixed[1]

    steps, rows_n = step_query.shape[0], step_query.shape[1]

    def by_head(ref):
        whole = ref[...].astype(f32).reshape(steps, rows_n * heads, HD)
        return jnp.swapaxes(whole, 0, 1)

    sq, sk, sv = by_head(step_query), by_head(step_key), by_head(step_value)
    decays = step_decay[...].reshape(rows_n * heads, steps)
    upto = (iota((steps, steps), 0) <= iota((steps, steps), 1)).astype(f32)
    cum_row = lax.dot_general(
        decays, upto, NN, precision=lax.Precision.HIGHEST, preferred_element_type=f32
    )
    cum_col = cum_row.T
    causal = iota((steps, steps), 0) >= iota((steps, steps), 1)
    for r in range(rows_n):
        owned = jnp.int32(0)
        for p in range(len(ends)):
            owned = owned + (owner[p] == device * rows_n + r).astype(jnp.int32)
        owned = jnp.where(owned > 0, 1.0, 0.0)
        for h in range(heads):
            n = r * heads + h
            cum = cum_col[:, n : n + 1]
            gap = jnp.where(causal, cum - cum_row[n : n + 1, :], 0.0)
            inner = mm(sq[n].astype(bf16), sk[n].astype(bf16), NT)
            inner = jnp.where(causal, inner * jnp.exp(gap), 0.0)
            fresh = lax.dot_general(
                inner, sv[n], NN, precision=lax.Precision.HIGHEST, preferred_element_type=f32
            )
            high, low = two(decode_state[r, h])
            read = mm(sq[n].astype(bf16), jnp.concatenate([high, low], axis=1))
            grown = jnp.exp(cum)
            read = (read[:, :HD] + read[:, HD:]) * grown
            base_out[n] = fresh + jnp.where(owned > 0.5, 0.0, read)
            coef_out[n] = jnp.broadcast_to(grown * owned, (steps, HD))

    fresh_keys = jnp.swapaxes(new_keys[...].astype(f32), 0, 1)
    fresh_values = jnp.swapaxes(new_values[...].astype(f32), 0, 1)
    group = soft_query.shape[2]
    cache = cache_keys.shape[1]
    scale = 1.0 / math.sqrt(HD)
    whole = soft_query[...].astype(f32)
    for r in range(rows_n):
        rows_q = whole[:, r].reshape(steps * group, HD).astype(bf16)
        cached = mm(rows_q, cache_keys[r], NT) * scale
        recent = mm(rows_q, fresh_keys[r].astype(bf16), NT) * scale
        slot = iota((steps * group, cache), 1)
        cached = jnp.where(slot < row_lengths[r], cached, -jnp.inf)
        step_of = iota((steps * group, steps), 0) // group
        recent = jnp.where(iota((steps * group, steps), 1) <= step_of, recent, -jnp.inf)
        top = jnp.maximum(
            jnp.max(cached, axis=1, keepdims=True), jnp.max(recent, axis=1, keepdims=True)
        )
        cached = jnp.exp(cached - top)
        recent = jnp.exp(recent - top)
        total = jnp.sum(cached, axis=1, keepdims=True) + jnp.sum(recent, axis=1, keepdims=True)
        cached = (cached / total).astype(bf16)
        recent = (recent / total).astype(bf16)
        mixed = mm(cached, cache_values[r]) + mm(recent, fresh_values[r].astype(bf16))
        soft_out[:, r, :, :] = mixed.reshape(steps, group, HD).astype(bf16)


def scan_kernel(
    block, lengths_in, owner_in, got, second, out, carried, lengths, owner, sems
):
    copies = [
        pltpu.make_async_copy(lengths_in, lengths, sems.at[0]),
        pltpu.make_async_copy(owner_in, owner, sems.at[1]),
    ]
    for copy in copies:
        copy.start()
    blocks = got.shape[0]
    device = lax.axis_index("ctx")
    head = device // 16
    padded = carried.shape[0]
    heads = blocks // 16

    decays = got[:, ROW_DECAY, 0, :]
    decay = jnp.sum(
        jnp.where(iota((blocks, HD), 1) == head, decays, 0.0), axis=1, keepdims=True
    )
    k_at, b_at = iota((blocks, blocks), 0), iota((blocks, blocks), 1)
    later = jnp.concatenate(
        [jnp.where(k_at > b_at, part.astype(f32), 0.0).astype(bf16) for part in three(decay)],
        axis=0,
    )
    earlier = iota((padded, 3 * blocks), 1) % blocks < iota((padded, 3 * blocks), 0)
    gap = mm(earlier.astype(f32).astype(bf16), later)
    right = []
    for i in range(8):
        high, low = two(got[:, i, 0, :])
        right.append(jnp.concatenate([high, low, high], axis=0))
    right = jnp.concatenate(right, axis=1)

    for copy in copies:
        copy.wait()
    starts, ends = prompt_bounds(lengths)
    to, frm = iota((padded, blocks), 0), iota((padded, blocks), 1)
    linked = frm < to
    for start in starts:
        restart = start // block
        linked = linked & ~((restart > frm) & (restart < to))
    weight = jnp.where(linked, jnp.exp(jnp.where(linked, gap, 0.0)), 0.0)
    high, low = two(weight)
    weights = jnp.concatenate([high, high, low], axis=1)
    product = mm(weights, right)
    for i in range(8):
        state = product[:, i * HD : (i + 1) * HD]
        carried[:, i, :] = state
        out[:, i, 0, :] = state[:blocks]
        if i < ROWS_BACK - 8:
            out[:, 8 + i, 0, :] = jnp.zeros((blocks, HD), f32)

    rows_n = (ROW_DECAY - ROW_QUERY) // 2
    steps = 8
    lane, step_at = iota((steps, HD), 1), iota((steps, HD), 0)
    mine = lane // QUARTER == step_at % 4
    reads = []
    for p in range(len(ends)):
        index = ends[p] // block
        source = jnp.minimum(index, blocks - 1)
        partial = lax.rem(ends[p], block) != 0
        leads = (starts[p] < index * block).astype(f32)
        if p % 2:
            shared = jnp.bool_(False)
            for other in range(0, len(ends), 2):
                shared = shared | block_shares(ends[p], ends[other], block)
        else:
            shared = jnp.bool_(False)
        run = got[source, ROW_DECAY, :, :]
        at = jnp.where(shared, 2 * heads, heads) + head
        run = jnp.sum(jnp.where(iota((1, HD), 1) == at, run, 0.0), axis=1, keepdims=True)
        lead = leads * jnp.exp(jnp.where(partial, run, 0.0))
        rest = got[source, ROW_END : ROW_END + 8, 0, :]
        if p % 2:
            rest = jnp.where(shared, second[source], rest)
        handed = carried[index] * lead + jnp.where(partial, rest, 0.0)
        handed = [handed[:, g * QUARTER : (g + 1) * QUARTER] for g in range(4)]
        high, low = two(jnp.concatenate(handed, axis=0))
        both = jnp.concatenate([jnp.concatenate([high, low], axis=1)] * 4, axis=0)
        place = owner[p] // rows_n
        side = lax.rem(owner[p], rows_n)
        query = jnp.where(
            step_at < 4,
            got[place, ROW_QUERY + side, :, :],
            got[place, ROW_QUERY + rows_n + side, :, :],
        )
        read = mm(jnp.where(mine, query, 0.0).astype(bf16), both)
        read = read[:, :QUARTER] + read[:, QUARTER:]
        reads.append((place, side, jnp.concatenate([read[:4], read[4:]] * 2, axis=1)))
    for place, side, read in reads:
        old = out[place, 8:ROWS_BACK, 0, :]
        kept = lane[:4] // (2 * QUARTER) == side
        out[place, 8:ROWS_BACK, 0, :] = jnp.where(kept, read, old)


def mix_kernel(got, intra, query, gate, base, coef, mixed_out, reads_out, squares_out):
    heads, block, _ = intra.shape
    total = None
    for h in range(heads):
        state = uncut(got[16 * h : 16 * h + 16, 0:8, 0, :])
        high, low = two(state)
        read = mm(query[h], jnp.concatenate([high, low], axis=1))
        mixed = intra[h] + (read[:, :HD] + read[:, HD:]) * gate[:, h : h + 1]
        mixed_out[h] = mixed
        total = mixed * mixed if total is None else total + mixed * mixed
    ones = jnp.ones((8, HD), bf16)
    high, low = two(total)
    planes = squares_out.shape[0]
    squares_out[:, 0, :block] = (mm(ones, high, NT) + mm(ones, low, NT))[:planes]

    rows_n = base.shape[0] // heads
    squares = [None] * rows_n
    for h in range(heads):
        pieces = []
        for e in range(4):
            total = got[16 * h + e, 8:ROWS_BACK, 0, :]
            for d in range(1, 4):
                total = total + got[16 * h + 4 * d + e, 8:ROWS_BACK, 0, :]
            pieces.append(total)
        pieces = turn(*pieces)
        for r in range(rows_n):
            handed = jnp.concatenate(pieces[2 * r : 2 * r + 2], axis=0)
            n = r * heads + h
            read = base[n] + coef[n] * handed
            reads_out[n] = read
            squares[r] = read * read if squares[r] is None else squares[r] + read * read
    high, low = two(jnp.concatenate(squares, axis=0))
    sums = mm(ones, high, NT) + mm(ones, low, NT)
    sums = jnp.concatenate([sums, jnp.zeros((8, HD - sums.shape[1]), f32)], axis=1)
    squares_out[:, 0, block:] = sums[:planes]


def norm_kernel(count, got, mixed, reads, prefill_out, decode_out):
    heads, block, _ = mixed.shape
    parts = jnp.concatenate(three(got[:, 0, :]), axis=0)
    ones = jnp.ones((parts.shape[0], HD), bf16)
    total = mm(parts, ones, TN)
    scale = lax.rsqrt(total / count + eps)
    scaled = jnp.stack([mixed[h] * scale[:block] for h in range(heads)], axis=0)
    prefill_out[...] = jnp.swapaxes(scaled, 0, 1).astype(bf16)
    steps, rows_n = decode_out.shape[0], decode_out.shape[1]
    pieces = []
    for r in range(rows_n):
        low = block + r * steps
        for h in range(heads):
            pieces.append(reads[r * heads + h] * scale[low : low + steps])
    scaled = jnp.swapaxes(jnp.stack(pieces, axis=0), 0, 1)
    decode_out[...] = scaled.reshape(decode_out.shape).astype(bf16)


def call(
    kernel,
    name,
    outs,
    scalars,
    arrays,
    scratch=(),
    cost=0,
    space=pltpu.VMEM,
    scalar_space=pltpu.HBM,
):
    scalars = [pltpu.with_memory_space_constraint(x, pltpu.HBM) for x in scalars]
    if space is pltpu.HBM:
        arrays = [pltpu.with_memory_space_constraint(x, space) for x in arrays]
    shapes = [jax.ShapeDtypeStruct(shape, dtype) for shape, dtype in outs]
    specs = [pl.BlockSpec(memory_space=scalar_space)] * len(scalars)
    specs += [pl.BlockSpec(memory_space=space)] * len(arrays)
    return pl.pallas_call(
        kernel,
        name=name,
        out_shape=shapes,
        in_specs=specs,
        out_specs=[
            pl.BlockSpec(memory_space=pltpu.SMEM if dtype == jnp.int32 else pltpu.VMEM)
            for _, dtype in outs
        ],
        scratch_shapes=list(scratch),
        compiler_params=pltpu.CompilerParams(vmem_limit_bytes=24 * 2**20),
        cost_estimate=pl.CostEstimate(flops=cost, bytes_accessed=4 * 2**20, transcendentals=0),
    )(*scalars, *arrays)


def body(
    prefill_query,
    prefill_key,
    prefill_value,
    log_decay,
    lengths,
    owner,
    decode_state,
    step_query,
    step_key,
    step_value,
    step_decay,
    soft_query,
    cache_keys,
    cache_values,
    new_keys,
    new_values,
    row_lengths,
):
    block, heads, _ = prefill_query.shape
    steps, rows_n = step_query.shape[0], step_query.shape[1]
    blocks = lax.axis_size("ctx")
    planes = lax.axis_size("head")
    pairs = rows_n * heads
    decay_rows = jnp.swapaxes(log_decay, 0, 1)
    outgoing, second, shared = call(
        summary_kernel,
        "summary",
        [
            ((blocks, ROWS_OUT, 1, HD), f32),
            ((blocks, 8, HD), f32),
            ((1,), jnp.int32),
        ],
        [lengths],
        [decay_rows, prefill_key, prefill_value, step_query],
        scratch=[
            pltpu.VMEM(prefill_key.shape, bf16),
            pltpu.VMEM(prefill_value.shape, bf16),
            pltpu.VMEM(decay_rows.shape, f32),
            pltpu.VMEM(step_query.shape, bf16),
            pltpu.SMEM(lengths.shape, jnp.int32),
            pltpu.SemaphoreType.DMA((11,)),
        ],
        space=pltpu.HBM,
    )
    gathered = lax.all_to_all(outgoing, "ctx", 0, 0, tiled=True)
    second = lax.cond(
        shared[0] > 0,
        lambda x: lax.all_to_all(x, "ctx", 0, 0, tiled=True),
        lambda x: x,
        second,
    )
    local_inputs = [
        decay_rows,
        prefill_query,
        prefill_key,
        prefill_value,
        decode_state,
        step_query,
        step_key,
        step_value,
        jnp.transpose(step_decay, (1, 2, 0)),
        soft_query,
        cache_keys.reshape(rows_n, -1, HD),
        cache_values.reshape(rows_n, -1, HD),
        new_keys.reshape(steps, rows_n, HD),
        new_values.reshape(steps, rows_n, HD),
    ]
    intra, queries, gate, base, coef, soft_out = call(
        local_kernel,
        "local",
        [
            ((heads, block, HD), f32),
            ((heads, block, HD), bf16),
            ((block, 8), f32),
            ((pairs, steps, HD), f32),
            ((pairs, steps, HD), f32),
            (soft_query.shape, bf16),
        ],
        [lengths, owner, row_lengths],
        local_inputs,
        scratch=[pltpu.VMEM(x.shape, x.dtype) for x in local_inputs]
        + [pltpu.SemaphoreType.DMA((len(local_inputs),))],
        cost=2 * 10**9,
        space=pltpu.HBM,
        scalar_space=pltpu.SMEM,
    )
    gathered, intra = lax.optimization_barrier((gathered, intra))
    returning = call(
        functools.partial(scan_kernel, block),
        "scan",
        [((blocks, ROWS_BACK, 1, HD), f32)],
        [lengths, owner],
        [gathered, second],
        scratch=[
            pltpu.VMEM((blocks + 8, 8, HD), f32),
            pltpu.SMEM(lengths.shape, jnp.int32),
            pltpu.SMEM(owner.shape, jnp.int32),
            pltpu.SemaphoreType.DMA((2,)),
        ],
    )[0]
    returned = lax.all_to_all(returning, "ctx", 0, 0, tiled=True)
    mixed, reads, squares = call(
        mix_kernel,
        "mix",
        [
            ((heads, block, HD), f32),
            ((pairs, steps, HD), f32),
            ((planes, 1, block + HD), f32),
        ],
        [],
        [returned, intra, queries, gate, base, coef],
    )
    squares = lax.all_to_all(squares, "head", 0, 0, tiled=True)
    prefill_out, decode_out = call(
        functools.partial(norm_kernel, float(planes * heads * HD)),
        "norm",
        [(prefill_query.shape, bf16), (step_query.shape, bf16)],
        [],
        [squares, mixed, reads],
    )
    return (prefill_out, decode_out, soft_out)


def solution(mesh):
    placed = (
        P("ctx", "head", None),
        P("ctx", "head", None),
        P("ctx", "head", None),
        P("ctx", "head"),
        P(),
        P(),
        P("ctx", "head", None, None),
        P(None, "ctx", "head", None),
        P(None, "ctx", "head", None),
        P(None, "ctx", "head", None),
        P(None, "ctx", "head"),
        P(None, "ctx", "head", None),
        P("ctx", None, "head", None),
        P("ctx", None, "head", None),
        P(None, "ctx", "head", None),
        P(None, "ctx", "head", None),
        P("ctx"),
    )
    return jax.shard_map(
        body,
        mesh=mesh,
        in_specs=placed,
        out_specs=(
            P("ctx", "head", None),
            P(None, "ctx", "head", None),
            P(None, "ctx", "head", None),
        ),
        check_vma=False,
    )
```

```python
import functools
import math

import jax
import jax.numpy as jnp
from jax import lax
from jax.experimental import pallas as pl
from jax.experimental.pallas import tpu as pltpu
from jax.sharding import PartitionSpec as P

f32 = jnp.float32
bf16 = jnp.bfloat16
eps = 1e-06
HD = 128
QUARTER = HD // 4
ROW_END = 8
ROW_QUERY = 16
ROW_DECAY = 18
ROWS_OUT = 19
ROWS_BACK = 10
ROWS_SECOND = 10
NT = (((1,), (1,)), ((), ()))
TN = (((0,), (0,)), ((), ()))
NN = (((1,), (0,)), ((), ()))


def mm(a, b, dims=NN):
    return lax.dot_general(a, b, dims, preferred_element_type=f32)


def iota(shape, dim):
    return lax.broadcasted_iota(jnp.int32, shape, dim)


def two(x):
    high = x.astype(bf16)
    return high, (x - high.astype(f32)).astype(bf16)


def three(x):
    high = x.astype(bf16)
    rest = x - high.astype(f32)
    mid = rest.astype(bf16)
    return high, mid, (rest - mid.astype(f32)).astype(bf16)


def prompt_bounds(lengths):
    ends, total = [], jnp.int32(0)
    starts = []
    for p in range(lengths.shape[0]):
        starts.append(total)
        total = total + lengths[p]
        ends.append(total)
    return starts, ends


def segment_of(positions, ends):
    segment = jnp.zeros(positions.shape, jnp.int32)
    for end in ends:
        segment = segment + (positions >= end).astype(jnp.int32)
    return segment


def scalar_segment(position, ends):
    segment = jnp.int32(0)
    for end in ends:
        segment = segment + (position >= end).astype(jnp.int32)
    return segment


def swap(first, second, width):
    shape = first.shape
    even = ((iota((1, HD), 1) // width) % 2 == 0).reshape((1,) * (len(shape) - 1) + (HD,))
    up = pltpu.roll(second.reshape(-1, HD), width, 1).reshape(shape)
    down = pltpu.roll(first.reshape(-1, HD), HD - width, 1).reshape(shape)
    return jnp.where(even, first, up), jnp.where(even, down, second)


def turn(a, b, c, d):
    a, c = swap(a, c, 2 * QUARTER)
    b, d = swap(b, d, 2 * QUARTER)
    a, b = swap(a, b, QUARTER)
    c, d = swap(c, d, QUARTER)
    return a, b, c, d


def cut(matrix):
    split = matrix.reshape(4, 4, 8, HD)
    return jnp.stack(turn(*(split[:, k] for k in range(4))), axis=1).reshape(16, 8, HD)


def uncut(chunks):
    return cut(chunks.reshape(HD, HD)).reshape(HD, HD)


def running_sums(decay):
    heads, block = decay.shape
    upto = (iota((HD, 1), 0) <= iota((1, HD), 1)).astype(f32).astype(bf16)
    pieces = [decay[:, low : low + HD] for low in range(0, block, HD)]
    stacked = jnp.concatenate(pieces, axis=0)
    local = sum(mm(part, upto) for part in three(stacked))
    out, before = [], None
    for k in range(len(pieces)):
        piece = local[k * heads : (k + 1) * heads]
        if before is not None:
            piece = piece + before
        out.append(piece)
        before = piece[:, HD - 1 : HD]
    return jnp.concatenate(out, axis=1)


def end_slot(slot, ends, block_start, block):
    prompt, offset = jnp.int32(-1), jnp.int32(-1)
    for p in range(len(ends)):
        if p % 2 != slot:
            continue
        local = ends[p] - 1 - block_start
        inside = (local >= 0) & (local < block) & (lax.rem(ends[p], block) != 0)
        prompt = jnp.where(inside, p, prompt)
        offset = jnp.where(inside, local, offset)
    return prompt, offset


def row_taken(owner, row):
    taken = jnp.bool_(False)
    for p in range(owner.shape[0]):
        taken = taken | (owner[p] == row)
    return taken


def block_shares(first, second, block):
    inside = (lax.rem(first, block) != 0) & (lax.rem(second, block) != 0)
    return inside & (first // block == second // block)


def summary_kernel(
    lengths_in,
    owner_in,
    decay,
    key,
    value,
    step_query,
    out,
    second_out,
    shared_out,
    key_buf,
    value_buf,
    decay_buf,
    query_buf,
    lengths,
    owner,
    sems,
):
    copies = [
        pltpu.make_async_copy(decay, decay_buf, sems.at[0]),
        pltpu.make_async_copy(step_query, query_buf, sems.at[1]),
    ]
    heads, block = decay_buf.shape
    quarter = block // 4
    for k in range(4):
        part = pl.ds(k * quarter, quarter)
        copies.append(pltpu.make_async_copy(key.at[part], key_buf.at[part], sems.at[2 + k]))
        copies.append(pltpu.make_async_copy(value.at[part], value_buf.at[part], sems.at[6 + k]))
    scalars = [
        pltpu.make_async_copy(lengths_in, lengths, sems.at[10]),
        pltpu.make_async_copy(owner_in, owner, sems.at[11]),
    ]
    for copy in scalars + copies:
        copy.start()
    device = lax.axis_index("ctx")
    block_start = device * block
    for copy in scalars:
        copy.wait()
    _, ends = prompt_bounds(lengths)
    shared = jnp.bool_(False)
    for other in range(0, len(ends), 2):
        shared = shared | block_shares(ends[1], ends[other], block)
    for p in range(len(ends)):
        for other in range(p):
            shared = shared | (owner[p] // 2 == owner[other] // 2)
    shared_out[0] = shared.astype(jnp.int32)
    second_row = jnp.logical_not(row_taken(owner, device * 2))
    place = iota((1, block), 1)
    segment = segment_of(place + block_start, ends)
    last = scalar_segment(block_start + block - 1, ends)
    prompt_a, offset_a = end_slot(0, ends, block_start, block)
    prompt_b, offset_b = end_slot(1, ends, block_start, block)
    both = (prompt_a >= 0) & (prompt_b >= 0)
    prompt_a = jnp.where(prompt_a >= 0, prompt_a, prompt_b)
    offset_a = jnp.where(offset_a >= 0, offset_a, offset_b)
    copies[0].wait()
    running = running_sums(decay_buf[...])

    def weight(prompt, offset):
        inside = segment == prompt
        at = jnp.sum(jnp.where(place == offset, running, 0.0), axis=1, keepdims=True)
        weight = jnp.where(inside, jnp.exp(jnp.where(inside, at - running, 0.0)), 0.0)
        return weight, at

    weight_last, _ = weight(last, jnp.int32(block - 1))
    weight_a, at_a = weight(prompt_a, offset_a)
    weight_b, at_b = weight(prompt_b, offset_b)
    whole = jnp.sum(jnp.where(segment == last, decay_buf[...], 0.0), axis=1, keepdims=True)
    lane, head = iota((heads, HD), 1), iota((heads, HD), 0)
    totals = jnp.where(lane == head, whole, 0.0)
    totals = jnp.where(lane == heads + head, at_a, totals)
    totals = jnp.where(lane == 2 * heads + head, at_b, totals)
    totals = jnp.sum(totals, axis=0, keepdims=True)
    out[:, ROW_DECAY, 0, :] = jnp.broadcast_to(totals, (out.shape[0], HD))

    copies[1].wait()
    steps, rows = query_buf.shape[0], query_buf.shape[1]
    pairs = rows * heads
    flat = query_buf[...].astype(f32).reshape(steps * pairs, HD).astype(bf16)
    lane = iota((1, 4 * HD), 1)
    pick = iota((HD, 1), 0) == (lane // HD) * QUARTER + lane % QUARTER
    read = mm(flat, pick.astype(f32).astype(bf16))
    spread = []
    for k in range(2):
        total = None
        for step in range(4):
            low = (4 * k + step) * pairs
            mine = (lane % HD) // QUARTER == step
            part = jnp.where(mine, read[low : low + pairs], 0.0)
            total = part if total is None else total + part
        spread.append(total)
    for h in range(heads):
        first = jnp.concatenate([part[h : h + 1] for part in spread], axis=0)
        other = jnp.concatenate([part[heads + h : heads + h + 1] for part in spread], axis=0)
        chosen = jnp.where(second_row, other, first)
        for d in range(4):
            j = 16 * h + 4 * d
            low = d * HD
            out[j : j + 4, ROW_QUERY:ROW_DECAY, 0, :] = jnp.broadcast_to(
                chosen[None, :, low : low + HD], (4, 2, HD)
            )
            second_out[j : j + 4, 8:ROWS_SECOND, 0, :] = jnp.broadcast_to(
                other[None, :, low : low + HD], (4, 2, HD)
            )

    for copy in copies[2:]:
        copy.wait()
    keys = jnp.swapaxes(key_buf[...], 0, 1)
    values = jnp.swapaxes(value_buf[...], 0, 1)
    for h in range(heads):
        key_h = keys[h].T.astype(f32)
        left = []
        for weight_k in (weight_last, weight_a):
            left.extend(two(key_h * weight_k[h : h + 1]))
        product = mm(jnp.concatenate(left, axis=0), values[h])
        for k in range(2):
            low = 2 * k * HD
            state = product[low : low + HD] + product[low + HD : low + 2 * HD]
            out[16 * h : 16 * h + 16, 8 * k : 8 * k + 8, 0, :] = cut(state)

    @pl.when(both)
    def _():
        for h in range(heads):
            left = two(keys[h].T.astype(f32) * weight_b[h : h + 1])
            product = mm(jnp.concatenate(left, axis=0), values[h])
            second_out[16 * h : 16 * h + 16, 0:8, 0, :] = cut(product[:HD] + product[HD:])

    @pl.when(jnp.logical_not(both))
    def _():
        second_out[:, 0:8, 0, :] = jnp.zeros((second_out.shape[0], 8, HD), f32)


def local_kernel(lengths, owner, row_lengths, *refs):
    count = (len(refs) - 7) // 2
    sources, outs = refs[:count], refs[count : count + 6]
    buffers, sems = refs[count + 6 : -1], refs[-1]
    copies = [
        pltpu.make_async_copy(source, buffer, sems.at[k])
        for k, (source, buffer) in enumerate(zip(sources, buffers))
    ]
    for copy in copies:
        copy.start()
    for copy in copies:
        copy.wait()
    (
        log_decay,
        query,
        key,
        value,
        decode_state,
        step_query,
        step_key,
        step_value,
        step_decay,
        soft_query,
        cache_keys,
        cache_values,
        new_keys,
        new_values,
    ) = buffers
    intra_out, query_out, gate_out, base_out, coef_out, soft_out = outs
    block, heads, _ = query.shape
    device = lax.axis_index("ctx")
    block_start = device * block
    _, ends = prompt_bounds(lengths)
    running = running_sums(log_decay[...])
    columns = jnp.concatenate([running, running], axis=0).T
    place_row = iota((1, block), 1) + block_start
    place_col = iota((block, 1), 0) + block_start
    segment_row = segment_of(place_row, ends)
    segment_col = segment_of(place_col, ends)
    before = jnp.where(block_start > 0, scalar_segment(block_start - 1, ends), -1)
    gate_out[...] = jnp.where(segment_col == before, jnp.exp(columns), 0.0)

    queries = jnp.swapaxes(query[...], 0, 1)
    keys = jnp.swapaxes(key[...], 0, 1)
    values = jnp.swapaxes(value[...], 0, 1)
    query_out[...] = queries
    half = block // 2
    tiles = ((0, 0), (1, 0), (1, 1))
    masks = {}
    for a, b in tiles:
        rows = slice(a * half, (a + 1) * half)
        cols = slice(b * half, (b + 1) * half)
        seen = segment_col[rows] == segment_row[:, cols]
        if a == b:
            seen = seen & (place_col[rows] >= place_row[:, cols])
        masks[a, b] = jnp.where(seen, 0.0, -1e30)
    for h in range(heads):
        mixed = [None, None]
        for a, b in tiles:
            rows = slice(a * half, (a + 1) * half)
            cols = slice(b * half, (b + 1) * half)
            scores = mm(queries[h][rows], keys[h][cols], NT)
            gap = columns[rows, h : h + 1] - running[h : h + 1, cols]
            weights = (scores * jnp.exp(gap + masks[a, b])).astype(bf16)
            term = mm(weights, values[h][cols])
            mixed[a] = term if mixed[a] is None else mixed[a] + term
        intra_out[h, :half, :] = mixed[0]
        intra_out[h, half:, :] = mixed[1]

    steps, rows_n = step_query.shape[0], step_query.shape[1]

    def by_head(ref):
        whole = ref[...].astype(f32).reshape(steps, rows_n * heads, HD)
        return jnp.swapaxes(whole, 0, 1)

    sq, sk, sv = by_head(step_query), by_head(step_key), by_head(step_value)
    decays = step_decay[...].reshape(rows_n * heads, steps)
    upto = (iota((steps, steps), 0) <= iota((steps, steps), 1)).astype(f32)
    cum_row = lax.dot_general(
        decays, upto, NN, precision=lax.Precision.HIGHEST, preferred_element_type=f32
    )
    cum_col = cum_row.T
    causal = iota((steps, steps), 0) >= iota((steps, steps), 1)
    for r in range(rows_n):
        taken = row_taken(owner, device * rows_n + r)
        owned = jnp.where(taken, 1.0, 0.0)
        late = jnp.where(taken & row_taken(owner, device * rows_n), r * 1.0, 0.0)
        for h in range(heads):
            n = r * heads + h
            cum = cum_col[:, n : n + 1]
            gap = jnp.where(causal, cum - cum_row[n : n + 1, :], 0.0)
            inner = mm(sq[n].astype(bf16), sk[n].astype(bf16), NT)
            inner = jnp.where(causal, inner * jnp.exp(gap), 0.0)
            fresh = lax.dot_general(
                inner, sv[n], NN, precision=lax.Precision.HIGHEST, preferred_element_type=f32
            )
            high, low = two(decode_state[r, h])
            read = mm(sq[n].astype(bf16), jnp.concatenate([high, low], axis=1))
            grown = jnp.exp(cum)
            read = (read[:, :HD] + read[:, HD:]) * grown
            base_out[n] = fresh + jnp.where(owned > 0.5, 0.0, read)
            coef_out[0, n] = jnp.broadcast_to(grown * (owned - late), (steps, HD))
            coef_out[1, n] = jnp.broadcast_to(grown * late, (steps, HD))

    fresh_keys = jnp.swapaxes(new_keys[...].astype(f32), 0, 1)
    fresh_values = jnp.swapaxes(new_values[...].astype(f32), 0, 1)
    group = soft_query.shape[2]
    cache = cache_keys.shape[1]
    scale = 1.0 / math.sqrt(HD)
    whole = soft_query[...].astype(f32)
    for r in range(rows_n):
        rows_q = whole[:, r].reshape(steps * group, HD).astype(bf16)
        cached = mm(rows_q, cache_keys[r], NT) * scale
        recent = mm(rows_q, fresh_keys[r].astype(bf16), NT) * scale
        slot = iota((steps * group, cache), 1)
        cached = jnp.where(slot < row_lengths[r], cached, -jnp.inf)
        step_of = iota((steps * group, steps), 0) // group
        recent = jnp.where(iota((steps * group, steps), 1) <= step_of, recent, -jnp.inf)
        top = jnp.maximum(
            jnp.max(cached, axis=1, keepdims=True), jnp.max(recent, axis=1, keepdims=True)
        )
        cached = jnp.exp(cached - top)
        recent = jnp.exp(recent - top)
        total = jnp.sum(cached, axis=1, keepdims=True) + jnp.sum(recent, axis=1, keepdims=True)
        cached = (cached / total).astype(bf16)
        recent = (recent / total).astype(bf16)
        mixed = mm(cached, cache_values[r]) + mm(recent, fresh_values[r].astype(bf16))
        soft_out[:, r, :, :] = mixed.reshape(steps, group, HD).astype(bf16)


def scan_kernel(
    block, lengths_in, owner_in, got, second, out, second_out, carried, lengths, owner, sems
):
    copies = [
        pltpu.make_async_copy(lengths_in, lengths, sems.at[0]),
        pltpu.make_async_copy(owner_in, owner, sems.at[1]),
    ]
    for copy in copies:
        copy.start()
    blocks = got.shape[0]
    device = lax.axis_index("ctx")
    head = device // 16
    padded = carried.shape[0]
    heads = blocks // 16

    decays = got[:, ROW_DECAY, 0, :]
    decay = jnp.sum(
        jnp.where(iota((blocks, HD), 1) == head, decays, 0.0), axis=1, keepdims=True
    )
    k_at, b_at = iota((blocks, blocks), 0), iota((blocks, blocks), 1)
    later = jnp.concatenate(
        [jnp.where(k_at > b_at, part.astype(f32), 0.0).astype(bf16) for part in three(decay)],
        axis=0,
    )
    earlier = iota((padded, 3 * blocks), 1) % blocks < iota((padded, 3 * blocks), 0)
    gap = mm(earlier.astype(f32).astype(bf16), later)
    right = []
    for i in range(8):
        high, low = two(got[:, i, 0, :])
        right.append(jnp.concatenate([high, low, high], axis=0))
    right = jnp.concatenate(right, axis=1)

    for copy in copies:
        copy.wait()
    starts, ends = prompt_bounds(lengths)
    to, frm = iota((padded, blocks), 0), iota((padded, blocks), 1)
    linked = frm < to
    for start in starts:
        restart = start // block
        linked = linked & ~((restart > frm) & (restart < to))
    weight = jnp.where(linked, jnp.exp(jnp.where(linked, gap, 0.0)), 0.0)
    high, low = two(weight)
    weights = jnp.concatenate([high, high, low], axis=1)
    product = mm(weights, right)
    for i in range(8):
        state = product[:, i * HD : (i + 1) * HD]
        carried[:, i, :] = state
        out[:, i, 0, :] = state[:blocks]
        if i < ROWS_BACK - 8:
            out[:, 8 + i, 0, :] = jnp.zeros((blocks, HD), f32)

    second_out[...] = jnp.zeros(second_out.shape, f32)
    mine = iota((HD, 1), 0) // QUARTER == iota((1, HD), 1) // QUARTER
    reads = []
    for p in range(len(ends)):
        index = ends[p] // block
        source = jnp.minimum(index, blocks - 1)
        partial = lax.rem(ends[p], block) != 0
        leads = (starts[p] < index * block).astype(f32)
        if p % 2:
            shared = jnp.bool_(False)
            for other in range(0, len(ends), 2):
                shared = shared | block_shares(ends[p], ends[other], block)
        else:
            shared = jnp.bool_(False)
        run = got[source, ROW_DECAY, :, :]
        at = jnp.where(shared, 2 * heads, heads) + head
        run = jnp.sum(jnp.where(iota((1, HD), 1) == at, run, 0.0), axis=1, keepdims=True)
        lead = leads * jnp.exp(jnp.where(partial, run, 0.0))
        rest = got[source, ROW_END : ROW_END + 8, 0, :]
        if p % 2:
            rest = jnp.where(shared, second[source, 0:8, 0, :], rest)
        handed = carried[index] * lead + jnp.where(partial, rest, 0.0)
        rows = []
        for g in range(4):
            rows.append(jnp.concatenate([handed[:, g * QUARTER : (g + 1) * QUARTER]] * 4, axis=1))
        rows = jnp.where(mine, jnp.concatenate(rows * 4, axis=0), 0.0)
        place = owner[p] // 2
        late = (lax.rem(owner[p], 2) == 1) & row_taken(owner, owner[p] - 1)
        query = jnp.where(
            late, second[place, 8:ROWS_SECOND, 0, :], got[place, ROW_QUERY:ROW_DECAY, 0, :]
        )
        read = mm(query.astype(bf16), jnp.concatenate(two(rows), axis=1))
        reads.append((place, late, read[:, :HD] + read[:, HD:]))
    for place, late, read in reads:

        @pl.when(late)
        def _():
            second_out[place, :, 0, :] = read

        @pl.when(jnp.logical_not(late))
        def _():
            out[place, 8:ROWS_BACK, 0, :] = read


def mix_kernel(got, second, intra, query, gate, base, coef, mixed_out, reads_out, squares_out):
    heads, block, _ = intra.shape
    total = None
    for h in range(heads):
        state = uncut(got[16 * h : 16 * h + 16, 0:8, 0, :])
        high, low = two(state)
        read = mm(query[h], jnp.concatenate([high, low], axis=1))
        mixed = intra[h] + (read[:, :HD] + read[:, HD:]) * gate[:, h : h + 1]
        mixed_out[h] = mixed
        total = mixed * mixed if total is None else total + mixed * mixed
    ones = jnp.ones((8, HD), bf16)
    high, low = two(total)
    planes = squares_out.shape[0]
    squares_out[:, 0, :block] = (mm(ones, high, NT) + mm(ones, low, NT))[:planes]

    def handed_reads(ref, low):
        pieces = []
        for e in range(4):
            parts = []
            for h in range(heads):
                total = ref[16 * h + e, low : low + 2, 0, :]
                for d in range(1, 4):
                    total = total + ref[16 * h + 4 * d + e, low : low + 2, 0, :]
                parts.append(total)
            pieces.append(jnp.concatenate(parts, axis=0))
        whole = jnp.swapaxes(jnp.stack(turn(*pieces), axis=0), 0, 1)
        return whole.reshape(heads, 8, HD)

    first, late = handed_reads(got, 8), handed_reads(second, 0)
    rows_n = base.shape[0] // heads
    squares = [None] * rows_n
    for h in range(heads):
        for r in range(rows_n):
            n = r * heads + h
            read = base[n] + coef[0, n] * first[h] + coef[1, n] * late[h]
            reads_out[n] = read
            squares[r] = read * read if squares[r] is None else squares[r] + read * read
    high, low = two(jnp.concatenate(squares, axis=0))
    sums = mm(ones, high, NT) + mm(ones, low, NT)
    sums = jnp.concatenate([sums, jnp.zeros((8, HD - sums.shape[1]), f32)], axis=1)
    squares_out[:, 0, block:] = sums[:planes]


def norm_kernel(count, got, mixed, reads, prefill_out, decode_out):
    heads, block, _ = mixed.shape
    parts = jnp.concatenate(three(got[:, 0, :]), axis=0)
    ones = jnp.ones((parts.shape[0], HD), bf16)
    total = mm(parts, ones, TN)
    scale = lax.rsqrt(total / count + eps)
    scaled = jnp.stack([mixed[h] * scale[:block] for h in range(heads)], axis=0)
    prefill_out[...] = jnp.swapaxes(scaled, 0, 1).astype(bf16)
    steps, rows_n = decode_out.shape[0], decode_out.shape[1]
    pieces = []
    for r in range(rows_n):
        low = block + r * steps
        for h in range(heads):
            pieces.append(reads[r * heads + h] * scale[low : low + steps])
    scaled = jnp.swapaxes(jnp.stack(pieces, axis=0), 0, 1)
    decode_out[...] = scaled.reshape(decode_out.shape).astype(bf16)


def call(
    kernel,
    name,
    outs,
    scalars,
    arrays,
    scratch=(),
    cost=0,
    space=pltpu.VMEM,
    scalar_space=pltpu.HBM,
):
    scalars = [pltpu.with_memory_space_constraint(x, pltpu.HBM) for x in scalars]
    if space is pltpu.HBM:
        arrays = [pltpu.with_memory_space_constraint(x, space) for x in arrays]
    shapes = [jax.ShapeDtypeStruct(shape, dtype) for shape, dtype in outs]
    specs = [pl.BlockSpec(memory_space=scalar_space)] * len(scalars)
    specs += [pl.BlockSpec(memory_space=space)] * len(arrays)
    return pl.pallas_call(
        kernel,
        name=name,
        out_shape=shapes,
        in_specs=specs,
        out_specs=[
            pl.BlockSpec(memory_space=pltpu.SMEM if dtype == jnp.int32 else pltpu.VMEM)
            for _, dtype in outs
        ],
        scratch_shapes=list(scratch),
        compiler_params=pltpu.CompilerParams(vmem_limit_bytes=24 * 2**20),
        cost_estimate=pl.CostEstimate(flops=cost, bytes_accessed=4 * 2**20, transcendentals=0),
    )(*scalars, *arrays)


def body(
    prefill_query,
    prefill_key,
    prefill_value,
    log_decay,
    lengths,
    owner,
    decode_state,
    step_query,
    step_key,
    step_value,
    step_decay,
    soft_query,
    cache_keys,
    cache_values,
    new_keys,
    new_values,
    row_lengths,
):
    block, heads, _ = prefill_query.shape
    steps, rows_n = step_query.shape[0], step_query.shape[1]
    blocks = lax.axis_size("ctx")
    planes = lax.axis_size("head")
    pairs = rows_n * heads
    decay_rows = jnp.swapaxes(log_decay, 0, 1)
    outgoing, second, shared = call(
        summary_kernel,
        "summary",
        [
            ((blocks, ROWS_OUT, 1, HD), f32),
            ((blocks, ROWS_SECOND, 1, HD), f32),
            ((1,), jnp.int32),
        ],
        [lengths, owner],
        [decay_rows, prefill_key, prefill_value, step_query],
        scratch=[
            pltpu.VMEM(prefill_key.shape, bf16),
            pltpu.VMEM(prefill_value.shape, bf16),
            pltpu.VMEM(decay_rows.shape, f32),
            pltpu.VMEM(step_query.shape, bf16),
            pltpu.SMEM(lengths.shape, jnp.int32),
            pltpu.SMEM(owner.shape, jnp.int32),
            pltpu.SemaphoreType.DMA((12,)),
        ],
        space=pltpu.HBM,
    )
    gathered = lax.all_to_all(outgoing, "ctx", 0, 0, tiled=True)
    local_inputs = [
        decay_rows,
        prefill_query,
        prefill_key,
        prefill_value,
        decode_state,
        step_query,
        step_key,
        step_value,
        jnp.transpose(step_decay, (1, 2, 0)),
        soft_query,
        cache_keys.reshape(rows_n, -1, HD),
        cache_values.reshape(rows_n, -1, HD),
        new_keys.reshape(steps, rows_n, HD),
        new_values.reshape(steps, rows_n, HD),
    ]
    intra, queries, gate, base, coef, soft_out = call(
        local_kernel,
        "local",
        [
            ((heads, block, HD), f32),
            ((heads, block, HD), bf16),
            ((block, 8), f32),
            ((pairs, steps, HD), f32),
            ((2, pairs, steps, HD), f32),
            (soft_query.shape, bf16),
        ],
        [lengths, owner, row_lengths],
        local_inputs,
        scratch=[pltpu.VMEM(x.shape, x.dtype) for x in local_inputs]
        + [pltpu.SemaphoreType.DMA((len(local_inputs),))],
        cost=2 * 10**9,
        space=pltpu.HBM,
        scalar_space=pltpu.SMEM,
    )
    shared, intra = lax.optimization_barrier((shared, intra))
    gathered, second = lax.optimization_barrier((gathered, second))
    slow = shared[0] > 0

    def exchange(x):
        return lax.all_to_all(x, "ctx", 0, 0, tiled=True)

    second = lax.cond(slow, exchange, lambda x: x, second)
    returning, second = call(
        functools.partial(scan_kernel, block),
        "scan",
        [((blocks, ROWS_BACK, 1, HD), f32), ((blocks, 2, 1, HD), f32)],
        [lengths, owner],
        [gathered, second],
        scratch=[
            pltpu.VMEM((blocks + 8, 8, HD), f32),
            pltpu.SMEM(lengths.shape, jnp.int32),
            pltpu.SMEM(owner.shape, jnp.int32),
            pltpu.SemaphoreType.DMA((2,)),
        ],
    )
    returned = lax.all_to_all(returning, "ctx", 0, 0, tiled=True)
    second = lax.cond(slow, exchange, lambda x: x, second)
    mixed, reads, squares = call(
        mix_kernel,
        "mix",
        [
            ((heads, block, HD), f32),
            ((pairs, steps, HD), f32),
            ((planes, 1, block + HD), f32),
        ],
        [],
        [returned, second, intra, queries, gate, base, coef],
    )
    squares = lax.all_to_all(squares, "head", 0, 0, tiled=True)
    prefill_out, decode_out = call(
        functools.partial(norm_kernel, float(planes * heads * HD)),
        "norm",
        [(prefill_query.shape, bf16), (step_query.shape, bf16)],
        [],
        [squares, mixed, reads],
    )
    return (prefill_out, decode_out, soft_out)


def solution(mesh):
    placed = (
        P("ctx", "head", None),
        P("ctx", "head", None),
        P("ctx", "head", None),
        P("ctx", "head"),
        P(),
        P(),
        P("ctx", "head", None, None),
        P(None, "ctx", "head", None),
        P(None, "ctx", "head", None),
        P(None, "ctx", "head", None),
        P(None, "ctx", "head"),
        P(None, "ctx", "head", None),
        P("ctx", None, "head", None),
        P("ctx", None, "head", None),
        P(None, "ctx", "head", None),
        P(None, "ctx", "head", None),
        P("ctx"),
    )
    return jax.shard_map(
        body,
        mesh=mesh,
        in_specs=placed,
        out_specs=(
            P("ctx", "head", None),
            P(None, "ctx", "head", None),
            P(None, "ctx", "head", None),
        ),
        check_vma=False,
    )
```

```python
import functools
import math

import jax
import jax.numpy as jnp
from jax import lax
from jax.experimental import pallas as pl
from jax.experimental.pallas import tpu as pltpu
from jax.sharding import PartitionSpec as P

f32 = jnp.float32
bf16 = jnp.bfloat16
eps = 1e-06
HD = 128
QUARTER = HD // 4
ROW_END = 8
ROW_QUERY = 16
ROW_DECAY = 18
ROWS_OUT = 19
ROWS_BACK = 10
ROWS_SECOND = 10
NT = (((1,), (1,)), ((), ()))
TN = (((0,), (0,)), ((), ()))
NN = (((1,), (0,)), ((), ()))


def mm(a, b, dims=NN):
    return lax.dot_general(a, b, dims, preferred_element_type=f32)


def iota(shape, dim):
    return lax.broadcasted_iota(jnp.int32, shape, dim)


def two(x):
    high = x.astype(bf16)
    return high, (x - high.astype(f32)).astype(bf16)


def three(x):
    high = x.astype(bf16)
    rest = x - high.astype(f32)
    mid = rest.astype(bf16)
    return high, mid, (rest - mid.astype(f32)).astype(bf16)


def prompt_bounds(lengths):
    ends, total = [], jnp.int32(0)
    starts = []
    for p in range(lengths.shape[0]):
        starts.append(total)
        total = total + lengths[p]
        ends.append(total)
    return starts, ends


def segment_of(positions, ends):
    segment = jnp.zeros(positions.shape, jnp.int32)
    for end in ends:
        segment = segment + (positions >= end).astype(jnp.int32)
    return segment


def scalar_segment(position, ends):
    segment = jnp.int32(0)
    for end in ends:
        segment = segment + (position >= end).astype(jnp.int32)
    return segment


def swap(first, second, width):
    shape = first.shape
    even = ((iota((1, HD), 1) // width) % 2 == 0).reshape((1,) * (len(shape) - 1) + (HD,))
    up = pltpu.roll(second.reshape(-1, HD), width, 1).reshape(shape)
    down = pltpu.roll(first.reshape(-1, HD), HD - width, 1).reshape(shape)
    return jnp.where(even, first, up), jnp.where(even, down, second)


def turn(a, b, c, d):
    a, c = swap(a, c, 2 * QUARTER)
    b, d = swap(b, d, 2 * QUARTER)
    a, b = swap(a, b, QUARTER)
    c, d = swap(c, d, QUARTER)
    return a, b, c, d


def cut(matrix):
    split = matrix.reshape(4, 4, 8, HD)
    return jnp.stack(turn(*(split[:, k] for k in range(4))), axis=1).reshape(16, 8, HD)


def uncut(chunks):
    return cut(chunks.reshape(HD, HD)).reshape(HD, HD)


def running_sums(decay):
    heads, block = decay.shape
    upto = (iota((HD, 1), 0) <= iota((1, HD), 1)).astype(f32).astype(bf16)
    pieces = [decay[:, low : low + HD] for low in range(0, block, HD)]
    stacked = jnp.concatenate(pieces, axis=0)
    local = sum(mm(part, upto) for part in three(stacked))
    out, before = [], None
    for k in range(len(pieces)):
        piece = local[k * heads : (k + 1) * heads]
        if before is not None:
            piece = piece + before
        out.append(piece)
        before = piece[:, HD - 1 : HD]
    return jnp.concatenate(out, axis=1)


def end_slot(slot, ends, block_start, block):
    prompt, offset = jnp.int32(-1), jnp.int32(-1)
    for p in range(len(ends)):
        if p % 2 != slot:
            continue
        local = ends[p] - 1 - block_start
        inside = (local >= 0) & (local < block) & (lax.rem(ends[p], block) != 0)
        prompt = jnp.where(inside, p, prompt)
        offset = jnp.where(inside, local, offset)
    return prompt, offset


def row_taken(owner, row):
    taken = jnp.bool_(False)
    for p in range(owner.shape[0]):
        taken = taken | (owner[p] == row)
    return taken


def block_shares(first, second, block):
    inside = (lax.rem(first, block) != 0) & (lax.rem(second, block) != 0)
    return inside & (first // block == second // block)


def summary_kernel(
    lengths_in,
    owner_in,
    decay,
    key,
    value,
    step_query,
    staged,
    second_out,
    key_buf,
    value_buf,
    decay_buf,
    query_buf,
    lengths,
    owner,
    sems,
):
    copies = [
        pltpu.make_async_copy(lengths_in, lengths, sems.at[0]),
        pltpu.make_async_copy(owner_in, owner, sems.at[1]),
        pltpu.make_async_copy(step_query, query_buf, sems.at[2]),
        pltpu.make_async_copy(decay, decay_buf, sems.at[3]),
    ]
    heads, block = decay_buf.shape
    quarter = block // 4
    for k in range(4):
        part = pl.ds(k * quarter, quarter)
        copies.append(pltpu.make_async_copy(key.at[part], key_buf.at[part], sems.at[4 + k]))
        copies.append(pltpu.make_async_copy(value.at[part], value_buf.at[part], sems.at[8 + k]))
    for copy in copies:
        copy.start()
    device = lax.axis_index("ctx")
    block_start = device * block

    copies[2].wait()
    steps, rows = query_buf.shape[0], query_buf.shape[1]
    pairs = rows * heads
    flat = query_buf[...].astype(f32).reshape(steps * pairs, HD).astype(bf16)
    lane = iota((1, 4 * HD), 1)
    pick = iota((HD, 1), 0) == (lane // HD) * QUARTER + lane % QUARTER
    read = mm(flat, pick.astype(f32).astype(bf16))
    spread = []
    for k in range(2):
        total = None
        for step in range(4):
            low = (4 * k + step) * pairs
            mine = (lane % HD) // QUARTER == step
            part = jnp.where(mine, read[low : low + pairs], 0.0)
            total = part if total is None else total + part
        spread.append(total)

    copies[3].wait()
    running = running_sums(decay_buf[...])

    for copy in copies[:2]:
        copy.wait()
    _, ends = prompt_bounds(lengths)
    place = iota((1, block), 1)
    segment = segment_of(place + block_start, ends)
    last = scalar_segment(block_start + block - 1, ends)
    prompt_a, offset_a = end_slot(0, ends, block_start, block)
    prompt_b, offset_b = end_slot(1, ends, block_start, block)
    both = (prompt_a >= 0) & (prompt_b >= 0)
    prompt_a = jnp.where(prompt_a >= 0, prompt_a, prompt_b)
    offset_a = jnp.where(offset_a >= 0, offset_a, offset_b)

    def weight(prompt, offset):
        inside = segment == prompt
        at = jnp.sum(jnp.where(place == offset, running, 0.0), axis=1, keepdims=True)
        weight = jnp.where(inside, jnp.exp(jnp.where(inside, at - running, 0.0)), 0.0)
        return weight, at

    weight_last, _ = weight(last, jnp.int32(block - 1))
    weight_a, at_a = weight(prompt_a, offset_a)
    weight_b, at_b = weight(prompt_b, offset_b)
    whole = jnp.sum(jnp.where(segment == last, decay_buf[...], 0.0), axis=1, keepdims=True)
    lane, head = iota((heads, HD), 1), iota((heads, HD), 0)
    totals = jnp.where(lane == head, whole, 0.0)
    totals = jnp.where(lane == heads + head, at_a, totals)
    totals = jnp.where(lane == 2 * heads + head, at_b, totals)
    totals = jnp.sum(totals, axis=0, keepdims=True)
    staged[:, ROW_DECAY, 0, :] = jnp.broadcast_to(totals, (staged.shape[0], HD))

    first_taken = row_taken(owner, device * rows)
    for h in range(heads):
        first = jnp.concatenate([part[h : h + 1] for part in spread], axis=0)
        other = jnp.concatenate([part[heads + h : heads + h + 1] for part in spread], axis=0)
        chosen = jnp.where(first_taken, first, other)
        for d in range(4):
            j = 16 * h + 4 * d
            staged[j : j + 4, ROW_QUERY:ROW_DECAY, 0, :] = jnp.broadcast_to(
                chosen[None, :, d * HD : (d + 1) * HD], (4, 2, HD)
            )

    @pl.when(first_taken & row_taken(owner, device * rows + 1))
    def _():
        for h in range(heads):
            other = jnp.concatenate([part[heads + h : heads + h + 1] for part in spread], axis=0)
            for d in range(4):
                j = 16 * h + 4 * d
                second_out[j : j + 4, 8:ROWS_SECOND, 0, :] = jnp.broadcast_to(
                    other[None, :, d * HD : (d + 1) * HD], (4, 2, HD)
                )

    for copy in copies[4:]:
        copy.wait()
    keys = jnp.swapaxes(key_buf[...], 0, 1)
    values = jnp.swapaxes(value_buf[...], 0, 1)
    for h in range(heads):
        key_h = keys[h].T.astype(f32)
        left = []
        for weight_k in (weight_last, weight_a):
            left.extend(two(key_h * weight_k[h : h + 1]))
        product = mm(jnp.concatenate(left, axis=0), values[h])
        for k in range(2):
            low = 2 * k * HD
            state = product[low : low + HD] + product[low + HD : low + 2 * HD]
            staged[16 * h : 16 * h + 16, 8 * k : 8 * k + 8, 0, :] = cut(state)

    @pl.when(both)
    def _():
        for h in range(heads):
            left = two(keys[h].T.astype(f32) * weight_b[h : h + 1])
            product = mm(jnp.concatenate(left, axis=0), values[h])
            second_out[16 * h : 16 * h + 16, 0:8, 0, :] = cut(product[:HD] + product[HD:])


def local_kernel(lengths, owner, row_lengths, *refs):
    count = (len(refs) - 9) // 2
    sources, outs = refs[:count], refs[count : count + 8]
    buffers, sems = refs[count + 8 : -1], refs[-1]
    copies = [
        pltpu.make_async_copy(source, buffer, sems.at[k])
        for k, (source, buffer) in enumerate(zip(sources, buffers))
    ]
    for copy in copies:
        copy.start()
    for copy in copies:
        copy.wait()
    (
        log_decay,
        query,
        key,
        value,
        decode_state,
        step_query,
        step_key,
        step_value,
        step_decay,
        soft_query,
        cache_keys,
        cache_values,
        new_keys,
        new_values,
    ) = buffers
    intra_out, query_out, gate_out, base_out, coef_out, soft_out, linked_out, shared_out = outs
    block, heads, _ = query.shape
    device = lax.axis_index("ctx")
    block_start = device * block
    starts, ends = prompt_bounds(lengths)
    shared_end, shared_row = jnp.bool_(False), jnp.bool_(False)
    for other in range(0, len(ends), 2):
        shared_end = shared_end | block_shares(ends[1], ends[other], block)
    for p in range(len(ends)):
        for other in range(p):
            shared_row = shared_row | (owner[p] // 2 == owner[other] // 2)
    shared_out[0] = (shared_end | shared_row).astype(jnp.int32)
    shared_out[1] = shared_row.astype(jnp.int32)
    to, frm = iota(linked_out.shape, 0), iota(linked_out.shape, 1)
    linked = frm < to
    for start in starts:
        restart = start // block
        linked = linked & ~((restart > frm) & (restart < to))
    linked_out[...] = linked.astype(f32)

    running = running_sums(log_decay[...])
    columns = jnp.concatenate([running, running], axis=0).T
    place_row = iota((1, block), 1) + block_start
    place_col = iota((block, 1), 0) + block_start
    segment_row = segment_of(place_row, ends)
    segment_col = segment_of(place_col, ends)
    before = jnp.where(block_start > 0, scalar_segment(block_start - 1, ends), -1)
    gate_out[...] = jnp.where(segment_col == before, jnp.exp(columns), 0.0)

    queries = jnp.swapaxes(query[...], 0, 1)
    keys = jnp.swapaxes(key[...], 0, 1)
    values = jnp.swapaxes(value[...], 0, 1)
    query_out[...] = queries
    half = block // 2
    tiles = ((0, 0), (1, 0), (1, 1))
    masks = {}
    for a, b in tiles:
        rows = slice(a * half, (a + 1) * half)
        cols = slice(b * half, (b + 1) * half)
        seen = segment_col[rows] == segment_row[:, cols]
        if a == b:
            seen = seen & (place_col[rows] >= place_row[:, cols])
        masks[a, b] = jnp.where(seen, 0.0, -1e30)
    for h in range(heads):
        mixed = [None, None]
        for a, b in tiles:
            rows = slice(a * half, (a + 1) * half)
            cols = slice(b * half, (b + 1) * half)
            scores = mm(queries[h][rows], keys[h][cols], NT)
            gap = columns[rows, h : h + 1] - running[h : h + 1, cols]
            weights = (scores * jnp.exp(gap + masks[a, b])).astype(bf16)
            term = mm(weights, values[h][cols])
            mixed[a] = term if mixed[a] is None else mixed[a] + term
        intra_out[h, :half, :] = mixed[0]
        intra_out[h, half:, :] = mixed[1]

    steps, rows_n = step_query.shape[0], step_query.shape[1]

    def by_head(ref):
        whole = ref[...].astype(f32).reshape(steps, rows_n * heads, HD)
        return jnp.swapaxes(whole, 0, 1)

    sq, sk, sv = by_head(step_query), by_head(step_key), by_head(step_value)
    decays = step_decay[...].reshape(rows_n * heads, steps)
    upto = (iota((steps, steps), 0) <= iota((steps, steps), 1)).astype(f32)
    cum_row = lax.dot_general(
        decays, upto, NN, precision=lax.Precision.HIGHEST, preferred_element_type=f32
    )
    cum_col = cum_row.T
    causal = iota((steps, steps), 0) >= iota((steps, steps), 1)
    for r in range(rows_n):
        taken = row_taken(owner, device * rows_n + r)
        owned = jnp.where(taken, 1.0, 0.0)
        late = jnp.where(taken & row_taken(owner, device * rows_n), r * 1.0, 0.0)
        for h in range(heads):
            n = r * heads + h
            cum = cum_col[:, n : n + 1]
            gap = jnp.where(causal, cum - cum_row[n : n + 1, :], 0.0)
            inner = mm(sq[n].astype(bf16), sk[n].astype(bf16), NT)
            inner = jnp.where(causal, inner * jnp.exp(gap), 0.0)
            fresh = lax.dot_general(
                inner, sv[n], NN, precision=lax.Precision.HIGHEST, preferred_element_type=f32
            )
            high, low = two(decode_state[r, h])
            read = mm(sq[n].astype(bf16), jnp.concatenate([high, low], axis=1))
            grown = jnp.exp(cum)
            read = (read[:, :HD] + read[:, HD:]) * grown
            base_out[n] = fresh + jnp.where(owned > 0.5, 0.0, read)
            coef_out[0, n] = jnp.broadcast_to(grown * (owned - late), (steps, HD))
            coef_out[1, n] = jnp.broadcast_to(grown * late, (steps, HD))

    fresh_keys = jnp.swapaxes(new_keys[...].astype(f32), 0, 1)
    fresh_values = jnp.swapaxes(new_values[...].astype(f32), 0, 1)
    group = soft_query.shape[2]
    cache = cache_keys.shape[1]
    scale = 1.0 / math.sqrt(HD)
    whole = soft_query[...].astype(f32)
    for r in range(rows_n):
        rows_q = whole[:, r].reshape(steps * group, HD).astype(bf16)
        cached = mm(rows_q, cache_keys[r], NT) * scale
        recent = mm(rows_q, fresh_keys[r].astype(bf16), NT) * scale
        slot = iota((steps * group, cache), 1)
        cached = jnp.where(slot < row_lengths[r], cached, -jnp.inf)
        step_of = iota((steps * group, steps), 0) // group
        recent = jnp.where(iota((steps * group, steps), 1) <= step_of, recent, -jnp.inf)
        top = jnp.maximum(
            jnp.max(cached, axis=1, keepdims=True), jnp.max(recent, axis=1, keepdims=True)
        )
        cached = jnp.exp(cached - top)
        recent = jnp.exp(recent - top)
        total = jnp.sum(cached, axis=1, keepdims=True) + jnp.sum(recent, axis=1, keepdims=True)
        cached = (cached / total).astype(bf16)
        recent = (recent / total).astype(bf16)
        mixed = mm(cached, cache_values[r]) + mm(recent, fresh_values[r].astype(bf16))
        soft_out[:, r, :, :] = mixed.reshape(steps, group, HD).astype(bf16)


def scan_kernel(
    block, lengths_in, owner_in, got, second, links, out, second_out, carried, lengths, owner, sems
):
    copies = [
        pltpu.make_async_copy(lengths_in, lengths, sems.at[0]),
        pltpu.make_async_copy(owner_in, owner, sems.at[1]),
    ]
    for copy in copies:
        copy.start()
    blocks = got.shape[0]
    device = lax.axis_index("ctx")
    head = device // 16
    padded = carried.shape[0]
    heads = blocks // 16

    decays = got[:, ROW_DECAY, 0, :]
    decay = jnp.sum(
        jnp.where(iota((blocks, HD), 1) == head, decays, 0.0), axis=1, keepdims=True
    )
    k_at, b_at = iota((blocks, blocks), 0), iota((blocks, blocks), 1)
    later = jnp.concatenate(
        [jnp.where(k_at > b_at, part.astype(f32), 0.0).astype(bf16) for part in three(decay)],
        axis=0,
    )
    earlier = iota((padded, 3 * blocks), 1) % blocks < iota((padded, 3 * blocks), 0)
    gap = mm(earlier.astype(f32).astype(bf16), later)
    right = []
    for i in range(8):
        high, low = two(got[:, i, 0, :])
        right.append(jnp.concatenate([high, low, high], axis=0))
    right = jnp.concatenate(right, axis=1)

    linked = links[...] > 0.5
    weight = jnp.where(linked, jnp.exp(jnp.where(linked, gap, 0.0)), 0.0)
    high, low = two(weight)
    weights = jnp.concatenate([high, high, low], axis=1)
    product = mm(weights, right)
    for i in range(8):
        state = product[:, i * HD : (i + 1) * HD]
        carried[:, i, :] = state
        out[:, i, 0, :] = state[:blocks]
        if i < ROWS_BACK - 8:
            out[:, 8 + i, 0, :] = jnp.zeros((blocks, HD), f32)

    second_out[...] = jnp.zeros(second_out.shape, f32)
    quarter_of = iota((1, HD), 1) // QUARTER
    for copy in copies:
        copy.wait()
    starts, ends = prompt_bounds(lengths)
    reads = []
    for p in range(len(ends)):
        index = ends[p] // block
        source = jnp.minimum(index, blocks - 1)
        partial = lax.rem(ends[p], block) != 0
        leads = (starts[p] < index * block).astype(f32)
        if p % 2:
            shared = jnp.bool_(False)
            for other in range(0, len(ends), 2):
                shared = shared | block_shares(ends[p], ends[other], block)
        else:
            shared = jnp.bool_(False)
        run = got[source, ROW_DECAY, :, :]
        at = jnp.where(shared, 2 * heads, heads) + head
        run = jnp.sum(jnp.where(iota((1, HD), 1) == at, run, 0.0), axis=1, keepdims=True)
        lead = leads * jnp.exp(jnp.where(partial, run, 0.0))
        rest = got[source, ROW_END : ROW_END + 8, 0, :]
        if p % 2:
            rest = jnp.where(shared, second[source, 0:8, 0, :], rest)
        handed = carried[index] * lead + jnp.where(partial, rest, 0.0)
        turned = [handed] + [pltpu.roll(handed, k * QUARTER, 1) for k in range(1, 4)]
        rows = []
        for k in range(4):
            for g in range(4):
                rows.append(jnp.where(quarter_of == k, turned[(k - g) % 4], 0.0))
        rows = jnp.concatenate(rows, axis=0)
        place = owner[p] // 2
        late = (lax.rem(owner[p], 2) == 1) & row_taken(owner, owner[p] - 1)
        query = jnp.where(
            late, second[place, 8:ROWS_SECOND, 0, :], got[place, ROW_QUERY:ROW_DECAY, 0, :]
        )
        read = mm(query.astype(bf16), jnp.concatenate(two(rows), axis=1))
        reads.append((place, late, read[:, :HD] + read[:, HD:]))
    for place, late, read in reads:

        @pl.when(late)
        def _():
            second_out[place, :, 0, :] = read

        @pl.when(jnp.logical_not(late))
        def _():
            out[place, 8:ROWS_BACK, 0, :] = read


def mix_kernel(got, second, intra, query, gate, base, coef, mixed_out, reads_out, squares_out):
    heads, block, _ = intra.shape
    total = None
    for h in range(heads):
        state = uncut(got[16 * h : 16 * h + 16, 0:8, 0, :])
        high, low = two(state)
        read = mm(query[h], jnp.concatenate([high, low], axis=1))
        mixed = intra[h] + (read[:, :HD] + read[:, HD:]) * gate[:, h : h + 1]
        mixed_out[h] = mixed
        total = mixed * mixed if total is None else total + mixed * mixed
    ones = jnp.ones((8, HD), bf16)
    high, low = two(total)
    planes = squares_out.shape[0]
    squares_out[:, 0, :block] = (mm(ones, high, NT) + mm(ones, low, NT))[:planes]

    def handed_reads(ref, low):
        pieces = []
        for e in range(4):
            parts = []
            for h in range(heads):
                total = ref[16 * h + e, low : low + 2, 0, :]
                for d in range(1, 4):
                    total = total + ref[16 * h + 4 * d + e, low : low + 2, 0, :]
                parts.append(total)
            pieces.append(jnp.concatenate(parts, axis=0))
        whole = jnp.swapaxes(jnp.stack(turn(*pieces), axis=0), 0, 1)
        return whole.reshape(heads, 8, HD)

    first, late = handed_reads(got, 8), handed_reads(second, 0)
    rows_n = base.shape[0] // heads
    squares = [None] * rows_n
    for h in range(heads):
        for r in range(rows_n):
            n = r * heads + h
            read = base[n] + coef[0, n] * first[h] + coef[1, n] * late[h]
            reads_out[n] = read
            squares[r] = read * read if squares[r] is None else squares[r] + read * read
    high, low = two(jnp.concatenate(squares, axis=0))
    sums = mm(ones, high, NT) + mm(ones, low, NT)
    sums = jnp.concatenate([sums, jnp.zeros((8, HD - sums.shape[1]), f32)], axis=1)
    squares_out[:, 0, block:] = sums[:planes]


def norm_kernel(count, got, mixed, reads, prefill_out, decode_out):
    heads, block, _ = mixed.shape
    parts = jnp.concatenate(three(got[:, 0, :]), axis=0)
    ones = jnp.ones((parts.shape[0], HD), bf16)
    total = mm(parts, ones, TN)
    scale = lax.rsqrt(total / count + eps)
    scaled = jnp.stack([mixed[h] * scale[:block] for h in range(heads)], axis=0)
    prefill_out[...] = jnp.swapaxes(scaled, 0, 1).astype(bf16)
    steps, rows_n = decode_out.shape[0], decode_out.shape[1]
    pieces = []
    for r in range(rows_n):
        low = block + r * steps
        for h in range(heads):
            pieces.append(reads[r * heads + h] * scale[low : low + steps])
    scaled = jnp.swapaxes(jnp.stack(pieces, axis=0), 0, 1)
    decode_out[...] = scaled.reshape(decode_out.shape).astype(bf16)


def call(
    kernel,
    name,
    outs,
    scalars,
    arrays,
    scratch=(),
    cost=0,
    space=pltpu.VMEM,
    scalar_space=pltpu.HBM,
    first_out=pltpu.VMEM,
):
    scalars = [pltpu.with_memory_space_constraint(x, pltpu.HBM) for x in scalars]
    if space is pltpu.HBM:
        arrays = [pltpu.with_memory_space_constraint(x, space) for x in arrays]
    shapes = [jax.ShapeDtypeStruct(shape, dtype) for shape, dtype in outs]
    specs = [pl.BlockSpec(memory_space=scalar_space)] * len(scalars)
    specs += [pl.BlockSpec(memory_space=space)] * len(arrays)
    return pl.pallas_call(
        kernel,
        name=name,
        out_shape=shapes,
        in_specs=specs,
        out_specs=[
            pl.BlockSpec(memory_space=pltpu.SMEM if dtype == jnp.int32 else space_k)
            for (_, dtype), space_k in zip(outs, [first_out] + [pltpu.VMEM] * len(outs))
        ],
        scratch_shapes=list(scratch),
        compiler_params=pltpu.CompilerParams(vmem_limit_bytes=24 * 2**20),
        cost_estimate=pl.CostEstimate(flops=cost, bytes_accessed=4 * 2**20, transcendentals=0),
    )(*scalars, *arrays)


def body(
    prefill_query,
    prefill_key,
    prefill_value,
    log_decay,
    lengths,
    owner,
    decode_state,
    step_query,
    step_key,
    step_value,
    step_decay,
    soft_query,
    cache_keys,
    cache_values,
    new_keys,
    new_values,
    row_lengths,
):
    block, heads, _ = prefill_query.shape
    steps, rows_n = step_query.shape[0], step_query.shape[1]
    blocks = lax.axis_size("ctx")
    planes = lax.axis_size("head")
    pairs = rows_n * heads
    decay_rows = jnp.swapaxes(log_decay, 0, 1)
    outgoing, second = call(
        summary_kernel,
        "summary",
        [
            ((blocks, ROWS_OUT, 1, HD), f32),
            ((blocks, ROWS_SECOND, 1, HD), f32),
        ],
        [lengths, owner],
        [decay_rows, prefill_key, prefill_value, step_query],
        scratch=[
            pltpu.VMEM(prefill_key.shape, bf16),
            pltpu.VMEM(prefill_value.shape, bf16),
            pltpu.VMEM(decay_rows.shape, f32),
            pltpu.VMEM(step_query.shape, bf16),
            pltpu.SMEM(lengths.shape, jnp.int32),
            pltpu.SMEM(owner.shape, jnp.int32),
            pltpu.SemaphoreType.DMA((12,)),
        ],
        space=pltpu.HBM,
    )
    gathered = lax.all_to_all(outgoing, "ctx", 0, 0, tiled=True)
    local_inputs = [
        decay_rows,
        prefill_query,
        prefill_key,
        prefill_value,
        decode_state,
        step_query,
        step_key,
        step_value,
        jnp.transpose(step_decay, (1, 2, 0)),
        soft_query,
        cache_keys.reshape(rows_n, -1, HD),
        cache_values.reshape(rows_n, -1, HD),
        new_keys.reshape(steps, rows_n, HD),
        new_values.reshape(steps, rows_n, HD),
    ]
    intra, queries, gate, base, coef, soft_out, links, shared = call(
        local_kernel,
        "local",
        [
            ((heads, block, HD), f32),
            ((heads, block, HD), bf16),
            ((block, 8), f32),
            ((pairs, steps, HD), f32),
            ((2, pairs, steps, HD), f32),
            (soft_query.shape, bf16),
            ((blocks + 8, blocks), f32),
            ((2,), jnp.int32),
        ],
        [lengths, owner, row_lengths],
        local_inputs,
        scratch=[pltpu.VMEM(x.shape, x.dtype) for x in local_inputs]
        + [pltpu.SemaphoreType.DMA((len(local_inputs),))],
        cost=2 * 10**9,
        space=pltpu.HBM,
        scalar_space=pltpu.SMEM,
    )
    shared, intra = lax.optimization_barrier((shared, intra))
    gathered, second = lax.optimization_barrier((gathered, second))

    def exchange(x):
        return lax.all_to_all(x, "ctx", 0, 0, tiled=True)

    second = lax.cond(shared[0] > 0, exchange, lambda x: x, second)
    returning, second = call(
        functools.partial(scan_kernel, block),
        "scan",
        [((blocks, ROWS_BACK, 1, HD), f32), ((blocks, 2, 1, HD), f32)],
        [lengths, owner],
        [gathered, second, links],
        scratch=[
            pltpu.VMEM((blocks + 8, 8, HD), f32),
            pltpu.SMEM(lengths.shape, jnp.int32),
            pltpu.SMEM(owner.shape, jnp.int32),
            pltpu.SemaphoreType.DMA((2,)),
        ],
    )
    returned = lax.all_to_all(returning, "ctx", 0, 0, tiled=True)
    second = lax.cond(shared[1] > 0, exchange, lambda x: x, second)
    mixed, reads, squares = call(
        mix_kernel,
        "mix",
        [
            ((heads, block, HD), f32),
            ((pairs, steps, HD), f32),
            ((planes, 1, block + HD), f32),
        ],
        [],
        [returned, second, intra, queries, gate, base, coef],
    )
    squares = lax.all_to_all(squares, "head", 0, 0, tiled=True)
    prefill_out, decode_out = call(
        functools.partial(norm_kernel, float(planes * heads * HD)),
        "norm",
        [(prefill_query.shape, bf16), (step_query.shape, bf16)],
        [],
        [squares, mixed, reads],
    )
    return (prefill_out, decode_out, soft_out)


def solution(mesh):
    placed = (
        P("ctx", "head", None),
        P("ctx", "head", None),
        P("ctx", "head", None),
        P("ctx", "head"),
        P(),
        P(),
        P("ctx", "head", None, None),
        P(None, "ctx", "head", None),
        P(None, "ctx", "head", None),
        P(None, "ctx", "head", None),
        P(None, "ctx", "head"),
        P(None, "ctx", "head", None),
        P("ctx", None, "head", None),
        P("ctx", None, "head", None),
        P(None, "ctx", "head", None),
        P(None, "ctx", "head", None),
        P("ctx"),
    )
    return jax.shard_map(
        body,
        mesh=mesh,
        in_specs=placed,
        out_specs=(
            P("ctx", "head", None),
            P(None, "ctx", "head", None),
            P(None, "ctx", "head", None),
        ),
        check_vma=False,
    )
```

```python
import functools
import math

import jax
import jax.numpy as jnp
from jax import lax
from jax.experimental import pallas as pl
from jax.experimental.pallas import tpu as pltpu
from jax.sharding import PartitionSpec as P

f32 = jnp.float32
bf16 = jnp.bfloat16
eps = 1e-06
HD = 128
QUARTER = HD // 4
ROW_END = 8
ROW_QUERY = 16
ROW_DECAY = 18
ROWS_OUT = 19
ROWS_BACK = 10
ROWS_SECOND = 10
NT = (((1,), (1,)), ((), ()))
TN = (((0,), (0,)), ((), ()))
NN = (((1,), (0,)), ((), ()))


def mm(a, b, dims=NN):
    return lax.dot_general(a, b, dims, preferred_element_type=f32)


def iota(shape, dim):
    return lax.broadcasted_iota(jnp.int32, shape, dim)


def two(x):
    high = x.astype(bf16)
    return high, (x - high.astype(f32)).astype(bf16)


def three(x):
    high = x.astype(bf16)
    rest = x - high.astype(f32)
    mid = rest.astype(bf16)
    return high, mid, (rest - mid.astype(f32)).astype(bf16)


def prompt_bounds(lengths):
    ends, total = [], jnp.int32(0)
    starts = []
    for p in range(lengths.shape[0]):
        starts.append(total)
        total = total + lengths[p]
        ends.append(total)
    return starts, ends


def segment_of(positions, ends):
    segment = jnp.zeros(positions.shape, jnp.int32)
    for end in ends:
        segment = segment + (positions >= end).astype(jnp.int32)
    return segment


def scalar_segment(position, ends):
    segment = jnp.int32(0)
    for end in ends:
        segment = segment + (position >= end).astype(jnp.int32)
    return segment


def swap(first, second, width):
    shape = first.shape
    even = ((iota((1, HD), 1) // width) % 2 == 0).reshape((1,) * (len(shape) - 1) + (HD,))
    up = pltpu.roll(second.reshape(-1, HD), width, 1).reshape(shape)
    down = pltpu.roll(first.reshape(-1, HD), HD - width, 1).reshape(shape)
    return jnp.where(even, first, up), jnp.where(even, down, second)


def turn(a, b, c, d):
    a, c = swap(a, c, 2 * QUARTER)
    b, d = swap(b, d, 2 * QUARTER)
    a, b = swap(a, b, QUARTER)
    c, d = swap(c, d, QUARTER)
    return a, b, c, d


def cut(matrix):
    split = matrix.reshape(4, 4, 8, HD)
    return jnp.stack(turn(*(split[:, k] for k in range(4))), axis=1).reshape(16, 8, HD)


def uncut(chunks):
    return cut(chunks.reshape(HD, HD)).reshape(HD, HD)


def running_sums(decay):
    heads, block = decay.shape
    upto = (iota((HD, 1), 0) <= iota((1, HD), 1)).astype(f32).astype(bf16)
    upto = jnp.concatenate([upto, jnp.ones((HD, HD), bf16)], axis=1)
    pieces = [decay[:, low : low + HD] for low in range(0, block, HD)]
    stacked = jnp.concatenate(pieces, axis=0)
    local = sum(mm(part, upto) for part in three(stacked))
    out, before = [], None
    for k in range(len(pieces)):
        rows = slice(k * heads, (k + 1) * heads)
        out.append(local[rows, :HD] if before is None else local[rows, :HD] + before)
        before = local[rows, HD:] if before is None else before + local[rows, HD:]
    return jnp.concatenate(out, axis=1)


def end_slot(slot, ends, block_start, block):
    prompt, offset = jnp.int32(-1), jnp.int32(-1)
    for p in range(len(ends)):
        if p % 2 != slot:
            continue
        local = ends[p] - 1 - block_start
        inside = (local >= 0) & (local < block) & (lax.rem(ends[p], block) != 0)
        prompt = jnp.where(inside, p, prompt)
        offset = jnp.where(inside, local, offset)
    return prompt, offset


def row_taken(owner, row):
    taken = jnp.bool_(False)
    for p in range(owner.shape[0]):
        taken = taken | (owner[p] == row)
    return taken


def block_shares(first, second, block):
    inside = (lax.rem(first, block) != 0) & (lax.rem(second, block) != 0)
    return inside & (first // block == second // block)


def summary_kernel(
    lengths_in,
    owner_in,
    decay,
    key,
    value,
    step_query,
    staged,
    second_out,
    key_buf,
    value_buf,
    decay_buf,
    query_buf,
    lengths,
    owner,
    sems,
):
    copies = [
        pltpu.make_async_copy(lengths_in, lengths, sems.at[0]),
        pltpu.make_async_copy(owner_in, owner, sems.at[1]),
        pltpu.make_async_copy(step_query, query_buf, sems.at[2]),
        pltpu.make_async_copy(decay, decay_buf, sems.at[3]),
    ]
    heads, block = decay_buf.shape
    quarter = block // 4
    for k in range(4):
        part = pl.ds(k * quarter, quarter)
        copies.append(pltpu.make_async_copy(key.at[part], key_buf.at[part], sems.at[4 + k]))
        copies.append(pltpu.make_async_copy(value.at[part], value_buf.at[part], sems.at[8 + k]))
    for copy in copies:
        copy.start()
    device = lax.axis_index("ctx")
    block_start = device * block

    copies[2].wait()
    steps, rows = query_buf.shape[0], query_buf.shape[1]
    pairs = rows * heads
    flat = query_buf[...].astype(f32).reshape(steps * pairs, HD).astype(bf16)
    lane = iota((1, 4 * HD), 1)
    pick = iota((HD, 1), 0) == (lane // HD) * QUARTER + lane % QUARTER
    read = mm(flat, pick.astype(f32).astype(bf16))
    spread = []
    for k in range(2):
        total = None
        for step in range(4):
            low = (4 * k + step) * pairs
            mine = (lane % HD) // QUARTER == step
            part = jnp.where(mine, read[low : low + pairs], 0.0)
            total = part if total is None else total + part
        spread.append(total)

    copies[3].wait()
    running = running_sums(decay_buf[...])

    for copy in copies[:2]:
        copy.wait()
    _, ends = prompt_bounds(lengths)
    place = iota((1, block), 1)
    segment = segment_of(place + block_start, ends)
    last = scalar_segment(block_start + block - 1, ends)
    prompt_a, offset_a = end_slot(0, ends, block_start, block)
    prompt_b, offset_b = end_slot(1, ends, block_start, block)
    both = (prompt_a >= 0) & (prompt_b >= 0)
    prompt_a = jnp.where(prompt_a >= 0, prompt_a, prompt_b)
    offset_a = jnp.where(offset_a >= 0, offset_a, offset_b)

    def weight(prompt, offset):
        inside = segment == prompt
        at = jnp.sum(jnp.where(place == offset, running, 0.0), axis=1, keepdims=True)
        weight = jnp.where(inside, jnp.exp(jnp.where(inside, at - running, 0.0)), 0.0)
        return weight, at

    weight_last, _ = weight(last, jnp.int32(block - 1))
    weight_a, at_a = weight(prompt_a, offset_a)
    whole = jnp.sum(jnp.where(segment == last, decay_buf[...], 0.0), axis=1, keepdims=True)
    lane, head = iota((heads, HD), 1), iota((heads, HD), 0)
    totals = jnp.where(lane == head, whole, 0.0)
    totals = jnp.where(lane == heads + head, at_a, totals)
    totals = jnp.sum(totals, axis=0, keepdims=True)
    staged[:, ROW_DECAY, 0, :] = jnp.broadcast_to(totals, (staged.shape[0], HD))

    first_taken = row_taken(owner, device * rows)
    for h in range(heads):
        first = jnp.concatenate([part[h : h + 1] for part in spread], axis=0)
        other = jnp.concatenate([part[heads + h : heads + h + 1] for part in spread], axis=0)
        chosen = jnp.where(first_taken, first, other)
        for d in range(4):
            j = 16 * h + 4 * d
            staged[j : j + 4, ROW_QUERY:ROW_DECAY, 0, :] = jnp.broadcast_to(
                chosen[None, :, d * HD : (d + 1) * HD], (4, 2, HD)
            )

    @pl.when(first_taken & row_taken(owner, device * rows + 1))
    def _():
        for h in range(heads):
            other = jnp.concatenate([part[heads + h : heads + h + 1] for part in spread], axis=0)
            for d in range(4):
                j = 16 * h + 4 * d
                second_out[j : j + 4, 8:ROWS_SECOND, 0, :] = jnp.broadcast_to(
                    other[None, :, d * HD : (d + 1) * HD], (4, 2, HD)
                )

    for copy in copies[4:]:
        copy.wait()
    keys = jnp.swapaxes(key_buf[...], 0, 1)
    values = jnp.swapaxes(value_buf[...], 0, 1)
    for h in range(heads):
        key_h = keys[h].T.astype(f32)
        left = []
        for weight_k in (weight_last, weight_a):
            left.extend(two(key_h * weight_k[h : h + 1]))
        product = mm(jnp.concatenate(left, axis=0), values[h])
        for k in range(2):
            low = 2 * k * HD
            state = product[low : low + HD] + product[low + HD : low + 2 * HD]
            staged[16 * h : 16 * h + 16, 8 * k : 8 * k + 8, 0, :] = cut(state)

    @pl.when(both)
    def _():
        weight_b, at_b = weight(prompt_b, offset_b)
        more = jnp.sum(jnp.where(lane == 2 * heads + head, at_b, 0.0), axis=0, keepdims=True)
        staged[:, ROW_DECAY, 0, :] = jnp.broadcast_to(totals + more, (staged.shape[0], HD))
        for h in range(heads):
            left = two(keys[h].T.astype(f32) * weight_b[h : h + 1])
            product = mm(jnp.concatenate(left, axis=0), values[h])
            second_out[16 * h : 16 * h + 16, 0:8, 0, :] = cut(product[:HD] + product[HD:])


def local_kernel(lengths, owner, row_lengths, *refs):
    count = (len(refs) - 9) // 2
    sources, outs = refs[:count], refs[count : count + 8]
    buffers, sems = refs[count + 8 : -1], refs[-1]
    copies = [
        pltpu.make_async_copy(source, buffer, sems.at[k])
        for k, (source, buffer) in enumerate(zip(sources, buffers))
    ]
    for copy in copies:
        copy.start()
    for copy in copies:
        copy.wait()
    (
        log_decay,
        query,
        key,
        value,
        decode_state,
        step_query,
        step_key,
        step_value,
        step_decay,
        soft_query,
        cache_keys,
        cache_values,
        new_keys,
        new_values,
    ) = buffers
    intra_out, query_out, gate_out, base_out, coef_out, soft_out, linked_out, shared_out = outs
    block, heads, _ = query.shape
    device = lax.axis_index("ctx")
    block_start = device * block
    starts, ends = prompt_bounds(lengths)
    shared_end, shared_row = jnp.bool_(False), jnp.bool_(False)
    for other in range(0, len(ends), 2):
        shared_end = shared_end | block_shares(ends[1], ends[other], block)
    for p in range(len(ends)):
        for other in range(p):
            shared_row = shared_row | (owner[p] // 2 == owner[other] // 2)
    shared_out[0] = (shared_end | shared_row).astype(jnp.int32)
    shared_out[1] = shared_row.astype(jnp.int32)
    to, frm = iota(linked_out.shape, 0), iota(linked_out.shape, 1)
    linked = frm < to
    for start in starts:
        restart = start // block
        linked = linked & ~((restart > frm) & (restart < to))
    linked_out[...] = linked.astype(f32)

    running = running_sums(log_decay[...])
    columns = jnp.concatenate([running, running], axis=0).T
    place_row = iota((1, block), 1) + block_start
    place_col = iota((block, 1), 0) + block_start
    segment_row = segment_of(place_row, ends)
    segment_col = segment_of(place_col, ends)
    before = jnp.where(block_start > 0, scalar_segment(block_start - 1, ends), -1)
    gate_out[...] = jnp.where(segment_col == before, jnp.exp(columns), 0.0)

    queries = jnp.swapaxes(query[...], 0, 1)
    keys = jnp.swapaxes(key[...], 0, 1)
    values = jnp.swapaxes(value[...], 0, 1)
    query_out[...] = queries
    half = block // 2
    tiles = ((0, 0), (1, 0), (1, 1))
    masks = {}
    for a, b in tiles:
        rows = slice(a * half, (a + 1) * half)
        cols = slice(b * half, (b + 1) * half)
        seen = segment_col[rows] == segment_row[:, cols]
        if a == b:
            seen = seen & (place_col[rows] >= place_row[:, cols])
        masks[a, b] = jnp.where(seen, 0.0, -1e30)
    for h in range(heads):
        mixed = [None, None]
        for a, b in tiles:
            rows = slice(a * half, (a + 1) * half)
            cols = slice(b * half, (b + 1) * half)
            scores = mm(queries[h][rows], keys[h][cols], NT)
            gap = columns[rows, h : h + 1] - running[h : h + 1, cols]
            weights = (scores * jnp.exp(gap + masks[a, b])).astype(bf16)
            term = mm(weights, values[h][cols])
            mixed[a] = term if mixed[a] is None else mixed[a] + term
        intra_out[h, :half, :] = mixed[0]
        intra_out[h, half:, :] = mixed[1]

    steps, rows_n = step_query.shape[0], step_query.shape[1]

    def by_head(ref):
        whole = ref[...].astype(f32).reshape(steps, rows_n * heads, HD)
        return jnp.swapaxes(whole, 0, 1)

    sq, sk, sv = by_head(step_query), by_head(step_key), by_head(step_value)
    decays = step_decay[...].reshape(rows_n * heads, steps)
    upto = (iota((steps, steps), 0) <= iota((steps, steps), 1)).astype(f32)
    cum_row = lax.dot_general(
        decays, upto, NN, precision=lax.Precision.HIGHEST, preferred_element_type=f32
    )
    cum_col = cum_row.T
    causal = iota((steps, steps), 0) >= iota((steps, steps), 1)
    for r in range(rows_n):
        taken = row_taken(owner, device * rows_n + r)
        owned = jnp.where(taken, 1.0, 0.0)
        late = jnp.where(taken & row_taken(owner, device * rows_n), r * 1.0, 0.0)
        for h in range(heads):
            n = r * heads + h
            cum = cum_col[:, n : n + 1]
            gap = jnp.where(causal, cum - cum_row[n : n + 1, :], 0.0)
            inner = mm(sq[n].astype(bf16), sk[n].astype(bf16), NT)
            inner = jnp.where(causal, inner * jnp.exp(gap), 0.0)
            fresh = lax.dot_general(
                inner, sv[n], NN, precision=lax.Precision.HIGHEST, preferred_element_type=f32
            )
            high, low = two(decode_state[r, h])
            read = mm(sq[n].astype(bf16), jnp.concatenate([high, low], axis=1))
            grown = jnp.exp(cum)
            read = (read[:, :HD] + read[:, HD:]) * grown
            base_out[n] = fresh + jnp.where(owned > 0.5, 0.0, read)
            coef_out[0, n] = jnp.broadcast_to(grown * (owned - late), (steps, HD))
            coef_out[1, n] = jnp.broadcast_to(grown * late, (steps, HD))

    fresh_keys = jnp.swapaxes(new_keys[...].astype(f32), 0, 1)
    fresh_values = jnp.swapaxes(new_values[...].astype(f32), 0, 1)
    group = soft_query.shape[2]
    cache = cache_keys.shape[1]
    scale = 1.0 / math.sqrt(HD)
    whole = soft_query[...].astype(f32)
    for r in range(rows_n):
        rows_q = whole[:, r].reshape(steps * group, HD).astype(bf16)
        cached = mm(rows_q, cache_keys[r], NT) * scale
        recent = mm(rows_q, fresh_keys[r].astype(bf16), NT) * scale
        slot = iota((steps * group, cache), 1)
        cached = jnp.where(slot < row_lengths[r], cached, -jnp.inf)
        step_of = iota((steps * group, steps), 0) // group
        recent = jnp.where(iota((steps * group, steps), 1) <= step_of, recent, -jnp.inf)
        top = jnp.maximum(
            jnp.max(cached, axis=1, keepdims=True), jnp.max(recent, axis=1, keepdims=True)
        )
        cached = jnp.exp(cached - top)
        recent = jnp.exp(recent - top)
        total = jnp.sum(cached, axis=1, keepdims=True) + jnp.sum(recent, axis=1, keepdims=True)
        cached = (cached / total).astype(bf16)
        recent = (recent / total).astype(bf16)
        mixed = mm(cached, cache_values[r]) + mm(recent, fresh_values[r].astype(bf16))
        soft_out[:, r, :, :] = mixed.reshape(steps, group, HD).astype(bf16)


def scan_kernel(
    block, lengths_in, owner_in, got, second, links, out, second_out, carried, lengths, owner, sems
):
    copies = [
        pltpu.make_async_copy(lengths_in, lengths, sems.at[0]),
        pltpu.make_async_copy(owner_in, owner, sems.at[1]),
    ]
    for copy in copies:
        copy.start()
    blocks = got.shape[0]
    device = lax.axis_index("ctx")
    head = device // 16
    padded = carried.shape[0]
    heads = blocks // 16

    decays = got[:, ROW_DECAY, 0, :]
    decay = jnp.sum(
        jnp.where(iota((blocks, HD), 1) == head, decays, 0.0), axis=1, keepdims=True
    )
    k_at, b_at = iota((blocks, blocks), 0), iota((blocks, blocks), 1)
    later = jnp.concatenate(
        [jnp.where(k_at > b_at, part.astype(f32), 0.0).astype(bf16) for part in three(decay)],
        axis=0,
    )
    earlier = iota((padded, 3 * blocks), 1) % blocks < iota((padded, 3 * blocks), 0)
    gap = mm(earlier.astype(f32).astype(bf16), later)
    right = []
    for i in range(8):
        high, low = two(got[:, i, 0, :])
        right.append(jnp.concatenate([high, low, high], axis=0))
    right = jnp.concatenate(right, axis=1)

    linked = links[...] > 0.5
    weight = jnp.where(linked, jnp.exp(jnp.where(linked, gap, 0.0)), 0.0)
    high, low = two(weight)
    weights = jnp.concatenate([high, high, low], axis=1)
    product = mm(weights, right)
    for i in range(8):
        state = product[:, i * HD : (i + 1) * HD]
        carried[:, i, :] = state
        out[:, i, 0, :] = state[:blocks]
        if i < ROWS_BACK - 8:
            out[:, 8 + i, 0, :] = jnp.zeros((blocks, HD), f32)

    second_out[...] = jnp.zeros(second_out.shape, f32)
    quarter_of = iota((1, HD), 1) // QUARTER
    for copy in copies:
        copy.wait()
    starts, ends = prompt_bounds(lengths)
    reads = []
    for p in range(len(ends)):
        index = ends[p] // block
        source = jnp.minimum(index, blocks - 1)
        partial = lax.rem(ends[p], block) != 0
        leads = (starts[p] < index * block).astype(f32)
        if p % 2:
            shared = jnp.bool_(False)
            for other in range(0, len(ends), 2):
                shared = shared | block_shares(ends[p], ends[other], block)
        else:
            shared = jnp.bool_(False)
        run = got[source, ROW_DECAY, :, :]
        at = jnp.where(shared, 2 * heads, heads) + head
        run = jnp.sum(jnp.where(iota((1, HD), 1) == at, run, 0.0), axis=1, keepdims=True)
        lead = leads * jnp.exp(jnp.where(partial, run, 0.0))
        rest = got[source, ROW_END : ROW_END + 8, 0, :]
        if p % 2:
            rest = jnp.where(shared, second[source, 0:8, 0, :], rest)
        handed = carried[index] * lead + jnp.where(partial, rest, 0.0)
        turned = [handed] + [pltpu.roll(handed, k * QUARTER, 1) for k in range(1, 4)]
        rows = []
        for k in range(4):
            for g in range(4):
                rows.append(jnp.where(quarter_of == k, turned[(k - g) % 4], 0.0))
        rows = jnp.concatenate(rows, axis=0)
        place = owner[p] // 2
        late = (lax.rem(owner[p], 2) == 1) & row_taken(owner, owner[p] - 1)
        query = jnp.where(
            late, second[place, 8:ROWS_SECOND, 0, :], got[place, ROW_QUERY:ROW_DECAY, 0, :]
        )
        read = mm(query.astype(bf16), jnp.concatenate(two(rows), axis=1))
        reads.append((place, late, read[:, :HD] + read[:, HD:]))
    for place, late, read in reads:

        @pl.when(late)
        def _():
            second_out[place, :, 0, :] = read

        @pl.when(jnp.logical_not(late))
        def _():
            out[place, 8:ROWS_BACK, 0, :] = read


def mix_kernel(got, second, intra, query, gate, base, coef, mixed_out, reads_out, squares_out):
    heads, block, _ = intra.shape
    total = None
    for h in range(heads):
        state = uncut(got[16 * h : 16 * h + 16, 0:8, 0, :])
        high, low = two(state)
        read = mm(query[h], jnp.concatenate([high, low], axis=1))
        mixed = intra[h] + (read[:, :HD] + read[:, HD:]) * gate[:, h : h + 1]
        mixed_out[h] = mixed
        total = mixed * mixed if total is None else total + mixed * mixed
    ones = jnp.ones((8, HD), bf16)
    high, low = two(total)
    planes = squares_out.shape[0]
    squares_out[:, 0, :block] = (mm(ones, high, NT) + mm(ones, low, NT))[:planes]

    def handed_reads(ref, low):
        pieces = []
        for e in range(4):
            parts = []
            for h in range(heads):
                total = ref[16 * h + e, low : low + 2, 0, :]
                for d in range(1, 4):
                    total = total + ref[16 * h + 4 * d + e, low : low + 2, 0, :]
                parts.append(total)
            pieces.append(jnp.concatenate(parts, axis=0))
        whole = jnp.swapaxes(jnp.stack(turn(*pieces), axis=0), 0, 1)
        return whole.reshape(heads, 8, HD)

    first, late = handed_reads(got, 8), handed_reads(second, 0)
    rows_n = base.shape[0] // heads
    squares = [None] * rows_n
    for h in range(heads):
        for r in range(rows_n):
            n = r * heads + h
            read = base[n] + coef[0, n] * first[h] + coef[1, n] * late[h]
            reads_out[n] = read
            squares[r] = read * read if squares[r] is None else squares[r] + read * read
    high, low = two(jnp.concatenate(squares, axis=0))
    sums = mm(ones, high, NT) + mm(ones, low, NT)
    sums = jnp.concatenate([sums, jnp.zeros((8, HD - sums.shape[1]), f32)], axis=1)
    squares_out[:, 0, block:] = sums[:planes]


def norm_kernel(count, got, mixed, reads, prefill_out, decode_out, staged, staged_reads, sems):
    heads, block, _ = mixed.shape
    parts = jnp.concatenate(three(got[:, 0, :]), axis=0)
    ones = jnp.ones((parts.shape[0], HD), bf16)
    total = mm(parts, ones, TN)
    scale = lax.rsqrt(total / count + eps)
    sent = []
    half = block // 2
    for k in range(2):
        part = pl.ds(k * half, half)
        scaled = [mixed[h, part, :] * scale[k * half : (k + 1) * half] for h in range(heads)]
        staged[part] = jnp.swapaxes(jnp.stack(scaled, axis=0), 0, 1).astype(bf16)
        copy = pltpu.make_async_copy(staged.at[part], prefill_out.at[part], sems.at[k])
        copy.start()
        sent.append(copy)
    steps, rows_n = decode_out.shape[0], decode_out.shape[1]
    pieces = []
    for r in range(rows_n):
        low = block + r * steps
        for h in range(heads):
            pieces.append(reads[r * heads + h] * scale[low : low + steps])
    scaled = jnp.swapaxes(jnp.stack(pieces, axis=0), 0, 1)
    staged_reads[...] = scaled.reshape(decode_out.shape).astype(bf16)
    copy = pltpu.make_async_copy(staged_reads, decode_out, sems.at[2])
    copy.start()
    sent.append(copy)
    for copy in sent:
        copy.wait()


def call(
    kernel,
    name,
    outs,
    scalars,
    arrays,
    scratch=(),
    cost=0,
    space=pltpu.VMEM,
    scalar_space=pltpu.HBM,
    out_space=pltpu.VMEM,
):
    scalars = [pltpu.with_memory_space_constraint(x, pltpu.HBM) for x in scalars]
    if space is pltpu.HBM:
        arrays = [pltpu.with_memory_space_constraint(x, space) for x in arrays]
    shapes = [jax.ShapeDtypeStruct(shape, dtype) for shape, dtype in outs]
    specs = [pl.BlockSpec(memory_space=scalar_space)] * len(scalars)
    specs += [pl.BlockSpec(memory_space=space)] * len(arrays)
    return pl.pallas_call(
        kernel,
        name=name,
        out_shape=shapes,
        in_specs=specs,
        out_specs=[
            pl.BlockSpec(memory_space=pltpu.SMEM if dtype == jnp.int32 else out_space)
            for _, dtype in outs
        ],
        scratch_shapes=list(scratch),
        compiler_params=pltpu.CompilerParams(vmem_limit_bytes=24 * 2**20),
        cost_estimate=pl.CostEstimate(flops=cost, bytes_accessed=4 * 2**20, transcendentals=0),
    )(*scalars, *arrays)


def body(
    prefill_query,
    prefill_key,
    prefill_value,
    log_decay,
    lengths,
    owner,
    decode_state,
    step_query,
    step_key,
    step_value,
    step_decay,
    soft_query,
    cache_keys,
    cache_values,
    new_keys,
    new_values,
    row_lengths,
):
    block, heads, _ = prefill_query.shape
    steps, rows_n = step_query.shape[0], step_query.shape[1]
    blocks = lax.axis_size("ctx")
    planes = lax.axis_size("head")
    pairs = rows_n * heads
    decay_rows = jnp.swapaxes(log_decay, 0, 1)
    outgoing, second = call(
        summary_kernel,
        "summary",
        [
            ((blocks, ROWS_OUT, 1, HD), f32),
            ((blocks, ROWS_SECOND, 1, HD), f32),
        ],
        [lengths, owner],
        [decay_rows, prefill_key, prefill_value, step_query],
        scratch=[
            pltpu.VMEM(prefill_key.shape, bf16),
            pltpu.VMEM(prefill_value.shape, bf16),
            pltpu.VMEM(decay_rows.shape, f32),
            pltpu.VMEM(step_query.shape, bf16),
            pltpu.SMEM(lengths.shape, jnp.int32),
            pltpu.SMEM(owner.shape, jnp.int32),
            pltpu.SemaphoreType.DMA((12,)),
        ],
        space=pltpu.HBM,
    )
    gathered = lax.all_to_all(outgoing, "ctx", 0, 0, tiled=True)
    local_inputs = [
        decay_rows,
        prefill_query,
        prefill_key,
        prefill_value,
        decode_state,
        step_query,
        step_key,
        step_value,
        jnp.transpose(step_decay, (1, 2, 0)),
        soft_query,
        cache_keys.reshape(rows_n, -1, HD),
        cache_values.reshape(rows_n, -1, HD),
        new_keys.reshape(steps, rows_n, HD),
        new_values.reshape(steps, rows_n, HD),
    ]
    intra, queries, gate, base, coef, soft_out, links, shared = call(
        local_kernel,
        "local",
        [
            ((heads, block, HD), f32),
            ((heads, block, HD), bf16),
            ((block, 8), f32),
            ((pairs, steps, HD), f32),
            ((2, pairs, steps, HD), f32),
            (soft_query.shape, bf16),
            ((blocks + 8, blocks), f32),
            ((2,), jnp.int32),
        ],
        [lengths, owner, row_lengths],
        local_inputs,
        scratch=[pltpu.VMEM(x.shape, x.dtype) for x in local_inputs]
        + [pltpu.SemaphoreType.DMA((len(local_inputs),))],
        cost=2 * 10**9,
        space=pltpu.HBM,
        scalar_space=pltpu.SMEM,
    )
    shared, intra = lax.optimization_barrier((shared, intra))
    gathered, second = lax.optimization_barrier((gathered, second))

    def exchange(x):
        return lax.all_to_all(x, "ctx", 0, 0, tiled=True)

    second = lax.cond(shared[0] > 0, exchange, lambda x: x, second)
    returning, second = call(
        functools.partial(scan_kernel, block),
        "scan",
        [((blocks, ROWS_BACK, 1, HD), f32), ((blocks, 2, 1, HD), f32)],
        [lengths, owner],
        [gathered, second, links],
        scratch=[
            pltpu.VMEM((blocks + 8, 8, HD), f32),
            pltpu.SMEM(lengths.shape, jnp.int32),
            pltpu.SMEM(owner.shape, jnp.int32),
            pltpu.SemaphoreType.DMA((2,)),
        ],
    )
    returned = lax.all_to_all(returning, "ctx", 0, 0, tiled=True)
    second = lax.cond(shared[1] > 0, exchange, lambda x: x, second)
    mixed, reads, squares = call(
        mix_kernel,
        "mix",
        [
            ((heads, block, HD), f32),
            ((pairs, steps, HD), f32),
            ((planes, 1, block + HD), f32),
        ],
        [],
        [returned, second, intra, queries, gate, base, coef],
    )
    squares = lax.all_to_all(squares, "head", 0, 0, tiled=True)
    prefill_out, decode_out = call(
        functools.partial(norm_kernel, float(planes * heads * HD)),
        "norm",
        [(prefill_query.shape, bf16), (step_query.shape, bf16)],
        [],
        [squares, mixed, reads],
        scratch=[
            pltpu.VMEM(prefill_query.shape, bf16),
            pltpu.VMEM(step_query.shape, bf16),
            pltpu.SemaphoreType.DMA((3,)),
        ],
        out_space=pltpu.HBM,
    )
    return (prefill_out, decode_out, soft_out)


def solution(mesh):
    placed = (
        P("ctx", "head", None),
        P("ctx", "head", None),
        P("ctx", "head", None),
        P("ctx", "head"),
        P(),
        P(),
        P("ctx", "head", None, None),
        P(None, "ctx", "head", None),
        P(None, "ctx", "head", None),
        P(None, "ctx", "head", None),
        P(None, "ctx", "head"),
        P(None, "ctx", "head", None),
        P("ctx", None, "head", None),
        P("ctx", None, "head", None),
        P(None, "ctx", "head", None),
        P(None, "ctx", "head", None),
        P("ctx"),
    )
    return jax.shard_map(
        body,
        mesh=mesh,
        in_specs=placed,
        out_specs=(
            P("ctx", "head", None),
            P(None, "ctx", "head", None),
            P(None, "ctx", "head", None),
        ),
        check_vma=False,
    )
```

```python
import functools
import math

import jax
import jax.numpy as jnp
from jax import lax
from jax.experimental import pallas as pl
from jax.experimental.pallas import tpu as pltpu
from jax.sharding import PartitionSpec as P

f32 = jnp.float32
bf16 = jnp.bfloat16
eps = 1e-06
HD = 128
QUARTER = HD // 4
ROW_END = 8
ROW_QUERY = 16
ROW_DECAY = 18
ROWS_OUT = 19
ROWS_BACK = 10
ROWS_SECOND = 10
NT = (((1,), (1,)), ((), ()))
TN = (((0,), (0,)), ((), ()))
NN = (((1,), (0,)), ((), ()))


def mm(a, b, dims=NN):
    return lax.dot_general(a, b, dims, preferred_element_type=f32)


def iota(shape, dim):
    return lax.broadcasted_iota(jnp.int32, shape, dim)


def two(x):
    high = x.astype(bf16)
    return high, (x - high.astype(f32)).astype(bf16)


def three(x):
    high = x.astype(bf16)
    rest = x - high.astype(f32)
    mid = rest.astype(bf16)
    return high, mid, (rest - mid.astype(f32)).astype(bf16)


def prompt_bounds(lengths):
    ends, total = [], jnp.int32(0)
    starts = []
    for p in range(lengths.shape[0]):
        starts.append(total)
        total = total + lengths[p]
        ends.append(total)
    return starts, ends


def segment_of(positions, ends):
    segment = jnp.zeros(positions.shape, jnp.int32)
    for end in ends:
        segment = segment + (positions >= end).astype(jnp.int32)
    return segment


def scalar_segment(position, ends):
    segment = jnp.int32(0)
    for end in ends:
        segment = segment + (position >= end).astype(jnp.int32)
    return segment


def swap(first, second, width):
    shape = first.shape
    even = ((iota((1, HD), 1) // width) % 2 == 0).reshape((1,) * (len(shape) - 1) + (HD,))
    up = pltpu.roll(second.reshape(-1, HD), width, 1).reshape(shape)
    down = pltpu.roll(first.reshape(-1, HD), HD - width, 1).reshape(shape)
    return jnp.where(even, first, up), jnp.where(even, down, second)


def turn(a, b, c, d):
    a, c = swap(a, c, 2 * QUARTER)
    b, d = swap(b, d, 2 * QUARTER)
    a, b = swap(a, b, QUARTER)
    c, d = swap(c, d, QUARTER)
    return a, b, c, d


def cut(matrix):
    split = matrix.reshape(4, 4, 8, HD)
    return jnp.stack(turn(*(split[:, k] for k in range(4))), axis=1).reshape(16, 8, HD)


def uncut(chunks):
    return cut(chunks.reshape(HD, HD)).reshape(HD, HD)


def running_sums(decay):
    heads, block = decay.shape
    upto = (iota((HD, 1), 0) <= iota((1, HD), 1)).astype(f32).astype(bf16)
    upto = jnp.concatenate([upto, jnp.ones((HD, HD), bf16)], axis=1)
    pieces = [decay[:, low : low + HD] for low in range(0, block, HD)]
    stacked = jnp.concatenate(pieces, axis=0)
    local = sum(mm(part, upto) for part in three(stacked))
    out, before = [], None
    for k in range(len(pieces)):
        rows = slice(k * heads, (k + 1) * heads)
        out.append(local[rows, :HD] if before is None else local[rows, :HD] + before)
        before = local[rows, HD:] if before is None else before + local[rows, HD:]
    return jnp.concatenate(out, axis=1)


def end_slot(slot, ends, block_start, block):
    prompt, offset = jnp.int32(-1), jnp.int32(-1)
    for p in range(len(ends)):
        if p % 2 != slot:
            continue
        local = ends[p] - 1 - block_start
        inside = (local >= 0) & (local < block) & (lax.rem(ends[p], block) != 0)
        prompt = jnp.where(inside, p, prompt)
        offset = jnp.where(inside, local, offset)
    return prompt, offset


def row_taken(owner, row):
    taken = jnp.bool_(False)
    for p in range(owner.shape[0]):
        taken = taken | (owner[p] == row)
    return taken


def block_shares(first, second, block):
    inside = (lax.rem(first, block) != 0) & (lax.rem(second, block) != 0)
    return inside & (first // block == second // block)


def summary_kernel(
    lengths_in,
    owner_in,
    decay,
    key,
    value,
    step_query,
    staged,
    second_out,
    key_buf,
    value_buf,
    decay_buf,
    query_buf,
    lengths,
    owner,
    sems,
):
    copies = [
        pltpu.make_async_copy(lengths_in, lengths, sems.at[0]),
        pltpu.make_async_copy(owner_in, owner, sems.at[1]),
        pltpu.make_async_copy(step_query, query_buf, sems.at[2]),
        pltpu.make_async_copy(decay, decay_buf, sems.at[3]),
    ]
    heads, block = decay_buf.shape
    quarter = block // 4
    for k in range(4):
        part = pl.ds(k * quarter, quarter)
        copies.append(pltpu.make_async_copy(key.at[part], key_buf.at[part], sems.at[4 + k]))
        copies.append(pltpu.make_async_copy(value.at[part], value_buf.at[part], sems.at[8 + k]))
    for copy in copies:
        copy.start()
    device = lax.axis_index("ctx")
    block_start = device * block

    copies[2].wait()
    steps, rows = query_buf.shape[0], query_buf.shape[1]
    pairs = rows * heads
    flat = query_buf[...].astype(f32).reshape(steps * pairs, HD).astype(bf16)
    lane = iota((1, 4 * HD), 1)
    pick = iota((HD, 1), 0) == (lane // HD) * QUARTER + lane % QUARTER
    read = mm(flat, pick.astype(f32).astype(bf16))
    spread = []
    for k in range(2):
        total = None
        for step in range(4):
            low = (4 * k + step) * pairs
            mine = (lane % HD) // QUARTER == step
            part = jnp.where(mine, read[low : low + pairs], 0.0)
            total = part if total is None else total + part
        spread.append(total)

    copies[3].wait()
    running = running_sums(decay_buf[...])

    for copy in copies[:2]:
        copy.wait()
    _, ends = prompt_bounds(lengths)
    place = iota((1, block), 1)
    segment = segment_of(place + block_start, ends)
    last = scalar_segment(block_start + block - 1, ends)
    prompt_a, offset_a = end_slot(0, ends, block_start, block)
    prompt_b, offset_b = end_slot(1, ends, block_start, block)
    both = (prompt_a >= 0) & (prompt_b >= 0)
    prompt_a = jnp.where(prompt_a >= 0, prompt_a, prompt_b)
    offset_a = jnp.where(offset_a >= 0, offset_a, offset_b)

    def weight(prompt, offset):
        inside = segment == prompt
        at = jnp.sum(jnp.where(place == offset, running, 0.0), axis=1, keepdims=True)
        weight = jnp.where(inside, jnp.exp(jnp.where(inside, at - running, 0.0)), 0.0)
        return weight, at

    weight_last, _ = weight(last, jnp.int32(block - 1))
    weight_a, at_a = weight(prompt_a, offset_a)
    whole = jnp.sum(jnp.where(segment == last, decay_buf[...], 0.0), axis=1, keepdims=True)
    lane, head = iota((heads, HD), 1), iota((heads, HD), 0)
    totals = jnp.where(lane == head, whole, 0.0)
    totals = jnp.where(lane == heads + head, at_a, totals)
    totals = jnp.sum(totals, axis=0, keepdims=True)
    staged[:, ROW_DECAY, 0, :] = jnp.broadcast_to(totals, (staged.shape[0], HD))

    first_taken = row_taken(owner, device * rows)
    for h in range(heads):
        first = jnp.concatenate([part[h : h + 1] for part in spread], axis=0)
        other = jnp.concatenate([part[heads + h : heads + h + 1] for part in spread], axis=0)
        chosen = jnp.where(first_taken, first, other)
        for d in range(4):
            j = 16 * h + 4 * d
            staged[j : j + 4, ROW_QUERY:ROW_DECAY, 0, :] = jnp.broadcast_to(
                chosen[None, :, d * HD : (d + 1) * HD], (4, 2, HD)
            )

    @pl.when(first_taken & row_taken(owner, device * rows + 1))
    def _():
        for h in range(heads):
            other = jnp.concatenate([part[heads + h : heads + h + 1] for part in spread], axis=0)
            for d in range(4):
                j = 16 * h + 4 * d
                second_out[j : j + 4, 8:ROWS_SECOND, 0, :] = jnp.broadcast_to(
                    other[None, :, d * HD : (d + 1) * HD], (4, 2, HD)
                )

    for copy in copies[4:]:
        copy.wait()
    keys = jnp.swapaxes(key_buf[...], 0, 1)
    values = jnp.swapaxes(value_buf[...], 0, 1)
    for h in range(heads):
        key_h = keys[h].T.astype(f32)
        left = []
        for weight_k in (weight_last, weight_a):
            left.extend(two(key_h * weight_k[h : h + 1]))
        product = mm(jnp.concatenate(left, axis=0), values[h])
        for k in range(2):
            low = 2 * k * HD
            state = product[low : low + HD] + product[low + HD : low + 2 * HD]
            staged[16 * h : 16 * h + 16, 8 * k : 8 * k + 8, 0, :] = cut(state)

    @pl.when(both)
    def _():
        weight_b, at_b = weight(prompt_b, offset_b)
        more = jnp.sum(jnp.where(lane == 2 * heads + head, at_b, 0.0), axis=0, keepdims=True)
        staged[:, ROW_DECAY, 0, :] = jnp.broadcast_to(totals + more, (staged.shape[0], HD))
        for h in range(heads):
            left = two(keys[h].T.astype(f32) * weight_b[h : h + 1])
            product = mm(jnp.concatenate(left, axis=0), values[h])
            second_out[16 * h : 16 * h + 16, 0:8, 0, :] = cut(product[:HD] + product[HD:])


def local_kernel(lengths, owner, row_lengths, *refs):
    count = (len(refs) - 9) // 2
    sources, outs = refs[:count], refs[count : count + 8]
    buffers, sems = refs[count + 8 : -1], refs[-1]
    copies = [
        pltpu.make_async_copy(source, buffer, sems.at[k])
        for k, (source, buffer) in enumerate(zip(sources, buffers))
    ]
    for copy in copies:
        copy.start()
    for copy in copies:
        copy.wait()
    (
        log_decay,
        query,
        key,
        value,
        decode_state,
        step_query,
        step_key,
        step_value,
        step_decay,
        soft_query,
        cache_keys,
        cache_values,
        new_keys,
        new_values,
    ) = buffers
    intra_out, query_out, gate_out, base_out, coef_out, soft_out, linked_out, shared_out = outs
    block, heads, _ = query.shape
    device = lax.axis_index("ctx")
    block_start = device * block
    starts, ends = prompt_bounds(lengths)
    shared_end, shared_row = jnp.bool_(False), jnp.bool_(False)
    for other in range(0, len(ends), 2):
        shared_end = shared_end | block_shares(ends[1], ends[other], block)
    for p in range(len(ends)):
        for other in range(p):
            shared_row = shared_row | (owner[p] // 2 == owner[other] // 2)
    shared_out[0] = (shared_end | shared_row).astype(jnp.int32)
    shared_out[1] = shared_row.astype(jnp.int32)
    to, frm = iota(linked_out.shape, 0), iota(linked_out.shape, 1)
    linked = frm < to
    for start in starts:
        restart = start // block
        linked = linked & ~((restart > frm) & (restart < to))
    linked_out[...] = linked.astype(f32)

    running = running_sums(log_decay[...])
    columns = jnp.concatenate([running, running], axis=0).T
    place_row = iota((1, block), 1) + block_start
    place_col = iota((block, 1), 0) + block_start
    segment_row = segment_of(place_row, ends)
    segment_col = segment_of(place_col, ends)
    before = jnp.where(block_start > 0, scalar_segment(block_start - 1, ends), -1)
    gate_out[...] = jnp.where(segment_col == before, jnp.exp(columns), 0.0)

    queries = jnp.swapaxes(query[...], 0, 1)
    keys = jnp.swapaxes(key[...], 0, 1)
    values = jnp.swapaxes(value[...], 0, 1)
    query_out[...] = queries
    half = block // 2
    tiles = ((0, 0), (1, 0), (1, 1))
    masks = {}
    for a, b in tiles:
        rows = slice(a * half, (a + 1) * half)
        cols = slice(b * half, (b + 1) * half)
        seen = segment_col[rows] == segment_row[:, cols]
        if a == b:
            seen = seen & (place_col[rows] >= place_row[:, cols])
        masks[a, b] = jnp.where(seen, 0.0, -1e30)
    for h in range(heads):
        mixed = [None, None]
        for a, b in tiles:
            rows = slice(a * half, (a + 1) * half)
            cols = slice(b * half, (b + 1) * half)
            scores = mm(queries[h][rows], keys[h][cols], NT)
            gap = columns[rows, h : h + 1] - running[h : h + 1, cols]
            weights = (scores * jnp.exp(gap + masks[a, b])).astype(bf16)
            term = mm(weights, values[h][cols])
            mixed[a] = term if mixed[a] is None else mixed[a] + term
        intra_out[h, :half, :] = mixed[0]
        intra_out[h, half:, :] = mixed[1]

    steps, rows_n = step_query.shape[0], step_query.shape[1]

    def by_head(ref):
        whole = ref[...].astype(f32).reshape(steps, rows_n * heads, HD)
        return jnp.swapaxes(whole, 0, 1)

    sq, sk, sv = by_head(step_query), by_head(step_key), by_head(step_value)
    decays = step_decay[...].reshape(rows_n * heads, steps)
    upto = (iota((steps, steps), 0) <= iota((steps, steps), 1)).astype(f32)
    cum_row = lax.dot_general(
        decays, upto, NN, precision=lax.Precision.HIGHEST, preferred_element_type=f32
    )
    cum_col = cum_row.T
    causal = iota((steps, steps), 0) >= iota((steps, steps), 1)
    for r in range(rows_n):
        taken = row_taken(owner, device * rows_n + r)
        owned = jnp.where(taken, 1.0, 0.0)
        late = jnp.where(taken & row_taken(owner, device * rows_n), r * 1.0, 0.0)
        for h in range(heads):
            n = r * heads + h
            cum = cum_col[:, n : n + 1]
            gap = jnp.where(causal, cum - cum_row[n : n + 1, :], 0.0)
            inner = mm(sq[n].astype(bf16), sk[n].astype(bf16), NT)
            inner = jnp.where(causal, inner * jnp.exp(gap), 0.0)
            fresh = lax.dot_general(
                inner, sv[n], NN, precision=lax.Precision.HIGHEST, preferred_element_type=f32
            )
            high, low = two(decode_state[r, h])
            read = mm(sq[n].astype(bf16), jnp.concatenate([high, low], axis=1))
            grown = jnp.exp(cum)
            read = (read[:, :HD] + read[:, HD:]) * grown
            base_out[n] = fresh + jnp.where(owned > 0.5, 0.0, read)
            coef_out[0, n] = jnp.broadcast_to(grown * (owned - late), (steps, HD))
            coef_out[1, n] = jnp.broadcast_to(grown * late, (steps, HD))

    fresh_keys = jnp.swapaxes(new_keys[...].astype(f32), 0, 1)
    fresh_values = jnp.swapaxes(new_values[...].astype(f32), 0, 1)
    group = soft_query.shape[2]
    cache = cache_keys.shape[1]
    scale = 1.0 / math.sqrt(HD)
    whole = soft_query[...].astype(f32)
    for r in range(rows_n):
        rows_q = whole[:, r].reshape(steps * group, HD).astype(bf16)
        cached = mm(rows_q, cache_keys[r], NT) * scale
        recent = mm(rows_q, fresh_keys[r].astype(bf16), NT) * scale
        slot = iota((steps * group, cache), 1)
        cached = jnp.where(slot < row_lengths[r], cached, -jnp.inf)
        step_of = iota((steps * group, steps), 0) // group
        recent = jnp.where(iota((steps * group, steps), 1) <= step_of, recent, -jnp.inf)
        top = jnp.maximum(
            jnp.max(cached, axis=1, keepdims=True), jnp.max(recent, axis=1, keepdims=True)
        )
        cached = jnp.exp(cached - top)
        recent = jnp.exp(recent - top)
        total = jnp.sum(cached, axis=1, keepdims=True) + jnp.sum(recent, axis=1, keepdims=True)
        cached = (cached / total).astype(bf16)
        recent = (recent / total).astype(bf16)
        mixed = mm(cached, cache_values[r]) + mm(recent, fresh_values[r].astype(bf16))
        soft_out[:, r, :, :] = mixed.reshape(steps, group, HD).astype(bf16)


def scan_kernel(
    block, lengths_in, owner_in, got, second, links, out, second_out, carried, lengths, owner, sems
):
    copies = [
        pltpu.make_async_copy(lengths_in, lengths, sems.at[0]),
        pltpu.make_async_copy(owner_in, owner, sems.at[1]),
    ]
    for copy in copies:
        copy.start()
    blocks = got.shape[0]
    device = lax.axis_index("ctx")
    head = device // 16
    padded = carried.shape[0]
    heads = blocks // 16

    decays = got[:, ROW_DECAY, 0, :]
    decay = jnp.sum(
        jnp.where(iota((blocks, HD), 1) == head, decays, 0.0), axis=1, keepdims=True
    )
    k_at, b_at = iota((blocks, blocks), 0), iota((blocks, blocks), 1)
    later = jnp.concatenate(
        [jnp.where(k_at > b_at, part.astype(f32), 0.0).astype(bf16) for part in three(decay)],
        axis=0,
    )
    earlier = iota((padded, 3 * blocks), 1) % blocks < iota((padded, 3 * blocks), 0)
    gap = mm(earlier.astype(f32).astype(bf16), later)
    right = []
    for i in range(8):
        high, low = two(got[:, i, 0, :])
        right.append(jnp.concatenate([high, low, high], axis=0))
    right = jnp.concatenate(right, axis=1)

    linked = links[...] > 0.5
    weight = jnp.where(linked, jnp.exp(jnp.where(linked, gap, 0.0)), 0.0)
    high, low = two(weight)
    weights = jnp.concatenate([high, high, low], axis=1)
    product = mm(weights, right)
    for i in range(8):
        state = product[:, i * HD : (i + 1) * HD]
        carried[:, i, :] = state
        out[:, i, 0, :] = state[:blocks]

    quarter_of = iota((1, HD), 1) // QUARTER
    for copy in copies:
        copy.wait()
    starts, ends = prompt_bounds(lengths)
    reads = []
    for p in range(len(ends)):
        index = ends[p] // block
        source = jnp.minimum(index, blocks - 1)
        partial = lax.rem(ends[p], block) != 0
        leads = (starts[p] < index * block).astype(f32)
        if p % 2:
            shared = jnp.bool_(False)
            for other in range(0, len(ends), 2):
                shared = shared | block_shares(ends[p], ends[other], block)
        else:
            shared = jnp.bool_(False)
        run = got[source, ROW_DECAY, :, :]
        at = jnp.where(shared, 2 * heads, heads) + head
        run = jnp.sum(jnp.where(iota((1, HD), 1) == at, run, 0.0), axis=1, keepdims=True)
        lead = leads * jnp.exp(jnp.where(partial, run, 0.0))
        rest = got[source, ROW_END : ROW_END + 8, 0, :]
        if p % 2:
            rest = jnp.where(shared, second[source, 0:8, 0, :], rest)
        handed = carried[index] * lead + jnp.where(partial, rest, 0.0)
        turned = [handed] + [pltpu.roll(handed, k * QUARTER, 1) for k in range(1, 4)]
        rows = []
        for k in range(4):
            for g in range(4):
                rows.append(jnp.where(quarter_of == k, turned[(k - g) % 4], 0.0))
        rows = jnp.concatenate(rows, axis=0)
        place = owner[p] // 2
        late = (lax.rem(owner[p], 2) == 1) & row_taken(owner, owner[p] - 1)
        query = jnp.where(
            late, second[place, 8:ROWS_SECOND, 0, :], got[place, ROW_QUERY:ROW_DECAY, 0, :]
        )
        read = mm(query.astype(bf16), jnp.concatenate(two(rows), axis=1))
        reads.append((place, late, read[:, :HD] + read[:, HD:]))
    for place, late, read in reads:

        @pl.when(late)
        def _():
            second_out[place, :, 0, :] = read

        @pl.when(jnp.logical_not(late))
        def _():
            out[place, 8:ROWS_BACK, 0, :] = read


def mix_kernel(got, second, intra, query, gate, base, coef, mixed_out, reads_out, squares_out):
    heads, block, _ = intra.shape
    total = None
    for h in range(heads):
        state = uncut(got[16 * h : 16 * h + 16, 0:8, 0, :])
        high, low = two(state)
        read = mm(query[h], jnp.concatenate([high, low], axis=1))
        mixed = intra[h] + (read[:, :HD] + read[:, HD:]) * gate[:, h : h + 1]
        mixed_out[h] = mixed
        total = mixed * mixed if total is None else total + mixed * mixed
    ones = jnp.ones((8, HD), bf16)
    high, low = two(total)
    planes = squares_out.shape[0]
    squares_out[:, 0, :block] = (mm(ones, high, NT) + mm(ones, low, NT))[:planes]

    def handed_reads(ref, low):
        pieces = []
        for e in range(4):
            parts = []
            for h in range(heads):
                total = ref[16 * h + e, low : low + 2, 0, :]
                for d in range(1, 4):
                    total = total + ref[16 * h + 4 * d + e, low : low + 2, 0, :]
                parts.append(total)
            pieces.append(jnp.concatenate(parts, axis=0))
        whole = jnp.swapaxes(jnp.stack(turn(*pieces), axis=0), 0, 1)
        return whole.reshape(heads, 8, HD)

    first, late = handed_reads(got, 8), handed_reads(second, 0)
    rows_n = base.shape[0] // heads
    squares = [None] * rows_n
    for h in range(heads):
        for r in range(rows_n):
            n = r * heads + h
            read = base[n] + jnp.where(coef[0, n] > 0, coef[0, n] * first[h], 0.0)
            read = read + jnp.where(coef[1, n] > 0, coef[1, n] * late[h], 0.0)
            reads_out[n] = read
            squares[r] = read * read if squares[r] is None else squares[r] + read * read
    high, low = two(jnp.concatenate(squares, axis=0))
    sums = mm(ones, high, NT) + mm(ones, low, NT)
    sums = jnp.concatenate([sums, jnp.zeros((8, HD - sums.shape[1]), f32)], axis=1)
    squares_out[:, 0, block:] = sums[:planes]


def norm_kernel(count, got, mixed, reads, prefill_out, decode_out, staged, staged_reads, sems):
    heads, block, _ = mixed.shape
    parts = jnp.concatenate(three(got[:, 0, :]), axis=0)
    ones = jnp.ones((parts.shape[0], HD), bf16)
    total = mm(parts, ones, TN)
    scale = lax.rsqrt(total / count + eps)
    sent = []
    half = block // 2
    for k in range(2):
        part = pl.ds(k * half, half)
        scaled = [mixed[h, part, :] * scale[k * half : (k + 1) * half] for h in range(heads)]
        staged[part] = jnp.swapaxes(jnp.stack(scaled, axis=0), 0, 1).astype(bf16)
        copy = pltpu.make_async_copy(staged.at[part], prefill_out.at[part], sems.at[k])
        copy.start()
        sent.append(copy)
    steps, rows_n = decode_out.shape[0], decode_out.shape[1]
    pieces = []
    for r in range(rows_n):
        low = block + r * steps
        for h in range(heads):
            pieces.append(reads[r * heads + h] * scale[low : low + steps])
    scaled = jnp.swapaxes(jnp.stack(pieces, axis=0), 0, 1)
    staged_reads[...] = scaled.reshape(decode_out.shape).astype(bf16)
    copy = pltpu.make_async_copy(staged_reads, decode_out, sems.at[2])
    copy.start()
    sent.append(copy)
    for copy in sent:
        copy.wait()


def call(
    kernel,
    name,
    outs,
    scalars,
    arrays,
    scratch=(),
    cost=0,
    space=pltpu.VMEM,
    scalar_space=pltpu.HBM,
    out_space=pltpu.VMEM,
):
    scalars = [pltpu.with_memory_space_constraint(x, pltpu.HBM) for x in scalars]
    if space is pltpu.HBM:
        arrays = [pltpu.with_memory_space_constraint(x, space) for x in arrays]
    shapes = [jax.ShapeDtypeStruct(shape, dtype) for shape, dtype in outs]
    specs = [pl.BlockSpec(memory_space=scalar_space)] * len(scalars)
    specs += [pl.BlockSpec(memory_space=space)] * len(arrays)
    return pl.pallas_call(
        kernel,
        name=name,
        out_shape=shapes,
        in_specs=specs,
        out_specs=[
            pl.BlockSpec(memory_space=pltpu.SMEM if dtype == jnp.int32 else out_space)
            for _, dtype in outs
        ],
        scratch_shapes=list(scratch),
        compiler_params=pltpu.CompilerParams(vmem_limit_bytes=24 * 2**20),
        cost_estimate=pl.CostEstimate(flops=cost, bytes_accessed=4 * 2**20, transcendentals=0),
    )(*scalars, *arrays)


def body(
    prefill_query,
    prefill_key,
    prefill_value,
    log_decay,
    lengths,
    owner,
    decode_state,
    step_query,
    step_key,
    step_value,
    step_decay,
    soft_query,
    cache_keys,
    cache_values,
    new_keys,
    new_values,
    row_lengths,
):
    block, heads, _ = prefill_query.shape
    steps, rows_n = step_query.shape[0], step_query.shape[1]
    blocks = lax.axis_size("ctx")
    planes = lax.axis_size("head")
    pairs = rows_n * heads
    decay_rows = jnp.swapaxes(log_decay, 0, 1)
    outgoing, second = call(
        summary_kernel,
        "summary",
        [
            ((blocks, ROWS_OUT, 1, HD), f32),
            ((blocks, ROWS_SECOND, 1, HD), f32),
        ],
        [lengths, owner],
        [decay_rows, prefill_key, prefill_value, step_query],
        scratch=[
            pltpu.VMEM(prefill_key.shape, bf16),
            pltpu.VMEM(prefill_value.shape, bf16),
            pltpu.VMEM(decay_rows.shape, f32),
            pltpu.VMEM(step_query.shape, bf16),
            pltpu.SMEM(lengths.shape, jnp.int32),
            pltpu.SMEM(owner.shape, jnp.int32),
            pltpu.SemaphoreType.DMA((12,)),
        ],
        space=pltpu.HBM,
    )
    gathered = lax.all_to_all(outgoing, "ctx", 0, 0, tiled=True)
    local_inputs = [
        decay_rows,
        prefill_query,
        prefill_key,
        prefill_value,
        decode_state,
        step_query,
        step_key,
        step_value,
        jnp.transpose(step_decay, (1, 2, 0)),
        soft_query,
        cache_keys.reshape(rows_n, -1, HD),
        cache_values.reshape(rows_n, -1, HD),
        new_keys.reshape(steps, rows_n, HD),
        new_values.reshape(steps, rows_n, HD),
    ]
    intra, queries, gate, base, coef, soft_out, links, shared = call(
        local_kernel,
        "local",
        [
            ((heads, block, HD), f32),
            ((heads, block, HD), bf16),
            ((block, 8), f32),
            ((pairs, steps, HD), f32),
            ((2, pairs, steps, HD), f32),
            (soft_query.shape, bf16),
            ((blocks + 8, blocks), f32),
            ((2,), jnp.int32),
        ],
        [lengths, owner, row_lengths],
        local_inputs,
        scratch=[pltpu.VMEM(x.shape, x.dtype) for x in local_inputs]
        + [pltpu.SemaphoreType.DMA((len(local_inputs),))],
        cost=2 * 10**9,
        space=pltpu.HBM,
        scalar_space=pltpu.SMEM,
    )
    shared, intra = lax.optimization_barrier((shared, intra))
    gathered, second = lax.optimization_barrier((gathered, second))

    def exchange(x):
        return lax.all_to_all(x, "ctx", 0, 0, tiled=True)

    second = lax.cond(shared[0] > 0, exchange, lambda x: x, second)
    returning, second = call(
        functools.partial(scan_kernel, block),
        "scan",
        [((blocks, ROWS_BACK, 1, HD), f32), ((blocks, 2, 1, HD), f32)],
        [lengths, owner],
        [gathered, second, links],
        scratch=[
            pltpu.VMEM((blocks + 8, 8, HD), f32),
            pltpu.SMEM(lengths.shape, jnp.int32),
            pltpu.SMEM(owner.shape, jnp.int32),
            pltpu.SemaphoreType.DMA((2,)),
        ],
    )
    returned = lax.all_to_all(returning, "ctx", 0, 0, tiled=True)
    second = lax.cond(shared[1] > 0, exchange, lambda x: x, second)
    mixed, reads, squares = call(
        mix_kernel,
        "mix",
        [
            ((heads, block, HD), f32),
            ((pairs, steps, HD), f32),
            ((planes, 1, block + HD), f32),
        ],
        [],
        [returned, second, intra, queries, gate, base, coef],
    )
    squares = lax.all_to_all(squares, "head", 0, 0, tiled=True)
    prefill_out, decode_out = call(
        functools.partial(norm_kernel, float(planes * heads * HD)),
        "norm",
        [(prefill_query.shape, bf16), (step_query.shape, bf16)],
        [],
        [squares, mixed, reads],
        scratch=[
            pltpu.VMEM(prefill_query.shape, bf16),
            pltpu.VMEM(step_query.shape, bf16),
            pltpu.SemaphoreType.DMA((3,)),
        ],
        out_space=pltpu.HBM,
    )
    return (prefill_out, decode_out, soft_out)


def solution(mesh):
    placed = (
        P("ctx", "head", None),
        P("ctx", "head", None),
        P("ctx", "head", None),
        P("ctx", "head"),
        P(),
        P(),
        P("ctx", "head", None, None),
        P(None, "ctx", "head", None),
        P(None, "ctx", "head", None),
        P(None, "ctx", "head", None),
        P(None, "ctx", "head"),
        P(None, "ctx", "head", None),
        P("ctx", None, "head", None),
        P("ctx", None, "head", None),
        P(None, "ctx", "head", None),
        P(None, "ctx", "head", None),
        P("ctx"),
    )
    return jax.shard_map(
        body,
        mesh=mesh,
        in_specs=placed,
        out_specs=(
            P("ctx", "head", None),
            P(None, "ctx", "head", None),
            P(None, "ctx", "head", None),
        ),
        check_vma=False,
    )
```
